32 devices in a mesh: gx: 4 (over y, x), gy: 2 (over core), gz: 4 (over z).
Axes of the slice: x: 2, y: 2, z: 4, core: 2. Of those that a mesh axis runs over, the one named last changes fastest.
Arguments:
- starting_warmth: float32 [32, 1024, 256], P('gz', 'gx', 'gy'), may hold values from -6 to 6
- sheet_stratum_number: int32 [32], replicated, may hold values from 0 to 15
- stratum_heat_conduction: float32 [16], replicated, may hold values from 1 to 16
- substance_kind: int32 [32, 1024, 256], P('gz', 'gx', 'gy'), may hold values from 0 to 3
- substance_kind_scaling: float32 [4], replicated, may hold values from 0.5 to 1.5
- wire_piece_amperes: float32 [131072], P(('gx', 'gy', 'gz')), may hold values from -6 to 6
- wire_piece_ohms_base: float32 [131072], P(('gx', 'gy', 'gz')), may hold values from 0.5 to 2
- wire_piece_tile: int32 [131072, 1], P(('gx', 'gy', 'gz')), may hold values from 0 to 31; in each aligned block of 4096 rows (0 to 4095, 4096 to 8191, ...) at most 256 rows name the same one
- wire_piece_voxel: int32 [131072], P(('gx', 'gy', 'gz')), may hold values from 0 to 262143
Outputs:
- warmed: float32 [32, 1024, 256], P('gz', 'gx', 'gy')
- ohmic_power_final: float32 [32, 1024, 256], P('gz', 'gx', 'gy')
The draws below stay inside these ranges and needn't reach their ends.
Inputs may be any that keep to these rules, and one draw needn't show every extreme that they name: `wire_piece_tile`: among the 4096 segments of one device, at most 256 name the same block, and some block is named by exactly 256 of them.
All inputs are finite; a program needn't handle non-finite values.
Results may differ from the reference program's by a relative error of at most 0.0029.
Values sent between devices are 32-bit elements; how exact they have to be, the bound alone decides.
No kernel may reach another device: no remote copies, remote signals or barrier semaphores. Data moves between devices by JAX's collectives and lax.ppermute only.
A program may use at most 128 MiB of HBM per device.

```python
import math
import jax
import jax.numpy as jnp
import numpy as np
from jax import lax

CX = 256
CY = 128
CZ = 8
S_DEV = 4096
LAYERS = 16
CLASSES = 4
STEPS = 2
GRID_WIDE_SIZE = 1024
GRID_DEEP_SIZE = 256
GRID_TALL_SIZE = 32
SEGS = 131072
MOST = 256
N_GY = 2
N_GZ = 4
DEVICES = 32


def plant(drawn, stream_key, smallest, largest):
    longest = drawn.shape.index(max(drawn.shape))
    spots = []
    for shift in (0, 1):
        where = [jax.random.randint(jax.random.fold_in(stream_key, axis), (), 0, length) for axis, length in enumerate(drawn.shape)]
        where[longest] = (where[longest] + shift) % drawn.shape[longest]
        spots.append(tuple(where))
    return drawn.at[spots[0]].set(smallest).at[spots[1]].set(largest)


def block_levels(own_key, extent, cuts, least, top_value):
    level, own = 1.0, jax.random.fold_in(own_key, 6)
    for axis_at, parts in cuts:
        draws = jnp.exp(jax.random.uniform(jax.random.fold_in(own, axis_at), (parts,), jnp.float32, least / len(cuts), top_value / len(cuts)))
        level = level * jnp.repeat(draws, extent[axis_at] // parts).reshape([-1 if axis == axis_at else 1 for axis in range(len(extent))])
    return level


def deal_out(own_key, own, number, rows, count, top, most, lean):
    order = jax.random.permutation(own_key, count)
    packed, ordinary = shares(count, rows * top, most, lean, True), shares(count, rows * top, most, lean, False)
    places = jnp.arange(count)

    def named(lengths, rotation):
        used = int((lengths > 0).sum())
        fixed = max(1, used // 4)
        shifted = fixed + (places - fixed + rotation * (used - fixed)) % max(1, count - fixed)
        return jnp.zeros((count,), jnp.int32).at[order[jnp.where(places < fixed, places, shifted)]].set(jnp.asarray(lengths, jnp.int32))

    lengths = jnp.where(number % 4 == 0, named(packed, number // 4), named(ordinary, number - number // 4 - 1))
    mixed = jax.random.permutation(jax.random.fold_in(own, 3), count)
    source_of, receiver = mixed[0:count // 2 * 2:2], mixed[1:count // 2 * 2:2]
    room = jnp.minimum(lengths[source_of] - 1, most - lengths[receiver]) // 2
    room = jnp.where((source_of == order[0]) | (receiver == order[0]) | (lengths[receiver] == 0), 0, jnp.maximum(room, 0))
    shifted = jax.random.randint(jax.random.fold_in(own, 4), (count // 2,), 0, 1 << 20) % (room + 1)
    lengths = lengths.at[source_of].add(-shifted).at[receiver].add(shifted)
    labels = jnp.searchsorted(jnp.cumsum(lengths), jnp.arange(rows * top), side="right").astype(jnp.int32)
    table = labels.reshape(top, rows).T
    table = table[jax.random.permutation(jax.random.fold_in(own, 1), rows)]
    rotation = jax.random.randint(jax.random.fold_in(own, 2), (rows, 1), 0, top)
    return jnp.take_along_axis(table, (jnp.arange(top)[None, :] + rotation) % top, axis=1)


def shares(amount, total, limit, lean, full):
    weights = [(1 << 20) // math.isqrt(grade ** lean) + 1 for grade in range(1, amount + 1)]
    largest = limit if full else min(limit, max(-(-total // amount), total * weights[0] // sum(weights)))
    least = 1 if total - largest >= amount - 1 else 0
    given, spare = [largest] + [least] * (amount - 1), total - largest - least * (amount - 1)
    while spare > 0:
        movable = [i for i in range(1, amount) if given[i] < largest] or [i for i in range(1, amount) if given[i] < limit]
        pool, remaining = sum([weights[i] for i in movable]), spare
        for i in movable:
            more = min(limit - given[i], max(1, remaining * weights[i] // pool), spare)
            given[i] = given[i] + more
            spare = spare - more
    return np.array(given)


def scatter_about(own_key, extent, width, most, split=(), held_as=jnp.bfloat16):
    drawn = width * jax.random.normal(own_key, extent, jnp.float32)
    if split:
        drawn = drawn * block_levels(own_key, extent, split, -0.22, 0.18)
    return jnp.clip(drawn, -most, most).astype(held_as)


def setup_inputs(seed: int = 0) -> dict:
    arg_keys = jax.random.split(jax.random.key(seed), 10)
    starting_warmth = scatter_about(arg_keys[0], (GRID_TALL_SIZE, GRID_WIDE_SIZE, GRID_DEEP_SIZE), 1.0, 6.0, ((0, 4), (1, 4), (2, 2)), jnp.float32)
    sheet_stratum_number = plant(jax.random.randint(arg_keys[1], (GRID_TALL_SIZE,), 0, LAYERS), jax.random.fold_in(arg_keys[1], 1), 0, LAYERS - 1).astype(jnp.int32)
    stratum_heat_conduction = jnp.clip(jnp.exp(jax.random.uniform(arg_keys[2], (LAYERS,), jnp.float32, math.log(1.0), math.log(16.0))), 1.0, 16.0)
    substance_kind = plant(jax.random.randint(arg_keys[3], (GRID_TALL_SIZE, GRID_WIDE_SIZE, GRID_DEEP_SIZE), 0, CLASSES), jax.random.fold_in(arg_keys[3], 1), 0, CLASSES - 1).astype(jnp.int32)
    substance_kind_scaling = jnp.clip(1.0 + 0.1 * jax.random.normal(arg_keys[4], (CLASSES,), jnp.float32), 0.5, 1.5)
    wire_piece_amperes = scatter_about(arg_keys[5], (SEGS,), 1.0, 6.0, ((0, 32),), jnp.float32)
    wire_piece_ohms_base = jnp.clip(jnp.exp(math.log(2.0) - 1.3862944 * jax.random.uniform(arg_keys[6], (SEGS,), jnp.float32) ** block_levels(arg_keys[6], (SEGS,), ((0, 32),), -0.2, 0.2)), 0.5, 2.0)
    wire_piece_tile_keys = jax.random.split(jax.random.fold_in(arg_keys[7], 1), SEGS // S_DEV)
    wire_piece_tile_turns = jax.random.permutation(jax.random.fold_in(arg_keys[7], 3), SEGS // S_DEV)
    wire_piece_tile = jax.vmap(lambda own, number: deal_out(jax.random.fold_in(arg_keys[7], 2), own, number, S_DEV, DEVICES, 1, MOST, 1))(wire_piece_tile_keys, wire_piece_tile_turns).reshape((SEGS, 1))
    wire_piece_voxel = plant(jax.random.randint(arg_keys[8], (SEGS,), 0, CZ * CX * CY), jax.random.fold_in(arg_keys[8], 1), 0, (CZ * CX * CY) - 1).astype(jnp.int32)
    return {"starting_warmth": starting_warmth, "sheet_stratum_number": sheet_stratum_number, "stratum_heat_conduction": stratum_heat_conduction, "substance_kind": substance_kind, "substance_kind_scaling": substance_kind_scaling, "wire_piece_amperes": wire_piece_amperes, "wire_piece_ohms_base": wire_piece_ohms_base, "wire_piece_tile": wire_piece_tile, "wire_piece_voxel": wire_piece_voxel}


HEAT_SPREADING = 1000.0
STIFF = 1.5
WARMING_SLOPE = 0.1
OHMIC_POWER = 8.0


def solve_lines(conductance, power_input):
    sub_band = -HEAT_SPREADING * conductance[:-1]
    super_band = -HEAT_SPREADING * conductance[1:]
    main_band = 1.0 + HEAT_SPREADING * (conductance[:-1] + conductance[1:])

    def forward(running, entries):
        factor_before, value_before = running
        lower_entry, middle, upper_entry, right_side = entries
        divisor = middle - lower_entry * factor_before
        factor_now = upper_entry / divisor
        value_now = (right_side - lower_entry * value_before) / divisor
        return (factor_now, value_now), (factor_now, value_now)

    initial = (jnp.zeros(conductance.shape[1:], jnp.float32), jnp.zeros(power_input.shape[1:], jnp.float32))
    ignored, (factors, values) = lax.scan(forward, initial, (sub_band, main_band, super_band, power_input))

    def backward(running, entries):
        factor_now, value_now = entries
        solved = value_now - factor_now * running
        return solved, solved

    ignored, solution = lax.scan(backward, jnp.zeros(power_input.shape[1:], jnp.float32), (factors, values), reverse=True)
    return solution


def outflow_balance(field, conduct, along, to_sink):
    length = field.shape[along]
    lead_field = lax.slice_in_dim(field, 0, length - 1, axis=along)
    next_field = lax.slice_in_dim(field, 1, length, axis=along)
    lead_cond = lax.slice_in_dim(conduct, 0, length - 1, axis=along)
    next_cond = lax.slice_in_dim(conduct, 1, length, axis=along)
    fluxes = 0.5 * (lead_cond + next_cond) * (next_field - lead_field)
    nothing = jnp.zeros_like(lax.slice_in_dim(field, 0, 1, axis=along))
    if to_sink:
        bottom = lax.slice_in_dim(conduct, 0, 1, axis=along) * lax.slice_in_dim(field, 0, 1, axis=along)
    else:
        bottom = nothing
    under = jnp.concatenate([bottom, fluxes], axis=along)
    over = jnp.concatenate([fluxes, nothing], axis=along)
    return over - under


def reference(starting_warmth, sheet_stratum_number, stratum_heat_conduction, substance_kind, substance_kind_scaling, wire_piece_amperes, wire_piece_ohms_base, wire_piece_tile, wire_piece_voxel):
    plane_cond = stratum_heat_conduction[sheet_stratum_number]
    voxel_conductance = plane_cond[:, None, None] * substance_kind_scaling[substance_kind]
    owner_block = wire_piece_tile[:, 0]
    owner_row = owner_block // (N_GY * N_GZ)
    owner_column = (owner_block // N_GZ) % N_GY
    owner_slab = owner_block % N_GZ
    inner_slab = wire_piece_voxel // (CX * CY)
    inner_row = (wire_piece_voxel // CY) % CX
    inner_column = wire_piece_voxel % CY
    flat_index = ((owner_slab * CZ + inner_slab) * GRID_WIDE_SIZE + owner_row * CX + inner_row) * GRID_DEEP_SIZE + owner_column * CY + inner_column
    power = wire_piece_amperes * wire_piece_amperes * wire_piece_ohms_base
    ohmic_loss = jnp.zeros((GRID_TALL_SIZE * GRID_WIDE_SIZE * GRID_DEEP_SIZE,), jnp.float32).at[flat_index.astype(jnp.int32)].add(power).reshape(GRID_TALL_SIZE, GRID_WIDE_SIZE, GRID_DEEP_SIZE)
    edge_zero = jnp.zeros((1, GRID_TALL_SIZE, 1), jnp.float32)
    lateral = STIFF * plane_cond[None, :, None]
    row_faces = jnp.concatenate([edge_zero, jnp.broadcast_to(lateral, (GRID_WIDE_SIZE - 1, GRID_TALL_SIZE, 1)), edge_zero], axis=0)
    column_faces = jnp.concatenate([edge_zero, jnp.broadcast_to(lateral, (GRID_DEEP_SIZE - 1, GRID_TALL_SIZE, 1)), edge_zero], axis=0)
    slab_faces = STIFF * jnp.concatenate([plane_cond[:1], 0.5 * (plane_cond[:-1] + plane_cond[1:]), jnp.zeros((1,), jnp.float32)])
    slab_faces = slab_faces[:, None, None]
    warmth_excess = starting_warmth
    for repeat in range(STEPS):
        warming_energy = (1.0 + WARMING_SLOPE * warmth_excess) * ohmic_loss
        diffusion_term = outflow_balance(warmth_excess, voxel_conductance, 0, True) + outflow_balance(warmth_excess, voxel_conductance, 1, False) + outflow_balance(warmth_excess, voxel_conductance, 2, False)
        power_input = HEAT_SPREADING * diffusion_term + OHMIC_POWER * warming_energy
        first_pass = jnp.moveaxis(solve_lines(row_faces, jnp.moveaxis(power_input, 1, 0)), 0, 1)
        second_pass = jnp.moveaxis(solve_lines(column_faces, jnp.moveaxis(first_pass, 2, 0)), 0, 2)
        vertical_sweep_final = solve_lines(slab_faces, second_pass)
        warmth_excess = warmth_excess + vertical_sweep_final
    ohmic_power_final = (1.0 + WARMING_SLOPE * warmth_excess) * ohmic_loss
    return warmth_excess, ohmic_power_final
```

```python
import functools

import jax
import jax.numpy as jnp
from jax import lax
from jax.experimental import pallas as pl
from jax.experimental.pallas import tpu as pltpu
from jax.sharding import PartitionSpec as P

STEPS = 2
HEAT_SPREADING = 1000.0
STIFF = 1.5
WARMING_SLOPE = 0.1
OHMIC_POWER = 8.0

F32 = jnp.float32
BF16 = jnp.bfloat16
EXTRA = 16
SLOT = 8
EXACT = lax.Precision.HIGHEST


def call(kernel, out_shapes, args, smem=0, vmem=48, flops=0):
    nbytes = sum(a.size * a.dtype.itemsize for a in args)
    nbytes += sum(o.size * o.dtype.itemsize for o in out_shapes)
    specs = [pl.BlockSpec(memory_space=pltpu.SMEM)] * smem
    specs += [pl.BlockSpec(memory_space=pltpu.VMEM)] * (len(args) - smem)
    return pl.pallas_call(
        kernel,
        out_shape=out_shapes,
        in_specs=specs,
        out_specs=[pl.BlockSpec(memory_space=pltpu.VMEM)] * len(out_shapes),
        compiler_params=pltpu.CompilerParams(vmem_limit_bytes=vmem * 2**20),
        cost_estimate=pl.CostEstimate(flops=flops, bytes_accessed=nbytes, transcendentals=0),
    )(*args)


def shaped(*shape, dtype=F32):
    return jax.ShapeDtypeStruct(shape, dtype)


def split(x):
    high = x.astype(BF16)
    return high, (x - high.astype(F32)).astype(BF16)


def iota(shape, dim):
    return lax.broadcasted_iota(jnp.int32, shape, dim)


def mm(a, b):
    return jnp.dot(a, b, preferred_element_type=F32)


def mm_nt(a, b):
    return lax.dot_general(a, b, (((1,), (1,)), ((), ())), preferred_element_type=F32)


def partner(me, k, n):
    return me ^ k if n & (n - 1) == 0 else lax.rem(me + k, n)


def groups(n):
    return [k.bit_length() - 1 for k in range(1, n)]


def all_pairs(arrays, axis):
    n = lax.axis_size(axis)
    return [
        lax.ppermute(arrays[b], axis, [(i, i ^ k) for i in range(n)])
        for k, b in zip(range(1, n), groups(n))
    ]


def next_pairs(even, odd, axis):
    n = lax.axis_size(axis)
    first = lax.ppermute(even, axis, [(i, i ^ 1) for i in range(n)])
    if n == 2:
        return first, first
    other = {i: (i + 1) % n if i % 2 else (i - 1) % n for i in range(n)}
    return first, lax.ppermute(odd, axis, list(other.items()))


def faces_kernel(
    idx, sheet, table, scaling, u_ref, kind_ref, c_ref, xs0, xs1, ys0, ys1, zs0, zs1
):
    planes, rows, columns = u_ref.shape
    even = [idx[d] % 2 == 0 for d in range(3)]
    lane = iota((rows, columns), 1)
    low = jnp.zeros((rows, columns), F32)
    high = jnp.zeros((rows, columns), F32)
    for z in range(planes):
        u, kind = u_ref[z], kind_ref[z]
        factor = jnp.zeros((rows, columns), F32)
        for category in range(scaling.shape[0]):
            factor = jnp.where(kind == category, scaling[category], factor)
        c = table[sheet[idx[2] * planes + z]] * factor
        c_ref[z] = c
        for slot, values in ((0, u), (1, c)):
            at = z * SLOT + slot
            low = jnp.where(lane == at, pltpu.roll(values, at, 1) if at else values, low)
            high = jnp.where(lane == at, pltpu.roll(values, at + 1, 1), high)
            first, last = values[0:1, :], values[rows - 1 : rows, :]
            xs0[slot, z : z + 1, :] = jnp.where(even[0], last, first)
            xs1[slot, z : z + 1, :] = jnp.where(even[0], first, last)
    ys0[...] = jnp.where(even[1], high, low)
    ys1[...] = jnp.where(even[1], low, high)
    for slot, ref in ((0, u_ref), (1, c_ref)):
        zs0[slot] = jnp.where(even[2], ref[planes - 1], ref[0])
        zs1[slot] = jnp.where(even[2], ref[0], ref[planes - 1])


def dispatch_kernel(blocks, capacity, amps, ohms, tile, voxel, send, a_scr, b_scr, o_scr):
    chunks, lanes = amps.shape
    block_row = iota((blocks, lanes), 0)
    for c in range(chunks):
        hit = block_row == tile[c : c + 1, :]
        o_scr[c * blocks : (c + 1) * blocks, :] = jnp.where(hit, 1.0, 0.0).astype(BF16)
    ahead = jnp.where(iota((lanes, lanes), 0) < iota((lanes, lanes), 1), 1.0, 0.0)
    both = jnp.concatenate([ahead, jnp.ones((lanes, lanes), F32)], axis=1).astype(BF16)
    counted = mm(o_scr[...], both)
    base = jnp.zeros((blocks, lanes), F32)
    ranks = iota((capacity, lanes), 0)
    power = amps[...] * amps[...] * ohms[...]
    cell = voxel[...]
    p_high, p_mid = split(power)
    p_low = (power - p_high.astype(F32) - p_mid.astype(F32))
    pieces = [
        p_high.astype(F32),
        p_mid.astype(F32),
        p_low,
        (cell >> 16).astype(F32),
        ((cell >> 8) & 255).astype(F32),
        (cell & 255).astype(F32),
    ]
    for c in range(chunks):
        part = slice(c * blocks, (c + 1) * blocks)
        cols = slice(c * lanes, (c + 1) * lanes)
        hit = block_row == tile[c : c + 1, :]
        order = jnp.where(hit, counted[part, :lanes] + base, 0.0)
        base = base + counted[part, lanes:]
        rank = jnp.sum(order, axis=0, keepdims=True).astype(jnp.int32)
        b_scr[:, cols] = jnp.where(ranks == rank, 1.0, 0.0).astype(BF16)
        for k, piece in enumerate(pieces):
            a_scr[k * blocks : (k + 1) * blocks, cols] = jnp.where(
                hit, piece[c : c + 1, :], 0.0
            ).astype(BF16)
    out = mm_nt(a_scr[...], b_scr[...])
    r = [out[k * blocks : (k + 1) * blocks] for k in range(6)]
    send[...] = jnp.concatenate(
        [r[0] + r[1] + r[2], r[3] * 65536.0 + r[4] * 256.0 + r[5]], axis=1
    )


def joule_into(got, joule, r_scr, k_scr):
    planes, rows, columns = joule.shape
    sources, capacity = got.shape[0], got.shape[1] // 2
    column = iota((columns, capacity), 0)
    for s in range(sources):
        power = got[s : s + 1, :capacity]
        cell = got[s : s + 1, capacity:].astype(jnp.int32)
        part = slice(s * capacity, (s + 1) * capacity)
        high, low = split(power)
        hit = column == cell % columns
        r_scr[:columns, part] = jnp.where(hit, high.astype(F32), 0.0).astype(BF16)
        r_scr[columns:, part] = jnp.where(hit, low.astype(F32), 0.0).astype(BF16)
        k_scr[:, part] = jnp.broadcast_to(cell // columns, (8, capacity))
    total = sources * capacity
    step = min(total, 2048)
    row = iota((rows, step), 0)

    def plane(z, carry):
        sums = jnp.zeros((rows, 2 * columns), F32)
        for at in range(0, total, step):
            hit = row == k_scr[0:1, at : at + step] - z * rows
            onehot = jnp.where(hit, 1.0, 0.0).astype(BF16)
            sums = sums + mm_nt(onehot, r_scr[:, at : at + step])
        joule[z] = sums[:, :columns] + sums[:, columns:]
        return carry

    lax.fori_loop(0, planes, plane, 0)


def line_parts(position, theta, start, cells):
    growing = jnp.exp(position * theta)
    lower = growing * (1.0 + jnp.exp(-(2.0 * (start + position) + 1.0) * theta))
    upper = (1.0 + jnp.exp(-(2.0 * (cells - start - position) - 1.0) * theta)) / growing
    return lower, upper


def prep_kernel(
    sizes, idx, sheet, table, gx_ref, psx, phx, dx, gyh, gyl, dy, cyh, cyl, phz, psz, mz, wz,
    low_scr, high_scr,
):
    planes, rows, columns, nx, ny, nz = sizes
    lanes = 128
    extent = rows + EXTRA
    gx, gy, gz = idx[0], idx[1], idx[2]
    x0, xn = (gx * rows).astype(F32), float(nx * rows)
    y0, yn = (gy * columns).astype(F32), float(ny * columns)

    def line(conduct, cells):
        lead = HEAT_SPREADING * STIFF * conduct
        t = 0.5 / jnp.sqrt(lead)
        theta = 2.0 * jnp.log1p(t + t * t / (1.0 + jnp.sqrt(1.0 + t * t)))
        scale = 1.0 / (jnp.sqrt(4.0 * lead + 1.0) * (1.0 - jnp.exp(-2.0 * cells * theta)))
        return theta, scale

    lane_plane = iota((8, lanes), 1) // SLOT
    row8 = iota((8, lanes), 0)
    by_lane = jnp.ones((8, lanes), F32)
    by_row = jnp.ones((planes, lanes), F32)
    own = []
    for z in range(planes):
        value = table[sheet[gz * planes + z]]
        own.append(value)
        by_lane = jnp.where(lane_plane == z, value, by_lane)
        by_row = jnp.where(iota((planes, lanes), 0) == z, value, by_row)
    theta_rows, _ = line(by_row, 1.0)
    theta_lane, _ = line(by_lane, 1.0)
    for k in range(nx):
        dx[k] = jnp.exp(-float(k * rows) * theta_rows)
    for k in range(ny):
        dy[k] = jnp.exp(-float(k * columns) * theta_lane)

    order = iota((extent, lanes), 0)
    wide = jnp.where(order == rows, -1, jnp.where(order == rows + 1, rows, order))
    position = wide.astype(F32)
    real = order < rows + 2
    j = iota((8, rows), 1)
    wide2 = jnp.concatenate([wide] * (rows // lanes), axis=1)
    order2 = jnp.concatenate([order] * (rows // lanes), axis=1)
    jj = iota((extent, rows), 1)
    y_lane = iota((8, columns), 1).astype(F32)
    y_col = iota((columns, columns), 0).astype(F32)
    y_i, y_j = iota((columns, columns), 0), iota((columns, columns), 1)
    for z in range(planes):
        theta, k_x = line(jnp.full((8, lanes), own[z], F32), xn)
        theta1, k1 = theta[0:1, :], k_x[0:1, :]
        low_c, high_c = line_parts(position, theta1, x0, xn)
        phx[z] = jnp.where(real, low_c * k1, 0.0)
        psx[z] = jnp.where(real, high_c * k1, 0.0)
        theta2 = jnp.concatenate([theta1] * (rows // lanes), axis=1)
        low_r, high_r = line_parts(j.astype(F32), jnp.broadcast_to(theta2, (8, rows)), x0, xn)
        low_r, high_r = low_r[0:1, :], high_r[0:1, :]
        low_k = jnp.concatenate([phx[z]] * (rows // lanes), axis=1)
        high_k = jnp.concatenate([psx[z]] * (rows // lanes), axis=1)
        g = jnp.where(wide2 >= jj, high_k * low_r, low_k * high_r)
        g = jnp.where(order2 == rows + 2, low_r, jnp.where(order2 == rows + 3, high_r, g))
        gx_ref[z, :extent, :], gx_ref[z, extent:, :] = split(g)

        theta, k_y = line(jnp.full((8, lanes), own[z], F32), yn)
        theta1, k1 = theta[0:1, :], k_y[0:1, :]
        low_r, high_r = line_parts(y_lane[0:1, :], theta1, y0, yn)
        low_c, high_c = line_parts(y_col, theta1, y0, yn)
        low_b, high_b = line_parts(jnp.full((1, lanes), -1.0, F32), theta1, y0, yn)
        low_t, high_t = line_parts(jnp.full((1, lanes), float(columns), F32), theta1, y0, yn)
        g = k1 * jnp.where(y_j >= y_i, high_r * low_c, low_r * high_c)
        ext = jnp.zeros((columns, lanes), F32)
        for slot, values in enumerate((low_b * high_c * k1, high_t * low_c * k1, low_c, high_c)):
            ext = jnp.where(y_j == z * SLOT + slot, values, ext)
        gyh[z, :, :lanes], gyl[z, :, :lanes] = split(g)
        gyh[z, :, lanes:], gyl[z, :, lanes:] = split(ext)
        add = jnp.where(
            y_i == z * SLOT + 2, high_r * k1, jnp.where(y_i == z * SLOT + 3, low_r * k1, 0.0)
        )
        cyh[:, z * lanes : (z + 1) * lanes], cyl[:, z * lanes : (z + 1) * lanes] = split(add)
        ghost_low = jnp.where(
            y_i == z * SLOT + 2, high_b * k1, jnp.where(y_i == z * SLOT + 3, low_b * k1, 0.0)
        )
        ghost_high = jnp.where(
            y_i == z * SLOT + 2, high_t * k1, jnp.where(y_i == z * SLOT + 3, low_t * k1, 0.0)
        )
        low_scr[z] = jnp.where(
            y_j == z * SLOT, ghost_low, jnp.where(y_j == z * SLOT + 1, ghost_high, 0.0)
        )
    ghosts = low_scr[0]
    for z in range(1, planes):
        ghosts = ghosts + low_scr[z]
    cyh[:, planes * lanes :], cyl[:, planes * lanes :] = split(ghosts)

    total = planes * nz
    cond = [jnp.full((8, lanes), table[sheet[z]], F32) for z in range(total)]
    lead = [HEAT_SPREADING * STIFF * 0.5 * (cond[z] + cond[z + 1]) for z in range(total - 1)]
    lower = [jnp.ones((8, lanes), F32)]
    flux = HEAT_SPREADING * STIFF * cond[0]
    resist = [1.0 / value for value in lead]
    for z in range(total - 1):
        flux = flux + lower[z]
        lower.append(lower[z] + flux * resist[z])
    weight = 1.0 / (flux + lower[total - 1])
    upper = [None] * total
    upper[total - 1] = weight
    flux = jnp.zeros((8, lanes), F32)
    for z in range(total - 2, -1, -1):
        flux = flux + upper[z + 1]
        upper[z] = upper[z + 1] + flux * resist[z]
    zero = jnp.zeros((8, lanes), F32)
    high_scr[0], high_scr[total + 3] = zero, zero
    high_scr[total + 1], high_scr[total + 2] = zero, zero
    for z in range(total):
        high_scr[1 + z] = lower[z]
        high_scr[total + 3 + z] = upper[z]
    high_scr[2 * total + 3] = zero
    mine = gz * planes
    for z in range(planes + 2):
        phz[z] = high_scr[mine + z]
        psz[z] = jnp.where(mine + z == 0, zero, high_scr[total + 2 + mine + z])

    lower_lane, upper_lane = zero, zero
    for z in range(planes):
        lower_lane = jnp.where(lane_plane == z, phz[z + 1], lower_lane)
        upper_lane = jnp.where(lane_plane == z, psz[z + 1], upper_lane)
    lane8 = iota((8, lanes), 1)
    slot = lane8 % SLOT
    mz[...] = jnp.zeros(mz.shape, F32)
    for z in range(planes):
        part = slice(z * SLOT, (z + 1) * SLOT)
        g = jnp.where(lane_plane >= z, phz[z + 1] * upper_lane, psz[z + 1] * lower_lane)
        keep = (slot == row8) & (row8 < 2) & (lane_plane < planes)
        mz[part, :lanes] = jnp.where(keep, g, 0.0)
        mz[part, lanes:] = jnp.where(
            (lane8 == row8) & (row8 < 2),
            phz[z + 1],
            jnp.where((lane8 == row8 + 2) & (row8 < 2), psz[z + 1], 0.0),
        )
    wz[...] = jnp.where(
        (row8 < 2) & (slot == row8),
        upper_lane,
        jnp.where((row8 >= 2) & (row8 < 4) & (slot == row8 - 2), lower_lane, 0.0),
    )


def outflow(z, idx, counts, u_ref, c_ref, ux, cx, uy, cy, uz, cz):
    planes, rows, columns = u_ref.shape
    at_low = [idx[d] == 0 for d in range(3)]
    at_high = [idx[d] == counts[d] - 1 for d in range(3)]
    u, c = u_ref[z], c_ref[z]
    row, lane = iota((rows, columns), 0), iota((rows, columns), 1)

    def pair(other_u, other_c):
        return (c + other_c) * (other_u - u)

    lo_u = jnp.where(at_low[0], u[0:1, :], ux[z, 0:1, :])
    hi_u = jnp.where(at_high[0], u[rows - 1 : rows, :], ux[z, 1:2, :])
    total = pair(
        jnp.where(row == 0, lo_u, pltpu.roll(u, 1, 0)),
        jnp.where(row == 0, cx[z, 0:1, :], pltpu.roll(c, 1, 0)),
    )
    total += pair(
        jnp.where(row == rows - 1, hi_u, pltpu.roll(u, rows - 1, 0)),
        jnp.where(row == rows - 1, cx[z, 1:2, :], pltpu.roll(c, rows - 1, 0)),
    )
    low = (columns - z * SLOT) % columns
    high = columns - 2 - z * SLOT

    def moved(values, by):
        return pltpu.roll(values, by, 1) if by else values

    lo_u = jnp.where(at_low[1], u, moved(uy[:rows, :], low))
    hi_u = jnp.where(at_high[1], u, moved(uy[:rows, :], high))
    total += pair(
        jnp.where(lane == 0, lo_u, pltpu.roll(u, 1, 1)),
        jnp.where(lane == 0, moved(cy[...], low), pltpu.roll(c, 1, 1)),
    )
    total += pair(
        jnp.where(lane == columns - 1, hi_u, pltpu.roll(u, columns - 1, 1)),
        jnp.where(lane == columns - 1, moved(cy[...], high), pltpu.roll(c, columns - 1, 1)),
    )
    if z == 0:
        total += pair(jnp.where(at_low[2], 0.0, uz[0]), jnp.where(at_low[2], c, cz[0]))
    else:
        total += pair(u_ref[z - 1], c_ref[z - 1])
    if z == planes - 1:
        total += pair(jnp.where(at_high[2], u, uz[1]), cz[1])
    else:
        total += pair(u_ref[z + 1], c_ref[z + 1])
    return (0.5 * HEAT_SPREADING) * total


def slope_kernel(
    counts, idx, u_ref, c_ref, xr0, xr1, yr0, yr1, zr0, zr1, d_ref, ux, cx, uy, cy, uz, cz
):
    planes, rows, columns = u_ref.shape
    even = [idx[d] % 2 == 0 for d in range(3)]

    def ends(first, second, d):
        return jnp.where(even[d], second, first), jnp.where(even[d], first, second)

    for slot, out in ((0, ux), (1, cx)):
        low, high = ends(xr0[slot], xr1[slot], 0)
        out[...] = jnp.zeros(out.shape, F32)
        for z in range(planes):
            out[z, 0:1, :] = low[z : z + 1, :]
            out[z, 1:2, :] = high[z : z + 1, :]
    low, high = ends(yr0[...], yr1[...], 1)
    slot = iota((rows, 128), 1) % SLOT
    uy[...] = jnp.zeros(uy.shape, F32)
    uy[:rows, :] = jnp.where(slot == 0, low, jnp.where(slot == 1, pltpu.roll(high, 1, 1), 0.0))
    cy[...] = jnp.where(slot == 0, pltpu.roll(low, 127, 1), jnp.where(slot == 1, high, 0.0))
    for slot, out in ((0, uz), (1, cz)):
        out[0], out[1] = ends(zr0[slot], zr1[slot], 2)
    for z in range(planes):
        d_ref[z] = outflow(z, idx, counts, u_ref, c_ref, ux, cx, uy, cy, uz, cz)


def rows_solve(z, idx, source, gx_ref, t_ref, sends):
    rows = source.shape[0]
    columns = source.shape[1]
    extent = rows + EXTRA
    high, low = split(source)
    out = mm(gx_ref[z], jnp.concatenate([high, low], axis=1))
    t = out[:extent, :columns] + (out[:extent, columns:] + out[extent:, :columns])
    t_ref[z] = t
    for b, send in enumerate(sends):
        below = (idx[0] >> b) % 2 == 0
        send[z : z + 1, :] = jnp.where(
            below, t[rows + 2 : rows + 3, :], t[rows + 3 : rows + 4, :]
        )


def start_kernel(idx, got, d_ref, u_ref, gx_ref, joule, t_ref, *rest):
    sends, (r_scr, k_scr) = rest[:-2], rest[-2:]
    joule_into(got, joule, r_scr, k_scr)
    for z in range(u_ref.shape[0]):
        source = d_ref[z] + OHMIC_POWER * ((1.0 + WARMING_SLOPE * u_ref[z]) * joule[z])
        rows_solve(z, idx, source, gx_ref, t_ref, sends)


def columns_kernel(nx, idx, t_ref, dx, psx, phx, gyh, gyl, *rest):
    gots, (first_ref, y_ref) = rest[:-2], rest[-2:]
    planes, extent, columns = t_ref.shape
    me = idx[0]
    below = jnp.zeros(gots[0].shape, F32)
    above = jnp.zeros(gots[0].shape, F32)
    for k, got in zip(range(1, nx), gots):
        other = me ^ k
        value = got[...] * dx[jnp.abs(me - other)]
        below += jnp.where(other < me, value, 0.0)
        above += jnp.where(other > me, value, 0.0)
    sums = jnp.zeros((extent, 128), F32)
    for z in range(planes):
        first = t_ref[z] + psx[z] * below[z : z + 1, :] + phx[z] * above[z : z + 1, :]
        high, low = split(first)
        out = mm(jnp.concatenate([high, low], axis=0), gyh[z])
        out = out[:extent] + out[extent:] + mm(high, gyl[z])
        first_ref[z] = out[:, :columns]
        sums = sums + out[:, columns:]
    y_ref[...] = sums


def planes_kernel(ny, idx, t_ref, y_ref, dy, cyh, cyl, phz, psz, mz, *rest):
    gots, rest = rest[: ny - 1], rest[ny - 1 :]
    second_ref, q_ref = rest[:2]
    sends = rest[2:]
    planes, extent, columns = t_ref.shape
    rows = extent - EXTRA
    me = idx[1]
    slot = iota((8, 128), 1) % SLOT
    others = jnp.zeros((extent, 128), F32)
    for k, got in zip(range(1, ny), gots):
        other = me ^ k
        keep = jnp.where(other < me, 2, 3)
        factor = jnp.where(slot == keep, dy[jnp.abs(me - other)], 0.0)
        others += got[...] * factor[0:1, :]
    high, low = split(others)
    pair = jnp.concatenate([high, low], axis=0)
    below = jnp.zeros((extent, columns), F32)
    above = jnp.zeros((extent, columns), F32)

    def added(part):
        out = mm(pair, cyh[:, part])
        return out[:extent] + out[extent:] + mm(high, cyl[:, part])

    for z in range(planes):
        second = t_ref[z] + added(slice(z * 128, (z + 1) * 128))
        second_ref[z] = second
        below += phz[z + 1, 0:1, :] * second
        above += psz[z + 1, 0:1, :] * second
    slots = iota((extent, 128), 1) % SLOT
    q = y_ref[...] + added(slice(planes * 128, (planes + 1) * 128))
    q = jnp.where(slots < 2, q, 0.0)
    q_ref[...] = q
    edge = jnp.dot(q[:rows], mz[:, 128:], precision=EXACT, preferred_element_type=F32).T
    for b, send in enumerate(sends):
        lower = (idx[2] >> b) % 2 == 0
        send[: rows + 8, :] = jnp.where(lower, below[: rows + 8], above[: rows + 8])
        for part in range(rows // 128):
            at = rows + 8 + 8 * part
            send[at : at + 8, :] = edge[0:8, part * 128 : (part + 1) * 128]


def carried(nz, idx, gots, rows):
    me = idx[2]
    below, above = None, None
    for k, got in zip(range(1, nz), gots):
        other = me ^ k
        value = got[:rows]
        lower = jnp.where(other < me, value, 0.0)
        higher = jnp.where(other < me, 0.0, value)
        below = lower if below is None else below + lower
        above = higher if above is None else above + higher
    return below, above


def change(z_range, second_ref, phz, psz, below, above, rows, emit):
    planes = second_ref.shape[0]
    tails = [above]
    for z in range(planes - 1, -1, -1):
        tails.append(tails[-1] + psz[z + 1, 0:1, :] * second_ref[z, :rows, :])
    tails = tails[::-1]
    if z_range:
        emit(-1, psz[0, 0:1, :] * below + phz[0, 0:1, :] * tails[0])
    head = below
    for z in range(planes):
        head = head + phz[z + 1, 0:1, :] * second_ref[z, :rows, :]
        emit(z, psz[z + 1, 0:1, :] * head + phz[z + 1, 0:1, :] * tails[z + 1])
    if z_range:
        emit(planes, psz[planes + 1, 0:1, :] * head + phz[planes + 1, 0:1, :] * above)


def rise_kernel(counts, idx, second_ref, q_ref, phz, psz, mz, wz, u_ref, ux, uy, uz,
                c_ref, cx, cy, cz, joule, gx_ref, *rest):
    nz = counts[2]
    gots, rest = rest[: nz - 1], rest[nz - 1 :]
    u_out, ux_out, uy_out, uz_out, t_ref = rest[:5]
    sends = rest[5:]
    planes, rows, columns = u_ref.shape
    below, above = carried(nz, idx, gots, rows + 8)

    def emit(z, value):
        if z == -1:
            uz_out[0] = uz[0] + value[:rows]
        elif z == planes:
            uz_out[1] = uz[1] + value[:rows]
        else:
            u_out[z] = u_ref[z] + value[:rows]
            ux_out[z] = ux[z] + value[rows:]

    change(True, second_ref, phz, psz, below, above, rows + 8, emit)
    edges = jnp.zeros((8, rows), F32)
    sub = iota((8, rows), 0)
    me = idx[2]
    for k, got in zip(range(1, nz), gots):
        other = me ^ k
        value = jnp.concatenate(
            [got[rows + 8 + 8 * p : rows + 16 + 8 * p, :] for p in range(rows // 128)], axis=1
        )
        keep = jnp.where(other < me, 0, 1)
        edges += jnp.where(sub // 2 == keep, value, 0.0)
    q = q_ref[:rows, :]
    grown = jnp.dot(q, mz[:, :128], precision=EXACT, preferred_element_type=F32)
    grown += jnp.dot(edges.T, wz[...], precision=EXACT, preferred_element_type=F32)
    uy_out[...] = uy[...]
    uy_out[:rows, :] = uy[:rows, :] + grown
    for z in range(planes):
        source = outflow(
            z, idx, counts, u_out, c_ref, ux_out, cx, uy_out, cy, uz_out, cz
        ) + OHMIC_POWER * ((1.0 + WARMING_SLOPE * u_out[z]) * joule[z])
        rows_solve(z, idx, source, gx_ref, t_ref, sends)


def finish_kernel(counts, idx, second_ref, phz, psz, u_ref, joule, *rest):
    nz = counts[2]
    gots, (u_out, heat_out) = rest[: nz - 1], rest[nz - 1 :]
    rows = u_ref.shape[1]
    below, above = carried(nz, idx, gots, rows)

    def emit(z, value):
        u = u_ref[z] + value
        u_out[z] = u
        heat_out[z] = (1.0 + WARMING_SLOPE * u) * joule[z]

    change(False, second_ref, phz, psz, below, above, rows, emit)


def per_device(
    starting_warmth,
    sheet_stratum_number,
    stratum_heat_conduction,
    substance_kind,
    substance_kind_scaling,
    wire_piece_amperes,
    wire_piece_ohms_base,
    wire_piece_tile,
    wire_piece_voxel,
):
    planes, rows, columns = starting_warmth.shape
    counts = tuple(lax.axis_size(axis) for axis in ("gx", "gy", "gz"))
    nx, ny, nz = counts
    bits = [(n - 1).bit_length() for n in counts]
    devices = nx * ny * nz
    extent = rows + EXTRA
    idx = jnp.stack([lax.axis_index(axis) for axis in ("gx", "gy", "gz")]).astype(jnp.int32)
    block = shaped(planes, rows, columns)
    number, table = sheet_stratum_number, stratum_heat_conduction

    count = wire_piece_amperes.shape[0]
    capacity = 2 * count // devices
    lanes = 128
    chunks = count // lanes
    send = pl.pallas_call(
        functools.partial(dispatch_kernel, devices, capacity),
        out_shape=shaped(devices, 2 * capacity),
        in_specs=[pl.BlockSpec(memory_space=pltpu.VMEM)] * 4,
        out_specs=pl.BlockSpec(memory_space=pltpu.VMEM),
        scratch_shapes=[
            pltpu.VMEM((6 * devices, count), BF16),
            pltpu.VMEM((capacity, count), BF16),
            pltpu.VMEM((chunks * devices, lanes), BF16),
        ],
        compiler_params=pltpu.CompilerParams(vmem_limit_bytes=48 * 2**20),
    )(
        wire_piece_amperes.reshape(chunks, lanes),
        wire_piece_ohms_base.reshape(chunks, lanes),
        wire_piece_tile.reshape(chunks, lanes),
        wire_piece_voxel.reshape(chunks, lanes),
    )
    got = lax.all_to_all(send, ("gx", "gy", "gz"), split_axis=0, concat_axis=0, tiled=True)

    c, xs0, xs1, ys0, ys1, zs0, zs1 = call(
        faces_kernel,
        [block]
        + [shaped(2, planes, columns)] * 2
        + [shaped(rows, 128)] * 2
        + [shaped(2, rows, columns)] * 2,
        (idx, number, table, substance_kind_scaling, starting_warmth, substance_kind),
        smem=4,
    )
    zr = next_pairs(zs0, zs1, "gz")
    xr = next_pairs(xs0, xs1, "gx")
    yr = next_pairs(ys0, ys1, "gy")
    sizes = (planes, rows, columns, nx, ny, nz)
    prep_out = [
        shaped(planes, 2 * extent, rows, dtype=BF16),
        shaped(planes, extent, columns),
        shaped(planes, extent, columns),
        shaped(nx, planes, lanes),
        shaped(planes, columns, 256, dtype=BF16),
        shaped(planes, columns, 256, dtype=BF16),
        shaped(ny, 8, lanes),
        shaped(lanes, (planes + 1) * lanes, dtype=BF16),
        shaped(lanes, (planes + 1) * lanes, dtype=BF16),
        shaped(planes + 2, 8, lanes),
        shaped(planes + 2, 8, lanes),
        shaped(lanes, 256),
        shaped(8, lanes),
    ]
    gx_m, psx, phx, dx, gyh, gyl, dy, cyh, cyl, phz, psz, mz, wz = pl.pallas_call(
        functools.partial(prep_kernel, sizes),
        out_shape=prep_out,
        in_specs=[pl.BlockSpec(memory_space=pltpu.SMEM)] * 3,
        out_specs=[pl.BlockSpec(memory_space=pltpu.VMEM)] * len(prep_out),
        scratch_shapes=[
            pltpu.VMEM((planes, lanes, lanes), F32),
            pltpu.VMEM((2 * planes * nz + 4, 8, lanes), F32),
        ],
        compiler_params=pltpu.CompilerParams(vmem_limit_bytes=48 * 2**20),
    )(idx, number, table)
    d0, ux, cx, uy, cy, uz, cz = call(
        functools.partial(slope_kernel, counts),
        [block]
        + [shaped(planes, 8, columns)] * 2
        + [shaped(extent, 128), shaped(rows, 128)]
        + [shaped(2, rows, columns)] * 2,
        (idx, starting_warmth, c, *xr, *yr, *zr),
        smem=1,
    )
    x_sends = [shaped(planes, columns)] * bits[0]
    total = devices * capacity
    outs = [block, shaped(planes, extent, columns)] + x_sends
    joule, t, *sends = pl.pallas_call(
        start_kernel,
        out_shape=outs,
        in_specs=[pl.BlockSpec(memory_space=pltpu.SMEM)]
        + [pl.BlockSpec(memory_space=pltpu.VMEM)] * 4,
        out_specs=[pl.BlockSpec(memory_space=pltpu.VMEM)] * len(outs),
        scratch_shapes=[
            pltpu.VMEM((2 * columns, total), BF16),
            pltpu.VMEM((8, total), jnp.int32),
        ],
        compiler_params=pltpu.CompilerParams(vmem_limit_bytes=48 * 2**20),
    )(idx, got, d0, starting_warmth, gx_m)
    u = starting_warmth
    for repeat in range(STEPS):
        gots = all_pairs(sends, "gx")
        first, y_own = call(
            functools.partial(columns_kernel, nx),
            [shaped(planes, extent, columns), shaped(extent, 128)],
            (idx, t, dx, psx, phx, gyh, gyl, *gots),
            smem=1,
        )
        gots = all_pairs([y_own] * bits[1], "gy")
        z_rows = rows + 8 + 8 * (rows // 128)
        second, q, *sends = call(
            functools.partial(planes_kernel, ny),
            [shaped(planes, extent, columns), shaped(extent, 128)]
            + [shaped(z_rows, 128)] * bits[2],
            (idx, first, y_own, dy, cyh, cyl, phz, psz, mz, *gots),
            smem=1,
        )
        gots = all_pairs(sends, "gz")
        if repeat < STEPS - 1:
            u, ux, uy, uz, t, *sends = call(
                functools.partial(rise_kernel, counts),
                [block, shaped(planes, 8, columns), shaped(extent, 128)]
                + [shaped(2, rows, columns), shaped(planes, extent, columns)]
                + x_sends,
                (idx, second, q, phz, psz, mz, wz, u, ux, uy, uz, c, cx, cy, cz, joule, gx_m)
                + tuple(gots),
                smem=1,
            )
    return tuple(
        call(
            functools.partial(finish_kernel, counts),
            [block, block],
            (idx, second, phz, psz, u, joule, *gots),
            smem=1,
        )
    )


def solution(mesh):
    return jax.shard_map(
        per_device,
        mesh=mesh,
        in_specs=(
            P("gz", "gx", "gy"),
            P(),
            P(),
            P("gz", "gx", "gy"),
            P(),
            P(("gx", "gy", "gz")),
            P(("gx", "gy", "gz")),
            P(("gx", "gy", "gz"), None),
            P(("gx", "gy", "gz")),
        ),
        out_specs=(P("gz", "gx", "gy"), P("gz", "gx", "gy")),
        check_vma=False,
    )
```

```python
import functools

import jax
import jax.numpy as jnp
from jax import lax
from jax.experimental import pallas as pl
from jax.experimental.pallas import tpu as pltpu
from jax.sharding import PartitionSpec as P

STEPS = 2
HEAT_SPREADING = 1000.0
STIFF = 1.5
WARMING_SLOPE = 0.1
OHMIC_POWER = 8.0

F32 = jnp.float32
BF16 = jnp.bfloat16
EXTRA = 16
EXACT = lax.Precision.HIGHEST


def call(kernel, out_shapes, args, smem=0, scratch=(), vmem=24):
    specs = [pl.BlockSpec(memory_space=pltpu.SMEM)] * smem
    specs += [pl.BlockSpec(memory_space=pltpu.VMEM)] * (len(args) - smem)
    return pl.pallas_call(
        kernel,
        out_shape=out_shapes,
        in_specs=specs,
        out_specs=[pl.BlockSpec(memory_space=pltpu.VMEM)] * len(out_shapes),
        scratch_shapes=list(scratch),
        compiler_params=pltpu.CompilerParams(vmem_limit_bytes=vmem * 2**20),
        cost_estimate=pl.CostEstimate(flops=0, bytes_accessed=1, transcendentals=0),
    )(*args)


def shaped(*shape, dtype=F32):
    return jax.ShapeDtypeStruct(shape, dtype)


def split(x):
    high = x.astype(BF16)
    return high, (x - high.astype(F32)).astype(BF16)


def iota(shape, dim):
    return lax.broadcasted_iota(jnp.int32, shape, dim)


def mm(a, b):
    return jnp.dot(a, b, preferred_element_type=F32)


def exact(a, b, dims=((1,), (0,))):
    return lax.dot_general(a, b, (dims, ((), ())), precision=EXACT, preferred_element_type=F32)


def mm_nt(a, b):
    return lax.dot_general(a, b, (((1,), (1,)), ((), ())), preferred_element_type=F32)


def table_rows(planes, rows, columns, nx, ny, nz):
    at, places = 0, {}
    for name, items, each in (
        ("lx", 1, rows + EXTRA),
        ("ax", nz * (rows // 128), 2 * planes),
        ("by", nz, 2 * planes),
        ("dx", nx, planes),
        ("dxl", nx, 8),
        ("dy", ny, planes),
        ("cg", 1, 128),
        ("phz", planes + 2, 8),
        ("psz", planes + 2, 8),
        ("mz", 2, 128),
        ("wz", 1, 8),
    ):
        places[name] = (at, each)
        at += items * each
    return places, at


class Group:
    def __init__(self, ref, place):
        self.ref, (self.at, self.each) = ref, place

    def rows(self, k):
        at = self.at + k * self.each
        return pl.ds(at if isinstance(at, int) else pl.multiple_of(at, 8), self.each)

    def __getitem__(self, k):
        return self.ref[self.rows(k), :]

    def __setitem__(self, k, value):
        self.ref[self.rows(k), :] = value


def groups_of(sizes, ref, *names):
    places, _ = table_rows(*sizes)
    return [Group(ref, places[name]) for name in names]


def partner(me, k, n):
    return me ^ k


def groups(n):
    return [k.bit_length() - 1 for k in range(1, n)]


def all_pairs(arrays, axis):
    n = lax.axis_size(axis)
    return [
        lax.ppermute(arrays[b], axis, [(i, i ^ k) for i in range(n)])
        for k, b in zip(range(1, n), groups(n))
    ]


def next_pairs(even, odd, axis):
    n = lax.axis_size(axis)
    first = lax.ppermute(even, axis, [(i, i ^ 1) for i in range(n)])
    if n == 2:
        return first, first
    other = {i: (i + 1) % n if i % 2 else (i - 1) % n for i in range(n)}
    return first, lax.ppermute(odd, axis, list(other.items()))


def conductance(z, idx, scalars, kind_ref, n_planes):
    factor = jnp.zeros(kind_ref.shape[1:], F32)
    for category in range(scalars.shape[0] - n_planes):
        factor = jnp.where(kind_ref[z] == category, scalars[n_planes + category], factor)
    return scalars[idx[2] * kind_ref.shape[0] + z] * factor


def faces_kernel(
    n_planes, idx, scalars, u_ref, kind_ref, xs0, xs1, ys0, ys1, zs0, zs1
):
    planes, rows, columns = u_ref.shape
    even = [idx[d] % 2 == 0 for d in range(3)]
    lane = iota((rows, columns), 1)
    low = jnp.zeros((rows, columns), F32)
    high = jnp.zeros((rows, columns), F32)
    for z in range(planes):
        u, c = u_ref[z], conductance(z, idx, scalars, kind_ref, n_planes)
        if z == 0:
            zs0[1], zs1[1] = c, c
        elif z == planes - 1:
            zs0[1] = jnp.where(even[2], c, zs0[1])
            zs1[1] = jnp.where(even[2], zs1[1], c)
        for slot, values in ((0, u), (1, c)):
            at = slot * planes + z
            low = jnp.where(lane == at, pltpu.roll(values, at, 1) if at else values, low)
            high = jnp.where(lane == at, pltpu.roll(values, at + 1, 1), high)
            first, last = values[0:1, :], values[rows - 1 : rows, :]
            xs0[slot, z : z + 1, :] = jnp.where(even[0], last, first)
            xs1[slot, z : z + 1, :] = jnp.where(even[0], first, last)
    ys0[...] = jnp.where(even[1], high, low)
    ys1[...] = jnp.where(even[1], low, high)
    zs0[0] = jnp.where(even[2], u_ref[planes - 1], u_ref[0])
    zs1[0] = jnp.where(even[2], u_ref[0], u_ref[planes - 1])


def dispatch_kernel(blocks, capacity, segments, send, a_scr, b_scr, o_scr):
    _, chunks, lanes = segments.shape
    power, tile, cell = segments[0], segments[1].astype(jnp.int32), segments[2].astype(jnp.int32)
    block_row = iota((blocks, lanes), 0)
    for c in range(chunks):
        hit = block_row == tile[c : c + 1, :]
        o_scr[c * blocks : (c + 1) * blocks, :] = jnp.where(hit, 1.0, 0.0).astype(BF16)
    ahead = jnp.where(iota((lanes, lanes), 0) < iota((lanes, lanes), 1), 1.0, 0.0)
    both = jnp.concatenate([ahead, jnp.ones((lanes, lanes), F32)], axis=1).astype(BF16)
    counted = mm(o_scr[...], both)
    base = jnp.zeros((blocks, lanes), F32)
    ranks = iota((capacity, lanes), 0)
    p_high, p_mid = split(power)
    p_low = (power - p_high.astype(F32) - p_mid.astype(F32))
    pieces = [
        p_high.astype(F32),
        p_mid.astype(F32),
        p_low,
        (cell >> 16).astype(F32),
        ((cell >> 8) & 255).astype(F32),
        (cell & 255).astype(F32),
    ]
    for c in range(chunks):
        part = slice(c * blocks, (c + 1) * blocks)
        cols = slice(c * lanes, (c + 1) * lanes)
        hit = block_row == tile[c : c + 1, :]
        order = jnp.where(hit, counted[part, :lanes] + base, 0.0)
        base = base + counted[part, lanes:]
        rank = jnp.sum(order, axis=0, keepdims=True).astype(jnp.int32)
        b_scr[:, cols] = jnp.where(ranks == rank, 1.0, 0.0).astype(BF16)
        for k, piece in enumerate(pieces):
            a_scr[k * blocks : (k + 1) * blocks, cols] = jnp.where(
                hit, piece[c : c + 1, :], 0.0
            ).astype(BF16)
    out = mm_nt(a_scr[...], b_scr[...])
    r = [out[k * blocks : (k + 1) * blocks] for k in range(6)]
    send[...] = jnp.concatenate(
        [r[0] + r[1] + r[2], r[3] * 65536.0 + r[4] * 256.0 + r[5]], axis=1
    )


def joule_into(got, joule, r_scr, k_scr):
    planes, rows, columns = joule.shape
    sources, capacity = got.shape[0], got.shape[1] // 2
    column = iota((columns, capacity), 0)
    for s in range(sources):
        power = got[s : s + 1, :capacity]
        cell = got[s : s + 1, capacity:].astype(jnp.int32)
        part = slice(s * capacity, (s + 1) * capacity)
        high, low = split(power)
        hit = column == cell % columns
        r_scr[:columns, part] = jnp.where(hit, high.astype(F32), 0.0).astype(BF16)
        r_scr[columns:, part] = jnp.where(hit, low.astype(F32), 0.0).astype(BF16)
        k_scr[:, part] = jnp.broadcast_to(cell // columns, (8, capacity))
    total = sources * capacity
    step = min(total, 2048)
    row = iota((rows, step), 0)

    def plane(z, carry):
        sums = jnp.zeros((rows, 2 * columns), F32)
        for at in range(0, total, step):
            hit = row == k_scr[0:1, at : at + step] - z * rows
            onehot = jnp.where(hit, 1.0, 0.0).astype(BF16)
            sums = sums + mm_nt(onehot, r_scr[:, at : at + step])
        joule[z] = sums[:, :columns] + sums[:, columns:]
        return carry

    lax.fori_loop(0, planes, plane, 0)


def line_parts(position, theta, start, cells):
    growing, falling = jnp.exp(position * theta), jnp.exp(-position * theta)
    lower = growing + falling * jnp.exp(-(2.0 * start + 1.0) * theta)
    upper = falling + growing * jnp.exp(-(2.0 * (cells - start) - 1.0) * theta)
    return lower, upper


def line(conduct, cells):
    lead = HEAT_SPREADING * STIFF * conduct
    t = 0.5 / jnp.sqrt(lead)
    theta = 2.0 * jnp.log1p(t + t * t / (1.0 + jnp.sqrt(1.0 + t * t)))
    scale = 1.0 / (jnp.sqrt(4.0 * lead + 1.0) * (1.0 - jnp.exp(-2.0 * cells * theta)))
    return theta, scale


def prep_kernel(
    sizes, idx, scalars, gx_ref, gy_ref, co, z_scr,
):
    planes, rows, columns, nx, ny, nz = sizes
    lanes = 128
    extent = rows + EXTRA
    lx, ax, by, dx, dxl, dy, cg, phz, psz, mz, wz = groups_of(
        sizes, co, "lx", "ax", "by", "dx", "dxl", "dy", "cg", "phz", "psz", "mz", "wz"
    )
    gx, gy, gz = idx[0], idx[1], idx[2]
    x0, xn = (gx * rows).astype(F32), float(nx * rows)
    y0, yn = (gy * columns).astype(F32), float(ny * columns)

    def wide(array, width):
        return jnp.concatenate([array] * (width // lanes), axis=1)

    def rows_of(first):
        value = jnp.ones((planes, lanes), F32)
        for z in range(planes):
            one = scalars[first + z]
            value = jnp.where(iota((planes, lanes), 0) == z, one, value)
        return value

    lane_z = iota((8, lanes), 1) % planes
    lane_e = iota((8, lanes), 1) // planes
    by_lane = jnp.ones((8, lanes), F32)
    own = []
    for z in range(planes):
        value = scalars[gz * planes + z]
        own.append(value)
        by_lane = jnp.where(lane_z == z, value, by_lane)
    theta_lane, scale_lane = line(by_lane, yn)
    theta_rows, _ = line(rows_of(gz * planes), 1.0)
    for k in range(nx):
        dx[k] = jnp.exp(-float(k * rows) * theta_rows)
        dxl[k] = jnp.exp(-float(k * rows) * theta_lane)
    for k in range(ny):
        dy[k] = jnp.exp(-float(k * columns) * theta_rows)

    for part in range(nz):
        conduct = rows_of(part * planes)
        theta, scale = line(conduct, xn)
        low, high = line_parts(
            iota((planes, rows), 1).astype(F32), wide(theta, rows), x0, xn
        )
        both = jnp.concatenate([high * wide(scale, rows), low * wide(scale, rows)], axis=0)
        for half in range(rows // lanes):
            ax[part * (rows // lanes) + half] = both[:, half * lanes : (half + 1) * lanes]
        theta, scale = line(conduct, yn)
        low, high = line_parts(iota((planes, columns), 1).astype(F32), theta, y0, yn)
        by[part] = jnp.concatenate([high * scale, low * scale], axis=0)

    minus, plus = jnp.full((8, lanes), -1.0, F32), jnp.full((8, lanes), float(columns), F32)
    low_b, high_b = line_parts(minus, theta_lane, y0, yn)
    low_t, high_t = line_parts(plus, theta_lane, y0, yn)
    r, n = iota((lanes, lanes), 0), iota((lanes, lanes), 1)
    same = r % planes == n % planes
    kind = jnp.where(same, (r // planes) * 4 + n // planes, -1)
    cg[0] = jnp.where(
        kind == 8, (high_b * scale_lane)[0:1, :],
        jnp.where(
            kind == 9, (high_t * scale_lane)[0:1, :],
            jnp.where(
                kind == 12, (low_b * scale_lane)[0:1, :],
                jnp.where(kind == 13, (low_t * scale_lane)[0:1, :], 0.0),
            ),
        ),
    )

    order = iota((extent, lanes), 0)
    index = jnp.where(order == rows, -1, jnp.where(order == rows + 1, rows, order))
    position = index.astype(F32)
    real = order < rows + 2
    index_w, order_w = wide(index, rows), wide(order, rows)
    at_or_past = index_w >= iota((extent, rows), 1)
    lane = iota((extent, lanes), 1)
    packed = jnp.zeros((extent, lanes), F32)
    y_col = iota((columns, columns), 0).astype(F32)
    y_i, y_j = iota((columns, columns), 0), iota((columns, columns), 1)
    y_past = y_j >= y_i
    for z in range(planes):
        theta, k_x = line(jnp.full((8, lanes), own[z], F32), xn)
        theta1, k1 = theta[0:1, :], k_x[0:1, :]
        low_c, high_c = line_parts(position, theta1, x0, xn)
        low_c = jnp.where(real, low_c * k1, 0.0)
        high_c = jnp.where(real, high_c * k1, 0.0)
        packed = jnp.where(lane == z, high_c, jnp.where(lane == planes + z, low_c, packed))
        low_r, high_r = line_parts(
            iota((8, rows), 1).astype(F32), wide(theta, rows), x0, xn
        )
        low_r, high_r = low_r[0:1, :], high_r[0:1, :]
        g = jnp.where(at_or_past, wide(high_c, rows) * low_r, wide(low_c, rows) * high_r)
        g = jnp.where(order_w == rows + 2, low_r, jnp.where(order_w == rows + 3, high_r, g))
        gx_ref[z, :extent, :], gx_ref[z, extent:, :] = split(g)

        theta, k_y = line(jnp.full((8, lanes), own[z], F32), yn)
        theta1, k1 = theta[0:1, :], k_y[0:1, :]
        low_r, high_r = line_parts(iota((8, columns), 1).astype(F32), theta, y0, yn)
        low_r, high_r = low_r[0:1, :], high_r[0:1, :]
        low_c, high_c = line_parts(y_col, theta1, y0, yn)
        low_b, _ = line_parts(minus[0:1, :], theta1, y0, yn)
        _, high_t = line_parts(plus[0:1, :], theta1, y0, yn)
        g = k1 * jnp.where(y_past, high_r * low_c, low_r * high_c)
        ext = jnp.zeros((columns, lanes), F32)
        for e, values in enumerate((low_b * high_c * k1, high_t * low_c * k1, low_c, high_c)):
            ext = jnp.where(y_j == e * planes + z, values, ext)
        gy_ref[z, :, :lanes], gy_ref[planes + z, :, :lanes] = split(g)
        gy_ref[z, :, lanes:], gy_ref[planes + z, :, lanes:] = split(ext)
    lx[0] = packed

    total = planes * nz
    cond = [jnp.full((8, lanes), scalars[z], F32) for z in range(total)]
    lead = [HEAT_SPREADING * STIFF * 0.5 * (cond[z] + cond[z + 1]) for z in range(total - 1)]
    lower = [jnp.ones((8, lanes), F32)]
    flux = HEAT_SPREADING * STIFF * cond[0]
    resist = [1.0 / value for value in lead]
    for z in range(total - 1):
        flux = flux + lower[z]
        lower.append(lower[z] + flux * resist[z])
    weight = 1.0 / (flux + lower[total - 1])
    upper = [None] * total
    upper[total - 1] = weight
    flux = jnp.zeros((8, lanes), F32)
    for z in range(total - 2, -1, -1):
        flux = flux + upper[z + 1]
        upper[z] = upper[z + 1] + flux * resist[z]
    zero = jnp.zeros((8, lanes), F32)
    z_scr[0], z_scr[total + 3] = zero, zero
    z_scr[total + 1], z_scr[total + 2] = zero, zero
    for z in range(total):
        z_scr[1 + z] = lower[z]
        z_scr[total + 3 + z] = upper[z]
    z_scr[2 * total + 3] = zero
    mine = gz * planes
    for z in range(planes + 2):
        phz[z] = z_scr[mine + z]
        psz[z] = jnp.where(mine + z == 0, zero, z_scr[total + 2 + mine + z])

    low_lane, high_lane = zero, zero
    for z in range(planes):
        low_lane = jnp.where(lane_z == z, phz[z + 1], low_lane)
        high_lane = jnp.where(lane_z == z, psz[z + 1], high_lane)
    row_p, lane_p = iota((planes, lanes), 0), iota((planes, lanes), 1)
    low_rows, high_rows = jnp.zeros((planes, lanes), F32), jnp.zeros((planes, lanes), F32)
    for z in range(planes):
        low_rows = jnp.where(row_p == z, phz[z + 1][0:1, :], low_rows)
        high_rows = jnp.where(row_p == z, psz[z + 1][0:1, :], high_rows)
    blocks, ends = [], []
    for e in range(2):
        g = jnp.where(
            lane_p % planes >= row_p,
            low_rows * high_lane[0:1, :],
            high_rows * low_lane[0:1, :],
        )
        blocks.append(jnp.where(lane_p // planes == e, g, 0.0))
        ends.append(
            jnp.where(lane_p == e, low_rows, jnp.where(lane_p == 2 + e, high_rows, 0.0))
        )
    rest = jnp.zeros((lanes - 2 * planes, lanes), F32)
    mz[0] = jnp.concatenate(blocks + [rest], axis=0)
    mz[1] = jnp.concatenate(ends + [rest], axis=0)
    row8 = iota((8, lanes), 0)
    wz[0] = jnp.where(
        (row8 < 2) & (lane_e == row8),
        high_lane,
        jnp.where((row8 >= 2) & (row8 < 4) & (lane_e == row8 - 2), low_lane, 0.0),
    )


def slope_kernel(
    counts, n_planes, idx, scalars, u_ref, kind_ref, xr0, xr1, yr0, yr1, zr0, zr1,
    d_ref, ux, uy, uz, kx0, kx1, ky0, ky1, kz,
):
    planes, rows, columns = u_ref.shape
    even = [idx[d] % 2 == 0 for d in range(3)]
    at_low = [idx[d] == 0 for d in range(3)]
    at_high = [idx[d] == counts[d] - 1 for d in range(3)]
    row, lane = iota((rows, columns), 0), iota((rows, columns), 1)

    def ends(first, second, d):
        return jnp.where(even[d], second, first), jnp.where(even[d], first, second)

    low, high = ends(xr0[0], xr1[0], 0)
    ux[...] = jnp.zeros(ux.shape, F32)
    for z in range(planes):
        ux[z, 0:1, :] = low[z : z + 1, :]
        ux[z, 1:2, :] = high[z : z + 1, :]
    x_low, x_high = ends(xr0[1], xr1[1], 0)
    low, high = ends(yr0[...], yr1[...], 1)
    kind = iota((rows, 128), 1) // planes
    uy[...] = jnp.zeros(uy.shape, F32)
    uy[:rows, :] = jnp.where(
        kind == 0, low, jnp.where(kind == 1, pltpu.roll(high, planes, 1), 0.0)
    )
    low, high = ends(zr0[0], zr1[0], 2)
    uz[0] = jnp.where(at_low[2], 0.0, low)
    uz[1] = high
    z_low, z_high = ends(zr0[1], zr1[1], 2)
    half = 0.5 * HEAT_SPREADING
    y_low, y_high = ends(yr0[...], yr1[...], 1)
    c_before = None
    for z in range(planes):
        c = conductance(z, idx, scalars, kind_ref, n_planes)
        first = jnp.where(at_low[0], -c[0:1, :], x_low[z : z + 1, :])
        final = jnp.where(at_high[0], -c[rows - 1 :, :], x_high[z : z + 1, :])
        kx0[z] = half * (c + jnp.where(row == 0, first, pltpu.roll(c, 1, 0)))
        kx1[z] = half * (c + jnp.where(row == rows - 1, final, pltpu.roll(c, rows - 1, 0)))
        first = jnp.where(at_low[1], -c, pltpu.roll(y_low, columns - planes - z, 1))
        final = jnp.where(at_high[1], -c, pltpu.roll(y_high, columns - 1 - planes - z, 1))
        ky0[z] = half * (c + jnp.where(lane == 0, first, pltpu.roll(c, 1, 1)))
        ky1[z] = half * (c + jnp.where(lane == columns - 1, final, pltpu.roll(c, columns - 1, 1)))
        if z == 0:
            kz[z] = half * (c + jnp.where(at_low[2], c, z_low))
        else:
            kz[z] = half * (c + c_before)
        c_before = c
        if z == planes - 1:
            kz[planes] = half * jnp.where(at_high[2], 0.0, c + z_high)
    for z in range(planes):
        d_ref[z] = outflow(z, u_ref, ux, uy, uz, kx0, kx1, ky0, ky1, kz)


def outflow(z, u_ref, ux, uy, uz, kx0, kx1, ky0, ky1, kz):
    planes, rows, columns = u_ref.shape
    u = u_ref[z]
    row, lane = iota((rows, columns), 0), iota((rows, columns), 1)
    edge = uy[:rows, :]
    edge_low = pltpu.roll(edge, columns - z, 1) if z else edge
    edge_high = pltpu.roll(edge, columns - 1 - planes - z, 1)
    below = uz[0] if z == 0 else u_ref[z - 1]
    above = uz[1] if z == planes - 1 else u_ref[z + 1]
    total = kx0[z] * (jnp.where(row == 0, ux[z, 0:1, :], pltpu.roll(u, 1, 0)) - u)
    total += kx1[z] * (
        jnp.where(row == rows - 1, ux[z, 1:2, :], pltpu.roll(u, rows - 1, 0)) - u
    )
    total += ky0[z] * (jnp.where(lane == 0, edge_low, pltpu.roll(u, 1, 1)) - u)
    total += ky1[z] * (
        jnp.where(lane == columns - 1, edge_high, pltpu.roll(u, columns - 1, 1)) - u
    )
    return total + kz[z] * (below - u) + kz[z + 1] * (above - u)


def advance(idx, source_of, gx_ref, gy_ref, phz, psz, t_ref, e_ref, x_sends, z_sends):
    planes, extent, columns = t_ref.shape
    rows = extent - EXTRA
    sums = jnp.zeros((extent, 128), F32)
    below, above = jnp.zeros((rows, columns), F32), jnp.zeros((rows, columns), F32)
    for z in range(planes):
        high, low = split(source_of(z))
        out = mm(gx_ref[z], jnp.concatenate([high, low], axis=1))
        t = out[:extent, :columns] + (out[:extent, columns:] + out[extent:, :columns])
        high, low = split(t)
        out = mm(jnp.concatenate([high, low], axis=0), gy_ref[z])
        out = out[:extent] + (out[extent:] + mm(high, gy_ref[planes + z]))
        t_ref[z] = out[:, :columns]
        sums += out[:, columns:]
        main = out[:rows, :columns]
        below += phz[z + 1][0:1, :] * main
        above += psz[z + 1][0:1, :] * main
    e_ref[...] = sums
    for b, send in enumerate(x_sends):
        take = jnp.where((idx[0] >> b) % 2 == 0, 0, 1)
        for z in range(planes):
            pair = t_ref[z, rows + 2 : rows + 4, :]
            send[z : z + 1, :] = jnp.where(take == 0, pair[0:1], pair[1:2])
        pair = sums[rows + 2 : rows + 4, :]
        send[planes:, :] = jnp.broadcast_to(
            jnp.where(take == 0, pair[0:1], pair[1:2]), (8, 128)
        )
    for b, send in enumerate(z_sends):
        send[...] = jnp.where((idx[2] >> b) % 2 == 0, below, above)


def start_kernel(sizes, n_sends, idx, got, d_ref, u_ref, gx_ref, gy_ref, co,
                 joule, t_ref, e_ref, *rest):
    phz, psz = groups_of(sizes, co, "phz", "psz")
    sends, (r_scr, k_scr) = rest[:-2], rest[-2:]
    joule_into(got, joule, r_scr, k_scr)

    def source_of(z):
        return d_ref[z] + OHMIC_POWER * ((1.0 + WARMING_SLOPE * u_ref[z]) * joule[z])

    advance(
        idx, source_of, gx_ref, gy_ref, phz, psz, t_ref, e_ref,
        sends[: n_sends], sends[n_sends:],
    )


def x_kernel(sizes, idx, e_ref, co, *rest):
    gots, (e_out, f_out, send) = rest[:-3], rest[-3:]
    planes, nx = sizes[0], sizes[3]
    dx, dxl, lx = groups_of(sizes, co, "dx", "dxl", "lx")
    me = idx[0]
    sums = [[jnp.zeros((planes, 128), F32), jnp.zeros((8, 128), F32)] for _ in range(2)]
    for k, got in zip(range(1, nx), gots):
        other = partner(me, k, nx)
        far = jnp.abs(me - other)
        pair = got[:planes, :] * dx[far], got[planes:, :] * dxl[far]
        for side, keep in ((0, other < me), (1, other > me)):
            for part in range(2):
                sums[side][part] += jnp.where(keep, pair[part], 0.0)
    f_out[:planes, :], f_out[planes:, :] = sums[0][0], sums[1][0]
    row, lane = iota((planes, 128), 0), iota((planes, 128), 1)
    own = lane % planes == row
    ext = jnp.concatenate(
        [jnp.where(own, sums[0][1][0:1, :], 0.0), jnp.where(own, sums[1][1][0:1, :], 0.0)],
        axis=0,
    )
    e = e_ref[...] + exact(lx[0][:, : 2 * planes], ext)
    e_out[...] = e
    send[...] = e.T[2 * planes : 4 * planes]


def four(rows):
    return jnp.concatenate([rows] * 4, axis=0)


def weights(ref, planes):
    row = iota((planes, 128), 0)
    values = jnp.zeros((planes, 128), F32)
    for z in range(planes):
        values = jnp.where(row == z, ref[z + 1][0:1, :], values)
    return values


def y_kernel(sizes, idx, t_ref, e_ref, f_ref, co, *rest):
    ny = sizes[4]
    dy, lx, by, cg, phz, psz, mz = groups_of(
        sizes, co, "dy", "lx", "by", "cg", "phz", "psz", "mz"
    )
    gots, rest = rest[: ny - 1], rest[ny - 1 :]
    q_ref, l_ref, b_ref = rest[:3]
    sends = rest[3:]
    planes, extent, columns = t_ref.shape
    rows = extent - EXTRA
    me = idx[1]
    row = iota((2 * planes, extent), 0)
    across = jnp.zeros((2 * planes, extent), F32)
    for k, got in zip(range(1, ny), gots):
        other = partner(me, k, ny)
        far = jnp.concatenate([dy[jnp.abs(me - other)][:, 0:1]] * 2, axis=0)
        keep = (row < planes) == (other < me)
        across += jnp.where(keep, got[...] * far, 0.0)
    others = jnp.concatenate(
        [
            jnp.zeros((2 * planes, extent), F32),
            across,
            jnp.zeros((128 - 4 * planes, extent), F32),
        ],
        axis=0,
    ).T
    lane = iota((extent, 128), 1)
    q = jnp.where(lane < 2 * planes, e_ref[...], 0.0) + exact(others, cg[0])
    q_ref[...] = q
    left = lx[0] + others
    l_ref[...] = left
    right = jnp.concatenate([f_ref[...], by[idx[2]]], axis=0)
    b_ref[...] = right
    edge = exact(q[:rows], mz[1]).T
    ghost = slice(rows, rows + 8)
    low, high = weights(phz, planes), weights(psz, planes)
    both = jnp.concatenate([right * four(low), right * four(high)], axis=1)
    ghosts = exact(left[ghost, : 4 * planes], both)
    g_low, g_high = ghosts[:, :128], ghosts[:, 128:]
    for z in range(planes):
        value = t_ref[z, ghost, :]
        g_low += phz[z + 1][0:1, :] * value
        g_high += psz[z + 1][0:1, :] * value
    for b, send in enumerate(sends):
        lower = (idx[2] >> b) % 2 == 0
        scale = jnp.where(lower, low, high)
        twice = jnp.concatenate([scale] * 2, axis=0)
        send[:8, :] = jnp.where(lower, g_low, g_high)
        send[8 : 8 + 2 * planes, :] = f_ref[...] * twice
        at = 8 + 2 * planes
        for part in range(rows // 128):
            cols = slice(part * 128, (part + 1) * 128)
            send[at : at + 8, :] = edge[0:8, cols]
            send[at + 8 : at + 8 + 2 * planes, :] = across[:, cols] * twice
            at += 8 + 2 * planes


def carried(nz, idx, bigs, smalls, ax, by, rows, ghosts):
    me = idx[2]
    planes = by.each // 2
    below = above = None
    g_below = g_above = edges = 0.0
    lefts, rights = [], []
    sub = iota((8, rows), 0)
    for k, big, small in zip(range(1, nz), bigs, smalls):
        other = partner(me, k, nz)
        lower = other < me

        def add(total, value, keep):
            value = jnp.where(keep, value, 0.0)
            return value if total is None else total + value

        below = add(below, big[...], lower)
        above = add(above, big[...], jnp.logical_not(lower))
        at, stride = 8 + 2 * planes, 8 + 2 * planes
        parts = [at + p * stride for p in range(rows // 128)]
        across = jnp.concatenate([small[p + 8 : p + stride, :] for p in parts], axis=1)
        halves = rows // 128
        near = [ax[other * halves + half] for half in range(halves)]
        lefts += [jnp.concatenate(near, axis=1), across]
        right = jnp.concatenate([small[8:at, :], by[other]], axis=0)
        rights.append(
            jnp.concatenate(
                [jnp.where(lower, right, 0.0), jnp.where(lower, 0.0, right)], axis=1
            )
        )
        if ghosts:
            g_below += jnp.where(lower, small[:8, :], 0.0)
            g_above += jnp.where(lower, 0.0, small[:8, :])
            value = jnp.concatenate([small[p : p + 8, :] for p in parts], axis=1)
            edges += jnp.where(sub // 2 == jnp.where(lower, 0, 1), value, 0.0)
    more = exact(
        jnp.concatenate(lefts, axis=0), jnp.concatenate(rights, axis=0), ((0,), (0,))
    )
    below, above = below + more[:, :128], above + more[:, 128:]
    return below, above, g_below, g_above, edges


def whole_planes(t_ref, l_ref, b_ref, second, extent):
    planes = t_ref.shape[0]
    high, low = split(l_ref[:extent, : 4 * planes])
    pair = jnp.concatenate([high, low], axis=0)
    right = b_ref[...]
    row = iota(right.shape, 0) % planes
    for z in range(planes):
        r_high, r_low = split(jnp.where(row == z, right, 0.0))
        out = mm(pair, r_high)
        second[z] = t_ref[z, :extent, :] + (out[:extent] + (out[extent:] + mm(high, r_low)))


def change(outside, second, phz, psz, below, above, emit):
    planes = second.shape[0]
    tails = [above]
    for z in range(planes - 1, -1, -1):
        tails.append(tails[-1] + psz[z + 1][0:1, :] * second[z])
    tails = tails[::-1]
    if outside:
        emit(-1, psz[0][0:1, :] * below + phz[0][0:1, :] * tails[0])
    head = below
    for z in range(planes):
        head = head + phz[z + 1][0:1, :] * second[z]
        emit(z, psz[z + 1][0:1, :] * head + phz[z + 1][0:1, :] * tails[z + 1])
    if outside:
        emit(planes, psz[planes + 1][0:1, :] * head + phz[planes + 1][0:1, :] * above)


def rise_kernel(sizes, n_sends, idx, t_in, l_ref, b_ref, q_ref, co,
                u_ref, ux, uy, uz, kx0, kx1, ky0, ky1, kz, joule, gx_ref, gy_ref, *rest):
    nz = sizes[5]
    phz, psz, mz, wz, ax, by = groups_of(sizes, co, "phz", "psz", "mz", "wz", "ax", "by")
    bigs, smalls, rest = rest[: nz - 1], rest[nz - 1 : 2 * nz - 2], rest[2 * nz - 2 :]
    u_out, ux_out, uy_out, uz_out, t_ref, e_ref = rest[:6]
    sends, second = rest[6:-1], rest[-1]
    planes, rows, columns = u_ref.shape
    whole_planes(t_in, l_ref, b_ref, second, rows + 8)
    below, above, g_below, g_above, edges = carried(nz, idx, bigs, smalls, ax, by, rows, True)

    def emit(z, value):
        if z == -1:
            uz_out[0] = uz[0] + value[:rows]
        elif z == planes:
            uz_out[1] = uz[1] + value[:rows]
        else:
            u_out[z] = u_ref[z] + value[:rows]
            ux_out[z] = ux[z] + value[rows:]

    change(
        True, second, phz, psz,
        jnp.concatenate([below, g_below], axis=0),
        jnp.concatenate([above, g_above], axis=0),
        emit,
    )
    grown = exact(q_ref[:rows, :], mz[0]) + exact(edges, wz[0], ((0,), (0,)))
    uy_out[...] = uy[...]
    uy_out[:rows, :] = uy[:rows, :] + grown

    def source_of(z):
        out = outflow(z, u_out, ux_out, uy_out, uz_out, kx0, kx1, ky0, ky1, kz)
        return out + OHMIC_POWER * ((1.0 + WARMING_SLOPE * u_out[z]) * joule[z])

    advance(
        idx, source_of, gx_ref, gy_ref, phz, psz, t_ref, e_ref,
        sends[:n_sends], sends[n_sends:],
    )


def finish_kernel(sizes, idx, t_in, l_ref, b_ref, co, u_ref, joule, *rest):
    nz = sizes[5]
    phz, psz, ax, by = groups_of(sizes, co, "phz", "psz", "ax", "by")
    bigs, smalls, rest = rest[: nz - 1], rest[nz - 1 : 2 * nz - 2], rest[2 * nz - 2 :]
    u_out, heat_out, second = rest
    rows = u_ref.shape[1]
    whole_planes(t_in, l_ref, b_ref, second, rows)
    below, above, _, _, _ = carried(nz, idx, bigs, smalls, ax, by, rows, False)

    def emit(z, value):
        u = u_ref[z] + value
        u_out[z] = u
        heat_out[z] = (1.0 + WARMING_SLOPE * u) * joule[z]

    change(False, second, phz, psz, below, above, emit)


def per_device(
    starting_warmth,
    sheet_stratum_number,
    stratum_heat_conduction,
    substance_kind,
    substance_kind_scaling,
    wire_piece_amperes,
    wire_piece_ohms_base,
    wire_piece_tile,
    wire_piece_voxel,
):
    planes, rows, columns = starting_warmth.shape
    counts = tuple(lax.axis_size(axis) for axis in ("gx", "gy", "gz"))
    nx, ny, nz = counts
    bits = [(n - 1).bit_length() for n in counts]
    devices = nx * ny * nz
    extent = rows + EXTRA
    idx = jnp.stack([lax.axis_index(axis) for axis in ("gx", "gy", "gz")]).astype(jnp.int32)
    block = shaped(planes, rows, columns)
    n_planes = sheet_stratum_number.shape[0]
    layers = jnp.arange(stratum_heat_conduction.shape[0], dtype=jnp.int32)
    matches = sheet_stratum_number[:, None] == layers[None, :]
    scalars = jnp.concatenate(
        [
            jnp.sum(jnp.where(matches, stratum_heat_conduction[None, :], 0.0), axis=1),
            substance_kind_scaling,
        ]
    )

    count = wire_piece_amperes.shape[0]
    capacity = 2 * count // devices
    lanes = 128
    chunks = count // lanes
    segments = jnp.stack(
        [
            wire_piece_amperes * wire_piece_amperes * wire_piece_ohms_base,
            wire_piece_tile[:, 0].astype(F32),
            wire_piece_voxel.astype(F32),
        ]
    ).reshape(3, chunks, lanes)
    (send,) = call(
        functools.partial(dispatch_kernel, devices, capacity),
        [shaped(devices, 2 * capacity)],
        (segments,),
        scratch=[
            pltpu.VMEM((6 * devices, count), BF16),
            pltpu.VMEM((capacity, count), BF16),
            pltpu.VMEM((chunks * devices, lanes), BF16),
        ],
    )
    warmth, kinds, send = lax.optimization_barrier((starting_warmth, substance_kind, send))
    got = lax.all_to_all(send, ("gx", "gy", "gz"), split_axis=0, concat_axis=0, tiled=True)

    xs0, xs1, ys0, ys1, zs0, zs1 = call(
        functools.partial(faces_kernel, n_planes),
        [shaped(2, planes, columns)] * 2
        + [shaped(rows, 128)] * 2
        + [shaped(2, rows, columns)] * 2,
        (idx, scalars, warmth, kinds),
        smem=2,
    )
    zr = next_pairs(zs0, zs1, "gz")
    xr = next_pairs(xs0, xs1, "gx")
    yr = next_pairs(ys0, ys1, "gy")
    sizes = (planes, rows, columns, nx, ny, nz)
    gx_m, gy_m, co = call(
        functools.partial(prep_kernel, sizes),
        [
            shaped(planes, 2 * extent, rows, dtype=BF16),
            shaped(2 * planes, columns, 256, dtype=BF16),
            shaped(table_rows(*sizes)[1], lanes),
        ],
        (idx, scalars),
        smem=2,
        scratch=[pltpu.VMEM((2 * planes * nz + 4, 8, lanes), F32)],
    )
    d0, ux, uy, uz, *conduct = call(
        functools.partial(slope_kernel, counts, n_planes),
        [block, shaped(planes, 8, columns), shaped(extent, 128), shaped(2, rows, columns)]
        + [block] * 4
        + [shaped(planes + 1, rows, columns)],
        (idx, scalars, warmth, kinds, *xr, *yr, *zr),
        smem=2,
    )
    step_out = [shaped(planes, extent, columns), shaped(extent, 128)]
    step_out += [shaped(planes + 8, columns)] * bits[0] + [shaped(rows, columns)] * bits[2]
    total = devices * capacity
    joule, t, e, *sends = call(
        functools.partial(start_kernel, sizes, bits[0]),
        [block] + step_out,
        (idx, got, d0, warmth, gx_m, gy_m, co),
        smem=1,
        scratch=[
            pltpu.VMEM((2 * columns, total), BF16),
            pltpu.VMEM((8, total), jnp.int32),
        ],
    )
    u = warmth
    small = shaped(8 + 2 * planes + (8 + 2 * planes) * (rows // 128), 128)
    for repeat in range(STEPS):
        gots = all_pairs(sends[: bits[0]], "gx")
        bigs = all_pairs(sends[bits[0] :], "gz")
        e, f, send = call(
            functools.partial(x_kernel, sizes),
            [shaped(extent, 128), shaped(2 * planes, columns), shaped(2 * planes, extent)],
            (idx, e, co, *gots),
            smem=1,
        )
        gots = all_pairs([send] * bits[1], "gy")
        q, left, right, *sends = call(
            functools.partial(y_kernel, sizes),
            [shaped(extent, 128)] * 2 + [shaped(4 * planes, columns)] + [small] * bits[2],
            (idx, t, e, f, co, *gots),
            smem=1,
        )
        smalls = all_pairs(sends, "gz")
        if repeat < STEPS - 1:
            u, ux, uy, uz, t, e, *sends = call(
                functools.partial(rise_kernel, sizes, bits[0]),
                [block, shaped(planes, 8, columns), shaped(extent, 128)]
                + [shaped(2, rows, columns)]
                + step_out,
                (idx, t, left, right, q, co, u, ux, uy, uz, *conduct)
                + (joule, gx_m, gy_m, *bigs, *smalls),
                smem=1,
                scratch=[pltpu.VMEM((planes, rows + 8, columns), F32)],
            )
    return tuple(
        call(
            functools.partial(finish_kernel, sizes),
            [block, block],
            (idx, t, left, right, co, u, joule, *bigs, *smalls),
            smem=1,
            scratch=[pltpu.VMEM((planes, rows, columns), F32)],
        )
    )


def solution(mesh):
    return jax.shard_map(
        per_device,
        mesh=mesh,
        in_specs=(
            P("gz", "gx", "gy"),
            P(),
            P(),
            P("gz", "gx", "gy"),
            P(),
            P(("gx", "gy", "gz")),
            P(("gx", "gy", "gz")),
            P(("gx", "gy", "gz"), None),
            P(("gx", "gy", "gz")),
        ),
        out_specs=(P("gz", "gx", "gy"), P("gz", "gx", "gy")),
        check_vma=False,
    )
```

```python
import functools

import jax
import jax.numpy as jnp
from jax import lax
from jax.experimental import pallas as pl
from jax.experimental.pallas import tpu as pltpu
from jax.sharding import PartitionSpec as P

STEPS = 2
HEAT_SPREADING = 1000.0
STIFF = 1.5
WARMING_SLOPE = 0.1
OHMIC_POWER = 8.0

F32 = jnp.float32
BF16 = jnp.bfloat16
EXTRA = 16
EXACT = lax.Precision.HIGHEST


def call(kernel, out_shapes, args, smem=0, scratch=(), vmem=24, far=0, far_out=False):
    specs = [pl.BlockSpec(memory_space=pltpu.SMEM)] * smem
    specs += [pl.BlockSpec(memory_space=pltpu.VMEM)] * (len(args) - smem - far)
    specs += [pl.BlockSpec(memory_space=pl.ANY)] * far
    return pl.pallas_call(
        kernel,
        out_shape=out_shapes,
        in_specs=specs,
        out_specs=[pl.BlockSpec(memory_space=pl.ANY if far_out else pltpu.VMEM)]
        * len(out_shapes),
        scratch_shapes=list(scratch),
        compiler_params=pltpu.CompilerParams(vmem_limit_bytes=vmem * 2**20),
        cost_estimate=pl.CostEstimate(flops=0, bytes_accessed=1, transcendentals=0),
    )(*args)


def shaped(*shape, dtype=F32):
    return jax.ShapeDtypeStruct(shape, dtype)


def split(x):
    high = x.astype(BF16)
    return high, (x - high.astype(F32)).astype(BF16)


def iota(shape, dim):
    return lax.broadcasted_iota(jnp.int32, shape, dim)


def copies(pairs, sems):
    return [
        pltpu.make_async_copy(src, dst, sems.at[k]) for k, (src, dst) in enumerate(pairs)
    ]


def plane_copies(pairs, sems):
    started = [
        [
            pltpu.make_async_copy(src.at[z], dst.at[z], sems.at[k, z])
            for z in range(dst.shape[0])
        ]
        for k, (src, dst) in enumerate(pairs)
    ]
    for copies_of_plane in zip(*started):
        for copy in copies_of_plane:
            copy.start()
    return started


def mm(a, b):
    return jnp.dot(a, b, preferred_element_type=F32)


def exact(a, b, dims=((1,), (0,))):
    return lax.dot_general(a, b, (dims, ((), ())), precision=EXACT, preferred_element_type=F32)


def mm_nt(a, b):
    return lax.dot_general(a, b, (((1,), (1,)), ((), ())), preferred_element_type=F32)


def table_rows(planes, rows, columns, nx, ny, nz):
    at, places = 0, {}
    for name, items, each in (
        ("lx", 1, rows + EXTRA),
        ("ax", nz * (rows // 128), 2 * planes),
        ("by", nz, 2 * planes),
        ("dx", nx, planes),
        ("dxl", nx, 8),
        ("dy", ny, planes),
        ("cg", 1, 128),
        ("phz", planes + 2, 8),
        ("psz", planes + 2, 8),
        ("mz", 2, 128),
        ("wz", 1, 8),
    ):
        places[name] = (at, each)
        at += items * each
    return places, at


class Group:
    def __init__(self, ref, place):
        self.ref, (self.at, self.each) = ref, place

    def rows(self, k):
        at = self.at + k * self.each
        return pl.ds(at if isinstance(at, int) else pl.multiple_of(at, 8), self.each)

    def __getitem__(self, k):
        return self.ref[self.rows(k), :]

    def __setitem__(self, k, value):
        self.ref[self.rows(k), :] = value


def groups_of(sizes, ref, *names):
    places, _ = table_rows(*sizes)
    return [Group(ref, places[name]) for name in names]


def partner(me, k, n):
    return me ^ k


def groups(n):
    return [k.bit_length() - 1 for k in range(1, n)]


def all_pairs(arrays, axis):
    n = lax.axis_size(axis)
    return [
        lax.ppermute(arrays[b], axis, [(i, i ^ k) for i in range(n)])
        for k, b in zip(range(1, n), groups(n))
    ]


def crossed(array, k, axis):
    return lax.ppermute(array, axis, [(i, i ^ k) for i in range(lax.axis_size(axis))])


def next_pairs(even, odd, axis):
    n = lax.axis_size(axis)
    first = lax.ppermute(even, axis, [(i, i ^ 1) for i in range(n)])
    if n == 2:
        return first, first
    pairs = [(i, i + 1) for i in range(1, n - 1, 2)]
    return first, lax.ppermute(odd, axis, pairs + [(b, a) for a, b in pairs])


def conductance(z, idx, sheet, table, scaling, kind_ref):
    factor = jnp.zeros(kind_ref.shape[1:], F32)
    for category in range(scaling.shape[0]):
        factor = jnp.where(kind_ref[z] == category, scaling[category], factor)
    return table[sheet[idx[2] * kind_ref.shape[0] + z]] * factor


def faces_kernel(
    idx, sheet, table, scaling, u_in, kind_in, xs0, xs1, ys0, ys1, zs0, zs1, u_ref, kind_ref, sems
):
    planes, rows, columns = u_ref.shape
    started = plane_copies([(u_in, u_ref), (kind_in, kind_ref)], sems)
    even = [idx[d] % 2 == 0 for d in range(3)]
    lane = iota((rows, columns), 1)
    low = jnp.zeros((rows, columns), F32)
    high = jnp.zeros((rows, columns), F32)
    for z in range(planes):
        started[0][z].wait()
        started[1][z].wait()
        u, c = u_ref[z], conductance(z, idx, sheet, table, scaling, kind_ref)
        if z == 0:
            zs0[1], zs1[1] = c, c
        elif z == planes - 1:
            zs0[1] = jnp.where(even[2], c, zs0[1])
            zs1[1] = jnp.where(even[2], zs1[1], c)
        for slot, values in ((0, u), (1, c)):
            at = slot * planes + z
            low = jnp.where(lane == at, pltpu.roll(values, at, 1) if at else values, low)
            high = jnp.where(lane == at, pltpu.roll(values, at + 1, 1), high)
            first, last = values[0:1, :], values[rows - 1 : rows, :]
            xs0[slot, z : z + 1, :] = jnp.where(even[0], last, first)
            xs1[slot, z : z + 1, :] = jnp.where(even[0], first, last)
    ys0[...] = jnp.where(even[1], high, low)
    ys1[...] = jnp.where(even[1], low, high)
    zs0[0] = jnp.where(even[2], u_ref[planes - 1], u_ref[0])
    zs1[0] = jnp.where(even[2], u_ref[0], u_ref[planes - 1])


def shares(capacity):
    return capacity // 4, capacity - capacity // 4


def dispatch_kernel(blocks, planes, area, capacity, amps_in, ohms_in, tile_in, cell_in,
                    send, amps, ohms, tiles, cells, a_scr, b_scr, z_scr, k_scr, sems):
    started = copies(
        [(amps_in, amps), (ohms_in, ohms), (tile_in, tiles), (cell_in, cells)], sems
    )
    for copy in started:
        copy.start()
    for copy in started:
        copy.wait()
    chunks, lanes = amps.shape
    share, spare = shares(capacity)
    keys, main = blocks * planes, planes * share
    power = amps[...] * amps[...] * ohms[...]
    tile, cell = tiles[...], cells[...]
    plane, within = cell // area, cell % area
    key = tile * planes + plane
    p_high, p_low = split(power)
    pieces = [
        p_high.astype(F32),
        p_low.astype(F32),
        (within >> 8).astype(F32),
        (within & 255).astype(F32),
        plane.astype(F32),
    ]
    key_row, block_row = iota((keys, lanes), 0), iota((blocks, lanes), 0)
    place = iota((main, lanes), 0)
    ahead = jnp.where(iota((lanes, lanes), 0) < iota((lanes, lanes), 1), 1.0, 0.0)
    both = jnp.concatenate([ahead, jnp.ones((lanes, lanes), F32)], axis=1).astype(BF16)
    base = jnp.zeros((keys, lanes), F32)
    for c in range(chunks):
        row, cols = slice(c, c + 1), slice(c * lanes, (c + 1) * lanes)
        hit = key_row == key[row, :]
        counted = mm(jnp.where(hit, 1.0, 0.0).astype(BF16), both)
        rank = jnp.sum(jnp.where(hit, counted[:, :lanes] + base, 0.0), axis=0, keepdims=True)
        base = base + counted[:, lanes:]
        rank = rank.astype(jnp.int32)
        k_scr[row, :] = rank
        slot = jnp.where(rank < share, plane[row, :] * share + rank, -1)
        b_scr[:main, cols] = jnp.where(place == slot, 1.0, 0.0).astype(BF16)
        hit = block_row == tile[row, :]
        for k, piece in enumerate(pieces):
            a_scr[k * blocks : (k + 1) * blocks, cols] = jnp.where(
                hit, piece[row, :], 0.0
            ).astype(BF16)
    out = mm_nt(a_scr[: 4 * blocks, :], b_scr[:main, :])
    r = [out[k * blocks : (k + 1) * blocks] for k in range(4)]
    total = main + spare
    send[:, 0, :main] = r[0] + r[1]
    send[:, 0, total : total + main] = r[2] * 256.0 + r[3]
    send[:, 0, main:total] = jnp.zeros((blocks, spare), F32)
    send[:, 0, total + main :] = jnp.zeros((blocks, spare), F32)
    z_scr[...] = jnp.maximum(base - float(share), 0.0)

    @pl.when(jnp.max(z_scr[...]) > 0.0)
    def _():
        step = min(keys, 256)
        r, n = iota((step, step), 0), iota((step, step), 1)
        earlier = jnp.where((r // planes == n // planes) & (n < r), 1.0, 0.0).astype(BF16)
        for at in range(0, keys, step):
            part = slice(at, at + step)
            z_scr[part, :] = mm(earlier, z_scr[part, :].astype(BF16))
        place = iota((spare, lanes), 0)
        for c in range(chunks):
            row, cols = slice(c, c + 1), slice(c * lanes, (c + 1) * lanes)
            hit = key_row == key[row, :]
            first = jnp.sum(jnp.where(hit, z_scr[...], 0.0), axis=0, keepdims=True)
            rank = k_scr[row, :]
            slot = jnp.where(rank < share, -1, rank - share + first.astype(jnp.int32))
            b_scr[:spare, cols] = jnp.where(place == slot, 1.0, 0.0).astype(BF16)
        out = mm_nt(a_scr[...], b_scr[:spare, :])
        r = [out[k * blocks : (k + 1) * blocks] for k in range(5)]
        send[:, 0, main:total] = r[0] + r[1]
        send[:, 0, total + main :] = r[2] * 256.0 + r[3] + r[4] * float(area)


def joule_into(got, joule, r_scr, k_scr):
    planes, rows, columns = joule.shape
    sources, total = got.shape[0], got.shape[1] // 2
    spare = r_scr.shape[1] // sources
    main = total - spare
    share = main // planes
    lanes = 128
    per = lanes // share
    each = sources // per
    lane = iota((each, lanes), 1) // share
    row = iota((rows, lanes), 0).astype(F32).astype(BF16)
    column = iota((columns, lanes), 0).astype(F32).astype(BF16)
    one, none = jnp.ones((rows, lanes), BF16), jnp.zeros((rows, lanes), BF16)
    blank = jnp.zeros((columns, lanes), BF16)

    def gathered(values, h):
        out = values[:each]
        for g in range(per):
            part = values[g * each : (g + 1) * each]
            by = (g - h) * share % lanes
            part = pltpu.roll(part, by, 1) if by else part
            out = part if g == 0 else jnp.where(lane == g, part, out)
        return out

    for z in range(planes):
        at = z * share // lanes * lanes
        power = gathered(got[:, at : at + lanes], z % per)
        cell = gathered(got[:, total + at : total + at + lanes], z % per).astype(jnp.int32)
        high, low = split(power)
        high, low = high.astype(F32), low.astype(F32)
        x = (cell // columns).astype(F32)
        y = (cell % columns).astype(F32)
        lefts, rights = [], []
        for s in range(each):
            part = slice(s, s + 1)
            lefts.append(jnp.where(row == x[part, :].astype(BF16), one, none))
            hit = column == y[part, :].astype(BF16)
            rights.append(
                jnp.concatenate(
                    [
                        jnp.where(hit, high[part, :].astype(BF16), blank),
                        jnp.where(hit, low[part, :].astype(BF16), blank),
                    ],
                    axis=0,
                )
            )
        sums = mm_nt(jnp.concatenate(lefts, axis=1), jnp.concatenate(rights, axis=1))
        joule[z] = sums[:, :columns] + sums[:, columns:]

    @pl.when(jnp.max(got[:, main:total]) > 0.0)
    def _():
        column = iota((columns, spare), 0)
        for s in range(sources):
            power = got[s : s + 1, main:total]
            cell = got[s : s + 1, total + main :].astype(jnp.int32)
            part = slice(s * spare, (s + 1) * spare)
            high, low = split(power)
            hit = column == cell % columns
            r_scr[:columns, part] = jnp.where(hit, high.astype(F32), 0.0).astype(BF16)
            r_scr[columns:, part] = jnp.where(hit, low.astype(F32), 0.0).astype(BF16)
            k_scr[:, part] = jnp.broadcast_to(cell // columns, (8, spare))
        width = sources * spare
        step = 2048 if width % 2048 == 0 else width
        row = iota((rows, step), 0)

        def plane(z, carry):
            sums = jnp.zeros((rows, 2 * columns), F32)
            for at in range(0, width, step):
                hit = row == k_scr[0:1, at : at + step] - z * rows
                onehot = jnp.where(hit, 1.0, 0.0).astype(BF16)
                sums = sums + mm_nt(onehot, r_scr[:, at : at + step])
            joule[z] += sums[:, :columns] + sums[:, columns:]
            return carry

        lax.fori_loop(0, planes, plane, 0)


def line_parts(position, theta, start, cells):
    growing, falling = jnp.exp(position * theta), jnp.exp(-position * theta)
    lower = growing + falling * jnp.exp(-(2.0 * start + 1.0) * theta)
    upper = falling + growing * jnp.exp(-(2.0 * (cells - start) - 1.0) * theta)
    return lower, upper


def line(conduct, cells):
    lead = HEAT_SPREADING * STIFF * conduct
    t = 0.5 / jnp.sqrt(lead)
    theta = 2.0 * jnp.log1p(t + t * t / (1.0 + jnp.sqrt(1.0 + t * t)))
    scale = 1.0 / (jnp.sqrt(4.0 * lead + 1.0) * (1.0 - jnp.exp(-2.0 * cells * theta)))
    return theta, scale


def prep_kernel(
    sizes, idx, sheet, table, gx_out, gy_out, co_out, gx_ref, gy_ref, co, z_scr, sems,
):
    planes, rows, columns, nx, ny, nz = sizes
    lanes = 128
    extent = rows + EXTRA
    lx, ax, by, dx, dxl, dy, cg, phz, psz, mz, wz = groups_of(
        sizes, co, "lx", "ax", "by", "dx", "dxl", "dy", "cg", "phz", "psz", "mz", "wz"
    )
    gx, gy, gz = idx[0], idx[1], idx[2]
    x0, xn = (gx * rows).astype(F32), float(nx * rows)
    y0, yn = (gy * columns).astype(F32), float(ny * columns)

    def wide(array, width):
        return jnp.concatenate([array] * (width // lanes), axis=1)

    def rows_of(first):
        value = jnp.ones((planes, lanes), F32)
        for z in range(planes):
            one = table[sheet[first + z]]
            value = jnp.where(iota((planes, lanes), 0) == z, one, value)
        return value

    lane_z = iota((8, lanes), 1) % planes
    lane_e = iota((8, lanes), 1) // planes
    by_lane = jnp.ones((8, lanes), F32)
    own = []
    for z in range(planes):
        value = table[sheet[gz * planes + z]]
        own.append(value)
        by_lane = jnp.where(lane_z == z, value, by_lane)
    theta_lane, scale_lane = line(by_lane, yn)
    theta_rows, _ = line(rows_of(gz * planes), 1.0)
    for k in range(nx):
        dx[k] = jnp.exp(-float(k * rows) * theta_rows)
        dxl[k] = jnp.exp(-float(k * rows) * theta_lane)
    for k in range(ny):
        dy[k] = jnp.exp(-float(k * columns) * theta_rows)

    for part in range(nz):
        conduct = rows_of(part * planes)
        theta, scale = line(conduct, xn)
        low, high = line_parts(
            iota((planes, rows), 1).astype(F32), wide(theta, rows), x0, xn
        )
        both = jnp.concatenate([high * wide(scale, rows), low * wide(scale, rows)], axis=0)
        for half in range(rows // lanes):
            ax[part * (rows // lanes) + half] = both[:, half * lanes : (half + 1) * lanes]
        theta, scale = line(conduct, yn)
        low, high = line_parts(iota((planes, columns), 1).astype(F32), theta, y0, yn)
        by[part] = jnp.concatenate([high * scale, low * scale], axis=0)

    minus, plus = jnp.full((8, lanes), -1.0, F32), jnp.full((8, lanes), float(columns), F32)
    low_b, high_b = line_parts(minus, theta_lane, y0, yn)
    low_t, high_t = line_parts(plus, theta_lane, y0, yn)
    r, n = iota((lanes, lanes), 0), iota((lanes, lanes), 1)
    same = r % planes == n % planes
    kind = jnp.where(same, (r // planes) * 4 + n // planes, -1)
    cg[0] = jnp.where(
        kind == 8, (high_b * scale_lane)[0:1, :],
        jnp.where(
            kind == 9, (high_t * scale_lane)[0:1, :],
            jnp.where(
                kind == 12, (low_b * scale_lane)[0:1, :],
                jnp.where(kind == 13, (low_t * scale_lane)[0:1, :], 0.0),
            ),
        ),
    )

    order = iota((extent, lanes), 0)
    index = jnp.where(order == rows, -1, jnp.where(order == rows + 1, rows, order))
    position = index.astype(F32)
    real = order < rows + 2
    index_w, order_w = wide(index, rows), wide(order, rows)
    at_or_past = index_w >= iota((extent, rows), 1)
    lane = iota((extent, lanes), 1)
    packed = jnp.zeros((extent, lanes), F32)
    started = []
    y_col = iota((columns, columns), 0).astype(F32)
    y_i, y_j = iota((columns, columns), 0), iota((columns, columns), 1)
    y_past = y_j >= y_i
    for z in range(planes):
        theta, k_x = line(jnp.full((8, lanes), own[z], F32), xn)
        theta1, k1 = theta[0:1, :], k_x[0:1, :]
        low_c, high_c = line_parts(position, theta1, x0, xn)
        low_c = jnp.where(real, low_c * k1, 0.0)
        high_c = jnp.where(real, high_c * k1, 0.0)
        packed = jnp.where(lane == z, high_c, jnp.where(lane == planes + z, low_c, packed))
        low_r, high_r = line_parts(
            iota((8, rows), 1).astype(F32), wide(theta, rows), x0, xn
        )
        low_r, high_r = low_r[0:1, :], high_r[0:1, :]
        g = jnp.where(at_or_past, wide(high_c, rows) * low_r, wide(low_c, rows) * high_r)
        g = jnp.where(order_w == rows + 2, low_r, jnp.where(order_w == rows + 3, high_r, g))
        gx_ref[z, :extent, :], gx_ref[z, extent:, :] = split(g)

        theta, k_y = line(jnp.full((8, lanes), own[z], F32), yn)
        theta1, k1 = theta[0:1, :], k_y[0:1, :]
        low_r, high_r = line_parts(iota((8, columns), 1).astype(F32), theta, y0, yn)
        low_r, high_r = low_r[0:1, :], high_r[0:1, :]
        low_c, high_c = line_parts(y_col, theta1, y0, yn)
        low_b, _ = line_parts(minus[0:1, :], theta1, y0, yn)
        _, high_t = line_parts(plus[0:1, :], theta1, y0, yn)
        g = k1 * jnp.where(y_past, high_r * low_c, low_r * high_c)
        ext = jnp.zeros((columns, lanes), F32)
        for e, values in enumerate((low_b * high_c * k1, high_t * low_c * k1, low_c, high_c)):
            ext = jnp.where(y_j == e * planes + z, values, ext)
        gy_ref[z, :, :lanes], gy_ref[planes + z, :, :lanes] = split(g)
        gy_ref[z, :, lanes:], gy_ref[planes + z, :, lanes:] = split(ext)
        for k, (src, dst, at) in enumerate(
            ((gx_ref, gx_out, z), (gy_ref, gy_out, z), (gy_ref, gy_out, planes + z))
        ):
            started.append(pltpu.make_async_copy(src.at[at], dst.at[at], sems.at[3 * z + k]))
            started[-1].start()
    lx[0] = packed

    total = planes * nz
    cond = [jnp.full((8, lanes), table[sheet[z]], F32) for z in range(total)]
    lead = [HEAT_SPREADING * STIFF * 0.5 * (cond[z] + cond[z + 1]) for z in range(total - 1)]
    lower = [jnp.ones((8, lanes), F32)]
    flux = HEAT_SPREADING * STIFF * cond[0]
    resist = [1.0 / value for value in lead]
    for z in range(total - 1):
        flux = flux + lower[z]
        lower.append(lower[z] + flux * resist[z])
    weight = 1.0 / (flux + lower[total - 1])
    upper = [None] * total
    upper[total - 1] = weight
    flux = jnp.zeros((8, lanes), F32)
    for z in range(total - 2, -1, -1):
        flux = flux + upper[z + 1]
        upper[z] = upper[z + 1] + flux * resist[z]
    zero = jnp.zeros((8, lanes), F32)
    z_scr[0], z_scr[total + 3] = zero, zero
    z_scr[total + 1], z_scr[total + 2] = zero, zero
    for z in range(total):
        z_scr[1 + z] = lower[z]
        z_scr[total + 3 + z] = upper[z]
    z_scr[2 * total + 3] = zero
    mine = gz * planes
    for z in range(planes + 2):
        phz[z] = z_scr[mine + z]
        psz[z] = jnp.where(mine + z == 0, zero, z_scr[total + 2 + mine + z])

    low_lane, high_lane = zero, zero
    for z in range(planes):
        low_lane = jnp.where(lane_z == z, phz[z + 1], low_lane)
        high_lane = jnp.where(lane_z == z, psz[z + 1], high_lane)
    row_p, lane_p = iota((planes, lanes), 0), iota((planes, lanes), 1)
    low_rows, high_rows = jnp.zeros((planes, lanes), F32), jnp.zeros((planes, lanes), F32)
    for z in range(planes):
        low_rows = jnp.where(row_p == z, phz[z + 1][0:1, :], low_rows)
        high_rows = jnp.where(row_p == z, psz[z + 1][0:1, :], high_rows)
    blocks, ends = [], []
    for e in range(2):
        g = jnp.where(
            lane_p % planes >= row_p,
            low_rows * high_lane[0:1, :],
            high_rows * low_lane[0:1, :],
        )
        blocks.append(jnp.where(lane_p // planes == e, g, 0.0))
        ends.append(
            jnp.where(lane_p == e, low_rows, jnp.where(lane_p == 2 + e, high_rows, 0.0))
        )
    rest = jnp.zeros((lanes - 2 * planes, lanes), F32)
    mz[0] = jnp.concatenate(blocks + [rest], axis=0)
    mz[1] = jnp.concatenate(ends + [rest], axis=0)
    row8 = iota((8, lanes), 0)
    wz[0] = jnp.where(
        (row8 < 2) & (lane_e == row8),
        high_lane,
        jnp.where((row8 >= 2) & (row8 < 4) & (lane_e == row8 - 2), low_lane, 0.0),
    )
    started.append(pltpu.make_async_copy(co, co_out, sems.at[3 * planes]))
    started[-1].start()
    for copy in started:
        copy.wait()


def slopes(
    counts, idx, sheet, table, scaling, u_ref, kind_ref, xr0, xr1, yr0, yr1, zr0, zr1,
    ux, uy, uz, kx0, kx1, ky0, ky1, kz,
):
    planes, rows, columns = u_ref.shape
    even = [idx[d] % 2 == 0 for d in range(3)]
    at_low = [idx[d] == 0 for d in range(3)]
    at_high = [idx[d] == counts[d] - 1 for d in range(3)]
    row, lane = iota((rows, columns), 0), iota((rows, columns), 1)

    def ends(first, second, d):
        return jnp.where(even[d], second, first), jnp.where(even[d], first, second)

    low, high = ends(xr0[0], xr1[0], 0)
    ux[...] = jnp.zeros(ux.shape, F32)
    for z in range(planes):
        ux[z, 0:1, :] = low[z : z + 1, :]
        ux[z, 1:2, :] = high[z : z + 1, :]
    x_low, x_high = ends(xr0[1], xr1[1], 0)
    low, high = ends(yr0[...], yr1[...], 1)
    kind = iota((rows, 128), 1) // planes
    uy[...] = jnp.zeros(uy.shape, F32)
    uy[:rows, :] = jnp.where(
        kind == 0, low, jnp.where(kind == 1, pltpu.roll(high, planes, 1), 0.0)
    )
    low, high = ends(zr0[0], zr1[0], 2)
    uz[0] = jnp.where(at_low[2], 0.0, low)
    uz[1] = high
    z_low, z_high = ends(zr0[1], zr1[1], 2)
    half = 0.5 * HEAT_SPREADING
    y_low, y_high = ends(yr0[...], yr1[...], 1)
    c_before = None
    for z in range(planes):
        c = conductance(z, idx, sheet, table, scaling, kind_ref)
        first = jnp.where(at_low[0], -c[0:1, :], x_low[z : z + 1, :])
        final = jnp.where(at_high[0], -c[rows - 1 :, :], x_high[z : z + 1, :])
        kx0[z] = half * (c + jnp.where(row == 0, first, pltpu.roll(c, 1, 0)))
        kx1[z] = half * (c + jnp.where(row == rows - 1, final, pltpu.roll(c, rows - 1, 0)))
        first = jnp.where(at_low[1], -c, pltpu.roll(y_low, columns - planes - z, 1))
        final = jnp.where(at_high[1], -c, pltpu.roll(y_high, columns - 1 - planes - z, 1))
        ky0[z] = half * (c + jnp.where(lane == 0, first, pltpu.roll(c, 1, 1)))
        ky1[z] = half * (c + jnp.where(lane == columns - 1, final, pltpu.roll(c, columns - 1, 1)))
        if z == 0:
            kz[z] = half * (c + jnp.where(at_low[2], c, z_low))
        else:
            kz[z] = half * (c + c_before)
        c_before = c
        if z == planes - 1:
            kz[planes] = half * jnp.where(at_high[2], 0.0, c + z_high)


def outflow(z, u_ref, ux, uy, uz, kx0, kx1, ky0, ky1, kz):
    planes, rows, columns = u_ref.shape
    u = u_ref[z]
    row, lane = iota((rows, columns), 0), iota((rows, columns), 1)
    edge = uy[:rows, :]
    edge_low = pltpu.roll(edge, columns - z, 1) if z else edge
    edge_high = pltpu.roll(edge, columns - 1 - planes - z, 1)
    below = uz[0] if z == 0 else u_ref[z - 1]
    above = uz[1] if z == planes - 1 else u_ref[z + 1]
    total = kx0[z] * (jnp.where(row == 0, ux[z, 0:1, :], pltpu.roll(u, 1, 0)) - u)
    total += kx1[z] * (
        jnp.where(row == rows - 1, ux[z, 1:2, :], pltpu.roll(u, rows - 1, 0)) - u
    )
    total += ky0[z] * (jnp.where(lane == 0, edge_low, pltpu.roll(u, 1, 1)) - u)
    total += ky1[z] * (
        jnp.where(lane == columns - 1, edge_high, pltpu.roll(u, columns - 1, 1)) - u
    )
    return total + kz[z] * (below - u) + kz[z + 1] * (above - u)


def advance(idx, source_of, gx_ref, gy_ref, phz, psz, t_ref, e_ref, z_send, x_sends):
    planes, extent, columns = t_ref.shape
    rows = extent - EXTRA
    sums = jnp.zeros((extent, 128), F32)
    below, above = jnp.zeros((rows, columns), F32), jnp.zeros((rows, columns), F32)
    for z in range(planes):
        high, low = split(source_of(z))
        out = mm(gx_ref[z], jnp.concatenate([high, low], axis=1))
        t = out[:extent, :columns] + (out[:extent, columns:] + out[extent:, :columns])
        high, low = split(t)
        out = mm(jnp.concatenate([high, low], axis=0), gy_ref[z])
        out = out[:extent] + (out[extent:] + mm(high, gy_ref[planes + z]))
        t_ref[z] = out[:, :columns]
        sums += out[:, columns:]
        main = out[:rows, :columns]
        below += phz[z + 1][0:1, :] * main
        above += psz[z + 1][0:1, :] * main
    e_ref[...] = sums
    for b, send in enumerate(x_sends):
        take = jnp.where((idx[0] >> b) % 2 == 0, 0, 1)
        for z in range(planes):
            pair = t_ref[z, rows + 2 : rows + 4, :]
            send[z : z + 1, :] = jnp.where(take == 0, pair[0:1], pair[1:2])
        pair = sums[rows + 2 : rows + 4, :]
        send[planes:, :] = jnp.broadcast_to(
            jnp.where(take == 0, pair[0:1], pair[1:2]), (8, 128)
        )
    z_send[0], z_send[1] = below, above


def start_kernel(sizes, idx, sheet, table, scaling, u_ref, kind_ref,
                 xr0, xr1, yr0, yr1, zr0, zr1, got_in, gx_in, gy_in, co_in, ux, uy, uz, kx0, kx1, ky0, ky1, kz,
                 joule, t_ref, e_ref, *rest):
    sends, (r_scr, k_scr, gx_ref, gy_ref, co, got, sems) = rest[:-7], rest[-7:]
    started = copies(
        [(got_in.at[:, 0, :], got), (gx_in, gx_ref), (gy_in, gy_ref), (co_in, co)], sems
    )
    for copy in started:
        copy.start()
    phz, psz = groups_of(sizes, co, "phz", "psz")
    slopes(
        sizes[3:], idx, sheet, table, scaling, u_ref, kind_ref, xr0, xr1, yr0, yr1, zr0, zr1,
        ux, uy, uz, kx0, kx1, ky0, ky1, kz,
    )
    started[0].wait()
    joule_into(got, joule, r_scr, k_scr)
    for copy in started[1:]:
        copy.wait()

    def source_of(z):
        out = outflow(z, u_ref, ux, uy, uz, kx0, kx1, ky0, ky1, kz)
        return out + OHMIC_POWER * ((1.0 + WARMING_SLOPE * u_ref[z]) * joule[z])

    advance(
        idx, source_of, gx_ref, gy_ref, phz, psz, t_ref, e_ref, sends[0], sends[1:]
    )


def x_kernel(sizes, idx, e_ref, co, pair, near, *rest):
    planes, nx = sizes[0], sizes[3]
    gots, (e_out, f_out, send), far = rest[: nx - 1], rest[nx - 1 : nx + 2], rest[nx + 2 :]
    for out in far:
        out[...] = jnp.where((idx[2] >> 1) % 2 == 0, pair[0] + near[0], pair[1] + near[1])
    dx, dxl, lx = groups_of(sizes, co, "dx", "dxl", "lx")
    me = idx[0]
    sums = [[jnp.zeros((planes, 128), F32), jnp.zeros((8, 128), F32)] for _ in range(2)]
    for k, got in zip(range(1, nx), gots):
        other = partner(me, k, nx)
        far = jnp.abs(me - other)
        pair = got[:planes, :] * dx[far], got[planes:, :] * dxl[far]
        for side, keep in ((0, other < me), (1, other > me)):
            for part in range(2):
                sums[side][part] += jnp.where(keep, pair[part], 0.0)
    f_out[:planes, :], f_out[planes:, :] = sums[0][0], sums[1][0]
    row, lane = iota((planes, 128), 0), iota((planes, 128), 1)
    own = lane % planes == row
    ext = jnp.concatenate(
        [jnp.where(own, sums[0][1][0:1, :], 0.0), jnp.where(own, sums[1][1][0:1, :], 0.0)],
        axis=0,
    )
    e = e_ref[...] + exact(lx[0][:, : 2 * planes], ext)
    e_out[...] = e
    send[...] = e.T[2 * planes : 4 * planes]


def four(rows):
    return jnp.concatenate([rows] * 4, axis=0)


def weights(ref, planes):
    row = iota((planes, 128), 0)
    values = jnp.zeros((planes, 128), F32)
    for z in range(planes):
        values = jnp.where(row == z, ref[z + 1][0:1, :], values)
    return values


def y_kernel(sizes, idx, t_ref, e_ref, f_ref, co, *rest):
    ny = sizes[4]
    dy, lx, by, cg, phz, psz, mz = groups_of(
        sizes, co, "dy", "lx", "by", "cg", "phz", "psz", "mz"
    )
    gots, rest = rest[: ny - 1], rest[ny - 1 :]
    q_ref, l_ref, b_ref = rest[:3]
    sends = rest[3:]
    planes, extent, columns = t_ref.shape
    rows = extent - EXTRA
    me = idx[1]
    row = iota((2 * planes, extent), 0)
    across = jnp.zeros((2 * planes, extent), F32)
    for k, got in zip(range(1, ny), gots):
        other = partner(me, k, ny)
        far = jnp.concatenate([dy[jnp.abs(me - other)][:, 0:1]] * 2, axis=0)
        keep = (row < planes) == (other < me)
        across += jnp.where(keep, got[...] * far, 0.0)
    others = jnp.concatenate(
        [
            jnp.zeros((2 * planes, extent), F32),
            across,
            jnp.zeros((128 - 4 * planes, extent), F32),
        ],
        axis=0,
    ).T
    lane = iota((extent, 128), 1)
    q = jnp.where(lane < 2 * planes, e_ref[...], 0.0) + exact(others, cg[0])
    q_ref[...] = q
    left = lx[0] + others
    l_ref[...] = left
    right = jnp.concatenate([f_ref[...], by[idx[2]]], axis=0)
    b_ref[...] = right
    edge = exact(q[:rows], mz[1]).T
    ghost = slice(rows, rows + 8)
    low, high = weights(phz, planes), weights(psz, planes)
    both = jnp.concatenate([right * four(low), right * four(high)], axis=1)
    ghosts = exact(left[ghost, : 4 * planes], both)
    g_low, g_high = ghosts[:, :128], ghosts[:, 128:]
    for z in range(planes):
        value = t_ref[z, ghost, :]
        g_low += phz[z + 1][0:1, :] * value
        g_high += psz[z + 1][0:1, :] * value
    for b, send in enumerate(sends):
        lower = (idx[2] >> b) % 2 == 0
        scale = jnp.where(lower, low, high)
        twice = jnp.concatenate([scale] * 2, axis=0)
        send[:8, :] = jnp.where(lower, g_low, g_high)
        send[8 : 8 + 2 * planes, :] = f_ref[...] * twice
        at = 8 + 2 * planes
        for part in range(rows // 128):
            cols = slice(part * 128, (part + 1) * 128)
            send[at : at + 8, :] = edge[0:8, cols]
            send[at + 8 : at + 8 + 2 * planes, :] = across[:, cols] * twice
            at += 8 + 2 * planes


def carried(nz, idx, bigs, smalls, ax, by, rows, ghosts):
    me = idx[2]
    planes = by.each // 2
    at_top = me % 2 == 1
    below = jnp.where(at_top, bigs[0][0], 0.0)
    above = jnp.where(at_top, 0.0, bigs[0][1])
    for b, big in enumerate(bigs[1:], 1):
        at_top = (me >> b) % 2 == 1
        below += jnp.where(at_top, big[...], 0.0)
        above += jnp.where(at_top, 0.0, big[...])
    g_below = g_above = edges = 0.0
    lefts, rights = [], []
    sub = iota((8, rows), 0)
    for k, small in zip(range(1, nz), smalls):
        other = partner(me, k, nz)
        lower = other < me

        at, stride = 8 + 2 * planes, 8 + 2 * planes
        parts = [at + p * stride for p in range(rows // 128)]
        across = jnp.concatenate([small[p + 8 : p + stride, :] for p in parts], axis=1)
        halves = rows // 128
        near = [ax[other * halves + half] for half in range(halves)]
        lefts += [jnp.concatenate(near, axis=1), across]
        right = jnp.concatenate([small[8:at, :], by[other]], axis=0)
        rights.append(
            jnp.concatenate(
                [jnp.where(lower, right, 0.0), jnp.where(lower, 0.0, right)], axis=1
            )
        )
        if ghosts:
            g_below += jnp.where(lower, small[:8, :], 0.0)
            g_above += jnp.where(lower, 0.0, small[:8, :])
            value = jnp.concatenate([small[p : p + 8, :] for p in parts], axis=1)
            edges += jnp.where(sub // 2 == jnp.where(lower, 0, 1), value, 0.0)
    more = exact(
        jnp.concatenate(lefts, axis=0), jnp.concatenate(rights, axis=0), ((0,), (0,))
    )
    below, above = below + more[:, :128], above + more[:, 128:]
    return below, above, g_below, g_above, edges


def whole_planes(t_ref, l_ref, b_ref, second, extent):
    planes = t_ref.shape[0]
    high, low = split(l_ref[:extent, : 4 * planes])
    pair = jnp.concatenate([high, low], axis=0)
    right = b_ref[...]
    row = iota(right.shape, 0) % planes
    for z in range(planes):
        r_high, r_low = split(jnp.where(row == z, right, 0.0))
        out = mm(pair, r_high)
        second[z] = t_ref[z, :extent, :] + (out[:extent] + (out[extent:] + mm(high, r_low)))


def change(outside, second, phz, psz, below, above, emit):
    planes = second.shape[0]
    tails = [above]
    for z in range(planes - 1, -1, -1):
        tails.append(tails[-1] + psz[z + 1][0:1, :] * second[z])
    tails = tails[::-1]
    if outside:
        emit(-1, psz[0][0:1, :] * below + phz[0][0:1, :] * tails[0])
    head = below
    for z in range(planes):
        head = head + phz[z + 1][0:1, :] * second[z]
        emit(z, psz[z + 1][0:1, :] * head + phz[z + 1][0:1, :] * tails[z + 1])
    if outside:
        emit(planes, psz[planes + 1][0:1, :] * head + phz[planes + 1][0:1, :] * above)


def rise_kernel(sizes, idx, t_in, l_ref, b_ref, q_ref, co,
                u_ref, ux, uy, uz, kx0, kx1, ky0, ky1, kz, joule, gx_ref, gy_ref, *rest):
    nz = sizes[5]
    phz, psz, mz, wz, ax, by = groups_of(sizes, co, "phz", "psz", "mz", "wz", "ax", "by")
    deep = (nz - 1).bit_length()
    bigs, smalls, rest = rest[:deep], rest[deep : deep + nz - 1], rest[deep + nz - 1 :]
    u_out, ux_out, uy_out, uz_out, t_ref, e_ref = rest[:6]
    sends, second = rest[6:-1], rest[-1]
    planes, rows, columns = u_ref.shape
    whole_planes(t_in, l_ref, b_ref, second, rows + 8)
    below, above, g_below, g_above, edges = carried(nz, idx, bigs, smalls, ax, by, rows, True)

    def emit(z, value):
        if z == -1:
            uz_out[0] = uz[0] + value[:rows]
        elif z == planes:
            uz_out[1] = uz[1] + value[:rows]
        else:
            u_out[z] = u_ref[z] + value[:rows]
            ux_out[z] = ux[z] + value[rows:]

    change(
        True, second, phz, psz,
        jnp.concatenate([below, g_below], axis=0),
        jnp.concatenate([above, g_above], axis=0),
        emit,
    )
    grown = exact(q_ref[:rows, :], mz[0]) + exact(edges, wz[0], ((0,), (0,)))
    uy_out[...] = uy[...]
    uy_out[:rows, :] = uy[:rows, :] + grown

    def source_of(z):
        out = outflow(z, u_out, ux_out, uy_out, uz_out, kx0, kx1, ky0, ky1, kz)
        return out + OHMIC_POWER * ((1.0 + WARMING_SLOPE * u_out[z]) * joule[z])

    advance(
        idx, source_of, gx_ref, gy_ref, phz, psz, t_ref, e_ref, sends[0], sends[1:]
    )


def finish_kernel(sizes, idx, t_in, l_ref, b_ref, co, u_ref, joule, *rest):
    nz = sizes[5]
    phz, psz, ax, by = groups_of(sizes, co, "phz", "psz", "ax", "by")
    deep = (nz - 1).bit_length()
    bigs, smalls, rest = rest[:deep], rest[deep : deep + nz - 1], rest[deep + nz - 1 :]
    u_out, heat_out, second = rest
    rows = u_ref.shape[1]
    whole_planes(t_in, l_ref, b_ref, second, rows)
    below, above, _, _, _ = carried(nz, idx, bigs, smalls, ax, by, rows, False)

    def emit(z, value):
        u = u_ref[z] + value
        u_out[z] = u
        heat_out[z] = (1.0 + WARMING_SLOPE * u) * joule[z]

    change(False, second, phz, psz, below, above, emit)


def per_device(
    starting_warmth,
    sheet_stratum_number,
    stratum_heat_conduction,
    substance_kind,
    substance_kind_scaling,
    wire_piece_amperes,
    wire_piece_ohms_base,
    wire_piece_tile,
    wire_piece_voxel,
):
    planes, rows, columns = starting_warmth.shape
    counts = tuple(lax.axis_size(axis) for axis in ("gx", "gy", "gz"))
    nx, ny, nz = counts
    bits = [(n - 1).bit_length() for n in counts]
    devices = nx * ny * nz
    extent = rows + EXTRA
    idx = jnp.stack([lax.axis_index(axis) for axis in ("gx", "gy", "gz")]).astype(jnp.int32)
    block = shaped(planes, rows, columns)
    tables = sheet_stratum_number, stratum_heat_conduction, substance_kind_scaling

    count = wire_piece_amperes.shape[0]
    capacity = 2 * count // devices
    lanes = 128
    chunks = count // lanes
    segments = tuple(
        part.reshape(chunks, lanes)
        for part in (
            wire_piece_amperes, wire_piece_ohms_base, wire_piece_tile, wire_piece_voxel
        )
    )
    share, spare = shares(capacity)
    slots = planes * share + spare
    (send,) = call(
        functools.partial(dispatch_kernel, devices, planes, rows * columns, capacity),
        [shaped(devices, 1, 2 * slots)],
        segments,
        far=4,
        vmem=60,
        scratch=[pltpu.VMEM((chunks, lanes), part.dtype) for part in segments]
        + [
            pltpu.VMEM((5 * devices, count), BF16),
            pltpu.VMEM((max(planes * share, spare), count), BF16),
            pltpu.VMEM((devices * planes, lanes), F32),
            pltpu.VMEM((chunks, lanes), jnp.int32),
            pltpu.SemaphoreType.DMA((4,)),
        ],
    )
    got = lax.all_to_all(send, ("gx", "gy", "gz"), split_axis=0, concat_axis=0, tiled=True)

    xs0, xs1, ys0, ys1, zs0, zs1 = call(
        faces_kernel,
        [shaped(2, planes, columns)] * 2
        + [shaped(rows, 128)] * 2
        + [shaped(2, rows, columns)] * 2,
        (idx, *tables, starting_warmth, substance_kind),
        smem=4,
        far=2,
        vmem=60,
        scratch=[
            pltpu.VMEM(block.shape, F32),
            pltpu.VMEM(block.shape, jnp.int32),
            pltpu.SemaphoreType.DMA((2, planes)),
        ],
    )
    zr = next_pairs(zs0, zs1, "gz")
    xr = next_pairs(xs0, xs1, "gx")
    yr = next_pairs(ys0, ys1, "gy")
    sizes = (planes, rows, columns, nx, ny, nz)
    coefficients = [
        shaped(planes, 2 * extent, rows, dtype=BF16),
        shaped(2 * planes, columns, 256, dtype=BF16),
        shaped(table_rows(*sizes)[1], lanes),
    ]
    room = [pltpu.VMEM(o.shape, o.dtype) for o in coefficients]
    gx_m, gy_m, co = call(
        functools.partial(prep_kernel, sizes),
        coefficients,
        (idx, *tables[:2]),
        smem=3,
        vmem=60,
        scratch=room
        + [
            pltpu.VMEM((2 * planes * nz + 4, 8, lanes), F32),
            pltpu.SemaphoreType.DMA((3 * planes + 1,)),
        ],
        far_out=True,
    )
    step_out = [shaped(planes, extent, columns), shaped(extent, 128)]
    step_out += [shaped(2, rows, columns)] + [shaped(planes + 8, columns)] * bits[0]
    total = devices * spare
    ghosts = [shaped(planes, 8, columns), shaped(extent, 128), shaped(2, rows, columns)]
    ux, uy, uz, *rest = call(
        functools.partial(start_kernel, sizes),
        ghosts + [block] * 4 + [shaped(planes + 1, rows, columns), block] + step_out,
        (idx, *tables, starting_warmth, substance_kind, *xr, *yr, *zr, got, gx_m, gy_m, co),
        smem=4,
        far=4,
        scratch=[
            pltpu.VMEM((2 * columns, total), BF16),
            pltpu.VMEM((8, total), jnp.int32),
            *room,
            pltpu.VMEM((devices, 2 * slots), F32),
            pltpu.SemaphoreType.DMA((4,)),
        ],
    )
    conduct, (joule, t, e, *sends) = rest[:5], rest[5:]
    u = starting_warmth
    small = shaped(8 + 2 * planes + (8 + 2 * planes) * (rows // 128), 128)
    for repeat in range(STEPS):
        pair, *sends = sends
        gots = all_pairs(sends, "gx")
        near = crossed(pair, 1, "gz")
        e, f, send, *far = call(
            functools.partial(x_kernel, sizes),
            [shaped(extent, 128), shaped(2 * planes, columns), shaped(2 * planes, extent)]
            + [shaped(rows, columns)] * (bits[2] - 1),
            (idx, e, co, pair, near, *gots),
            smem=1,
        )
        bigs = [near] + [crossed(array, 2, "gz") for array in far]
        gots = all_pairs([send] * bits[1], "gy")
        q, left, right, *sends = call(
            functools.partial(y_kernel, sizes),
            [shaped(extent, 128)] * 2 + [shaped(4 * planes, columns)] + [small] * bits[2],
            (idx, t, e, f, co, *gots),
            smem=1,
        )
        smalls = all_pairs(sends, "gz")
        if repeat < STEPS - 1:
            u, ux, uy, uz, t, e, *sends = call(
                functools.partial(rise_kernel, sizes),
                [block, shaped(planes, 8, columns), shaped(extent, 128)]
                + [shaped(2, rows, columns)]
                + step_out,
                (idx, t, left, right, q, co, u, ux, uy, uz, *conduct)
                + (joule, gx_m, gy_m, *bigs, *smalls),
                smem=1,
                scratch=[pltpu.VMEM((planes, rows + 8, columns), F32)],
            )
    return tuple(
        call(
            functools.partial(finish_kernel, sizes),
            [block, block],
            (idx, t, left, right, co, u, joule, *bigs, *smalls),
            smem=1,
            scratch=[pltpu.VMEM((planes, rows, columns), F32)],
        )
    )


def solution(mesh):
    return jax.shard_map(
        per_device,
        mesh=mesh,
        in_specs=(
            P("gz", "gx", "gy"),
            P(),
            P(),
            P("gz", "gx", "gy"),
            P(),
            P(("gx", "gy", "gz")),
            P(("gx", "gy", "gz")),
            P(("gx", "gy", "gz"), None),
            P(("gx", "gy", "gz")),
        ),
        out_specs=(P("gz", "gx", "gy"), P("gz", "gx", "gy")),
        check_vma=False,
    )
```

```python
import functools

import jax
import jax.numpy as jnp
from jax import lax
from jax.experimental import pallas as pl
from jax.experimental.pallas import tpu as pltpu
from jax.sharding import PartitionSpec as P

STEPS = 2
HEAT_SPREADING = 1000.0
STIFF = 1.5
WARMING_SLOPE = 0.1
OHMIC_POWER = 8.0

F32 = jnp.float32
BF16 = jnp.bfloat16
EXTRA = 16
EXACT = lax.Precision.HIGHEST


def call(kernel, out_shapes, args, smem=0, scratch=(), vmem=24, far=0, far_out=False):
    specs = [pl.BlockSpec(memory_space=pltpu.SMEM)] * smem
    specs += [pl.BlockSpec(memory_space=pltpu.VMEM)] * (len(args) - smem - far)
    specs += [pl.BlockSpec(memory_space=pl.ANY)] * far
    return pl.pallas_call(
        kernel,
        out_shape=out_shapes,
        in_specs=specs,
        out_specs=[pl.BlockSpec(memory_space=pl.ANY if far_out else pltpu.VMEM)]
        * len(out_shapes),
        scratch_shapes=list(scratch),
        compiler_params=pltpu.CompilerParams(vmem_limit_bytes=vmem * 2**20),
        cost_estimate=pl.CostEstimate(flops=0, bytes_accessed=1, transcendentals=0),
    )(*args)


def shaped(*shape, dtype=F32):
    return jax.ShapeDtypeStruct(shape, dtype)


def split(x):
    high = x.astype(BF16)
    return high, (x - high.astype(F32)).astype(BF16)


def iota(shape, dim):
    return lax.broadcasted_iota(jnp.int32, shape, dim)


def copies(pairs, sems):
    return [
        pltpu.make_async_copy(src, dst, sems.at[k]) for k, (src, dst) in enumerate(pairs)
    ]


def plane_copies(pairs, sems):
    started = [
        [
            pltpu.make_async_copy(src.at[z], dst.at[z], sems.at[k, z])
            for z in range(dst.shape[0])
        ]
        for k, (src, dst) in enumerate(pairs)
    ]
    for copies_of_plane in zip(*started):
        for copy in copies_of_plane:
            copy.start()
    return started


def mm(a, b):
    return jnp.dot(a, b, preferred_element_type=F32)


def exact(a, b, dims=((1,), (0,))):
    return lax.dot_general(a, b, (dims, ((), ())), precision=EXACT, preferred_element_type=F32)


def stacked(a, b):
    (a_high, a_low), (b_high, b_low) = split(a), split(b)
    return mm(
        jnp.concatenate([a_high, a_low, a_high], axis=1),
        jnp.concatenate([b_high, b_high, b_low], axis=0),
    )


def mm_nt(a, b):
    return lax.dot_general(a, b, (((1,), (1,)), ((), ())), preferred_element_type=F32)


def table_rows(planes, rows, columns, nx, ny, nz):
    at, places = 0, {}
    for name, items, each in (
        ("lx", 1, rows + EXTRA),
        ("ax", nz * (rows // 128), 2 * planes),
        ("by", nz, 2 * planes),
        ("dx", nx, planes),
        ("dxl", nx, 8),
        ("dy", ny, planes),
        ("cg", 1, 128),
        ("phz", planes + 2, 8),
        ("psz", planes + 2, 8),
        ("mz", 2, 128),
        ("wz", 1, 8),
    ):
        places[name] = (at, each)
        at += items * each
    return places, at


class Group:
    def __init__(self, ref, place):
        self.ref, (self.at, self.each) = ref, place

    def rows(self, k):
        at = self.at + k * self.each
        return pl.ds(at if isinstance(at, int) else pl.multiple_of(at, 8), self.each)

    def __getitem__(self, k):
        return self.ref[self.rows(k), :]

    def __setitem__(self, k, value):
        self.ref[self.rows(k), :] = value


def groups_of(sizes, ref, *names):
    places, _ = table_rows(*sizes)
    return [Group(ref, places[name]) for name in names]


def partner(me, k, n):
    return me ^ k


def groups(n):
    return [k.bit_length() - 1 for k in range(1, n)]


def all_pairs(arrays, axis):
    n = lax.axis_size(axis)
    return [
        lax.ppermute(arrays[b], axis, [(i, i ^ k) for i in range(n)])
        for k, b in zip(range(1, n), groups(n))
    ]


def crossed(array, k, axis):
    return lax.ppermute(array, axis, [(i, i ^ k) for i in range(lax.axis_size(axis))])


def next_pairs(even, odd, axis):
    n = lax.axis_size(axis)
    first = lax.ppermute(even, axis, [(i, i ^ 1) for i in range(n)])
    if n == 2:
        return first, first
    pairs = [(i, i + 1) for i in range(1, n - 1, 2)]
    return first, lax.ppermute(odd, axis, pairs + [(b, a) for a, b in pairs])


def conductance(z, idx, sheet, table, scaling, kind_ref):
    factor = jnp.zeros(kind_ref.shape[1:], F32)
    for category in range(scaling.shape[0]):
        factor = jnp.where(kind_ref[z] == category, scaling[category], factor)
    return table[sheet[idx[2] * kind_ref.shape[0] + z]] * factor


def faces(
    idx, sheet, table, scaling, u_ref, kind_ref, started, xs0, xs1, ys0, ys1, zs0, zs1
):
    planes, rows, columns = u_ref.shape
    even = [idx[d] % 2 == 0 for d in range(3)]
    lane = iota((rows, columns), 1)
    low = jnp.zeros((rows, columns), F32)
    high = jnp.zeros((rows, columns), F32)
    for z in range(planes):
        started[0][z].wait()
        started[1][z].wait()
        u, c = u_ref[z], conductance(z, idx, sheet, table, scaling, kind_ref)
        if z == 0:
            zs0[1], zs1[1] = c, c
        elif z == planes - 1:
            zs0[1] = jnp.where(even[2], c, zs0[1])
            zs1[1] = jnp.where(even[2], zs1[1], c)
        for slot, values in ((0, u), (1, c)):
            at = slot * planes + z
            low = jnp.where(lane == at, pltpu.roll(values, at, 1) if at else values, low)
            high = jnp.where(lane == at, pltpu.roll(values, at + 1, 1), high)
            first, last = values[0:1, :], values[rows - 1 : rows, :]
            xs0[slot, z : z + 1, :] = jnp.where(even[0], last, first)
            xs1[slot, z : z + 1, :] = jnp.where(even[0], first, last)
    ys0[...] = jnp.where(even[1], high, low)
    ys1[...] = jnp.where(even[1], low, high)
    zs0[0] = jnp.where(even[2], u_ref[planes - 1], u_ref[0])
    zs1[0] = jnp.where(even[2], u_ref[0], u_ref[planes - 1])


def shares(capacity):
    return capacity // 4, capacity - capacity // 4


def first_kernel(blocks, planes, area, capacity, idx, sheet, table, scaling,
                 amps_in, ohms_in, tile_in, cell_in, u_in, kind_in,
                 send, xs0, xs1, ys0, ys1, zs0, zs1,
                 amps, ohms, tiles, cells, a_scr, b_scr, z_scr, k_scr, u_ref, kind_ref,
                 sems, plane_sems):
    started = copies(
        [(amps_in, amps), (ohms_in, ohms), (tile_in, tiles), (cell_in, cells)], sems
    )
    for copy in started:
        copy.start()
    loads = plane_copies([(u_in, u_ref), (kind_in, kind_ref)], plane_sems)
    for copy in started:
        copy.wait()
    dispatch(
        blocks, planes, area, capacity, amps, ohms, tiles, cells, send,
        a_scr, b_scr, z_scr, k_scr,
    )
    faces(
        idx, sheet, table, scaling, u_ref, kind_ref, loads, xs0, xs1, ys0, ys1, zs0, zs1
    )


def dispatch(blocks, planes, area, capacity, amps, ohms, tiles, cells, send,
             a_scr, b_scr, z_scr, k_scr):
    chunks, lanes = amps.shape
    share, spare = shares(capacity)
    keys, main = blocks * planes, planes * share
    power = amps[...] * amps[...] * ohms[...]
    tile, cell = tiles[...], cells[...]
    plane, within = cell // area, cell % area
    key = tile * planes + plane
    p_high, p_low = split(power)
    pieces = [
        p_high.astype(F32),
        p_low.astype(F32),
        (within >> 8).astype(F32),
        (within & 255).astype(F32),
        plane.astype(F32),
    ]
    key_row, block_row = iota((keys, lanes), 0), iota((blocks, lanes), 0)
    place = iota((main, lanes), 0)
    pair = 2 * lanes
    ahead = jnp.where(iota((pair, pair), 0) < iota((pair, pair), 1), 1.0, 0.0).astype(BF16)
    base = jnp.zeros((keys, lanes), F32)
    for c in range(0, chunks, 2):
        hits = [key_row == key[c + k : c + k + 1, :] for k in range(2)]
        ones = [jnp.where(hit, 1.0, 0.0) for hit in hits]
        counted = mm(jnp.concatenate(ones, axis=1).astype(BF16), ahead)
        for k in range(2):
            row, cols = slice(c + k, c + k + 1), slice((c + k) * lanes, (c + k + 1) * lanes)
            order = counted[:, k * lanes : (k + 1) * lanes] + base
            rank = jnp.sum(jnp.where(hits[k], order, 0.0), axis=0, keepdims=True)
            rank = rank.astype(jnp.int32)
            k_scr[row, :] = rank
            slot = jnp.where(rank < share, plane[row, :] * share + rank, -1)
            b_scr[:main, cols] = jnp.where(place == slot, 1.0, 0.0).astype(BF16)
            hit = block_row == tile[row, :]
            for n, piece in enumerate(pieces):
                a_scr[n * blocks : (n + 1) * blocks, cols] = jnp.where(
                    hit, piece[row, :], 0.0
                ).astype(BF16)
        base = base + (counted[:, pair - 1 :] + ones[1][:, lanes - 1 :])
    out = mm_nt(a_scr[: 4 * blocks, :], b_scr[:main, :])
    r = [out[k * blocks : (k + 1) * blocks] for k in range(4)]
    total = main + spare
    send[:, 0, :main] = r[0] + r[1]
    send[:, 0, total : total + main] = r[2] * 256.0 + r[3]
    send[:, 0, main:total] = jnp.zeros((blocks, spare), F32)
    send[:, 0, total + main :] = jnp.zeros((blocks, spare), F32)
    z_scr[...] = jnp.maximum(base - float(share), 0.0)

    @pl.when(jnp.max(z_scr[...]) > 0.0)
    def _():
        step = min(keys, 256)
        r, n = iota((step, step), 0), iota((step, step), 1)
        earlier = jnp.where((r // planes == n // planes) & (n < r), 1.0, 0.0).astype(BF16)
        for at in range(0, keys, step):
            part = slice(at, at + step)
            z_scr[part, :] = mm(earlier, z_scr[part, :].astype(BF16))
        place = iota((spare, lanes), 0)
        for c in range(chunks):
            row, cols = slice(c, c + 1), slice(c * lanes, (c + 1) * lanes)
            hit = key_row == key[row, :]
            first = jnp.sum(jnp.where(hit, z_scr[...], 0.0), axis=0, keepdims=True)
            rank = k_scr[row, :]
            slot = jnp.where(rank < share, -1, rank - share + first.astype(jnp.int32))
            b_scr[:spare, cols] = jnp.where(place == slot, 1.0, 0.0).astype(BF16)
        out = mm_nt(a_scr[...], b_scr[:spare, :])
        r = [out[k * blocks : (k + 1) * blocks] for k in range(5)]
        send[:, 0, main:total] = r[0] + r[1]
        send[:, 0, total + main :] = r[2] * 256.0 + r[3] + r[4] * float(area)


def joule_into(got, joule, r_scr, k_scr):
    planes, rows, columns = joule.shape
    sources, total = got.shape[0], got.shape[1] // 2
    spare = r_scr.shape[1] // sources
    main = total - spare
    share = main // planes
    lanes = 128
    per = lanes // share
    each = sources // per
    lane = iota((each, lanes), 1) // share
    row = iota((rows, lanes), 0).astype(F32).astype(BF16)
    column = iota((columns, lanes), 0).astype(F32).astype(BF16)
    one, none = jnp.ones((rows, lanes), BF16), jnp.zeros((rows, lanes), BF16)
    blank = jnp.zeros((columns, lanes), BF16)

    def gathered(values, h):
        out = values[:each]
        for g in range(per):
            part = values[g * each : (g + 1) * each]
            by = (g - h) * share % lanes
            part = pltpu.roll(part, by, 1) if by else part
            out = part if g == 0 else jnp.where(lane == g, part, out)
        return out

    for z in range(planes):
        at = z * share // lanes * lanes
        power = gathered(got[:, at : at + lanes], z % per)
        cell = gathered(got[:, total + at : total + at + lanes], z % per).astype(jnp.int32)
        high, low = split(power)
        high, low = high.astype(F32), low.astype(F32)
        x = (cell // columns).astype(F32)
        y = (cell % columns).astype(F32)
        lefts, rights = [], []
        for s in range(each):
            part = slice(s, s + 1)
            lefts.append(jnp.where(row == x[part, :].astype(BF16), one, none))
            hit = column == y[part, :].astype(BF16)
            rights.append(
                jnp.concatenate(
                    [
                        jnp.where(hit, high[part, :].astype(BF16), blank),
                        jnp.where(hit, low[part, :].astype(BF16), blank),
                    ],
                    axis=0,
                )
            )
        sums = mm_nt(jnp.concatenate(lefts, axis=1), jnp.concatenate(rights, axis=1))
        joule[z] = sums[:, :columns] + sums[:, columns:]

    @pl.when(jnp.max(got[:, main:total]) > 0.0)
    def _():
        column = iota((columns, spare), 0)
        for s in range(sources):
            power = got[s : s + 1, main:total]
            cell = got[s : s + 1, total + main :].astype(jnp.int32)
            part = slice(s * spare, (s + 1) * spare)
            high, low = split(power)
            hit = column == cell % columns
            r_scr[:columns, part] = jnp.where(hit, high.astype(F32), 0.0).astype(BF16)
            r_scr[columns:, part] = jnp.where(hit, low.astype(F32), 0.0).astype(BF16)
            k_scr[:, part] = jnp.broadcast_to(cell // columns, (8, spare))
        width = sources * spare
        step = 2048 if width % 2048 == 0 else width
        row = iota((rows, step), 0)

        def plane(z, carry):
            sums = jnp.zeros((rows, 2 * columns), F32)
            for at in range(0, width, step):
                hit = row == k_scr[0:1, at : at + step] - z * rows
                onehot = jnp.where(hit, 1.0, 0.0).astype(BF16)
                sums = sums + mm_nt(onehot, r_scr[:, at : at + step])
            joule[z] += sums[:, :columns] + sums[:, columns:]
            return carry

        lax.fori_loop(0, planes, plane, 0)


def line_parts(position, theta, start, cells):
    growing, falling = jnp.exp(position * theta), jnp.exp(-position * theta)
    lower = growing + falling * jnp.exp(-(2.0 * start + 1.0) * theta)
    upper = falling + growing * jnp.exp(-(2.0 * (cells - start) - 1.0) * theta)
    return lower, upper


def line(conduct, cells):
    lead = HEAT_SPREADING * STIFF * conduct
    t = 0.5 / jnp.sqrt(lead)
    theta = 2.0 * jnp.log1p(t + t * t / (1.0 + jnp.sqrt(1.0 + t * t)))
    scale = 1.0 / (jnp.sqrt(4.0 * lead + 1.0) * (1.0 - jnp.exp(-2.0 * cells * theta)))
    return theta, scale


def coefficients(sizes, idx, sheet, table, gx_ref, gy_ref, co, z_scr):
    planes, rows, columns, nx, ny, nz = sizes
    lanes = 128
    extent = rows + EXTRA
    lx, ax, by, dx, dxl, dy, cg, phz, psz, mz, wz = groups_of(
        sizes, co, "lx", "ax", "by", "dx", "dxl", "dy", "cg", "phz", "psz", "mz", "wz"
    )
    gx, gy, gz = idx[0], idx[1], idx[2]
    x0, xn = (gx * rows).astype(F32), float(nx * rows)
    y0, yn = (gy * columns).astype(F32), float(ny * columns)

    def wide(array, width):
        return jnp.concatenate([array] * (width // lanes), axis=1)

    def rows_of(first):
        value = jnp.ones((planes, lanes), F32)
        for z in range(planes):
            one = table[sheet[first + z]]
            value = jnp.where(iota((planes, lanes), 0) == z, one, value)
        return value

    lane_z = iota((8, lanes), 1) % planes
    lane_e = iota((8, lanes), 1) // planes
    by_lane = jnp.ones((8, lanes), F32)
    own = []
    for z in range(planes):
        value = table[sheet[gz * planes + z]]
        own.append(value)
        by_lane = jnp.where(lane_z == z, value, by_lane)
    theta_lane, scale_lane = line(by_lane, yn)
    theta_rows, _ = line(rows_of(gz * planes), 1.0)
    for k in range(nx):
        dx[k] = jnp.exp(-float(k * rows) * theta_rows)
        dxl[k] = jnp.exp(-float(k * rows) * theta_lane)
    for k in range(ny):
        dy[k] = jnp.exp(-float(k * columns) * theta_rows)

    for part in range(nz):
        conduct = rows_of(part * planes)
        theta, scale = line(conduct, xn)
        low, high = line_parts(
            iota((planes, rows), 1).astype(F32), wide(theta, rows), x0, xn
        )
        both = jnp.concatenate([high * wide(scale, rows), low * wide(scale, rows)], axis=0)
        for half in range(rows // lanes):
            ax[part * (rows // lanes) + half] = both[:, half * lanes : (half + 1) * lanes]
        theta, scale = line(conduct, yn)
        low, high = line_parts(iota((planes, columns), 1).astype(F32), theta, y0, yn)
        by[part] = jnp.concatenate([high * scale, low * scale], axis=0)

    minus, plus = jnp.full((8, lanes), -1.0, F32), jnp.full((8, lanes), float(columns), F32)
    low_b, high_b = line_parts(minus, theta_lane, y0, yn)
    low_t, high_t = line_parts(plus, theta_lane, y0, yn)
    r, n = iota((lanes, lanes), 0), iota((lanes, lanes), 1)
    same = r % planes == n % planes
    kind = jnp.where(same, (r // planes) * 4 + n // planes, -1)
    cg[0] = jnp.where(
        kind == 8, (high_b * scale_lane)[0:1, :],
        jnp.where(
            kind == 9, (high_t * scale_lane)[0:1, :],
            jnp.where(
                kind == 12, (low_b * scale_lane)[0:1, :],
                jnp.where(kind == 13, (low_t * scale_lane)[0:1, :], 0.0),
            ),
        ),
    )

    order = iota((extent, lanes), 0)
    index = jnp.where(order == rows, -1, jnp.where(order == rows + 1, rows, order))
    position = index.astype(F32)
    real = order < rows + 2
    index_w, order_w = wide(index, rows), wide(order, rows)
    at_or_past = index_w >= iota((extent, rows), 1)
    lane = iota((extent, lanes), 1)
    packed = jnp.zeros((extent, lanes), F32)
    y_col = iota((columns, columns), 0).astype(F32)
    y_i, y_j = iota((columns, columns), 0), iota((columns, columns), 1)
    y_past = y_j >= y_i
    for z in range(planes):
        theta, k_x = line(jnp.full((8, lanes), own[z], F32), xn)
        theta1, k1 = theta[0:1, :], k_x[0:1, :]
        low_c, high_c = line_parts(position, theta1, x0, xn)
        low_c = jnp.where(real, low_c * k1, 0.0)
        high_c = jnp.where(real, high_c * k1, 0.0)
        packed = jnp.where(lane == z, high_c, jnp.where(lane == planes + z, low_c, packed))
        low_r, high_r = line_parts(
            iota((8, rows), 1).astype(F32), wide(theta, rows), x0, xn
        )
        low_r, high_r = low_r[0:1, :], high_r[0:1, :]
        g = jnp.where(at_or_past, wide(high_c, rows) * low_r, wide(low_c, rows) * high_r)
        g = jnp.where(order_w == rows + 2, low_r, jnp.where(order_w == rows + 3, high_r, g))
        gx_ref[z, :extent, :], gx_ref[z, extent:, :] = split(g)

        theta, k_y = line(jnp.full((8, lanes), own[z], F32), yn)
        theta1, k1 = theta[0:1, :], k_y[0:1, :]
        low_r, high_r = line_parts(iota((8, columns), 1).astype(F32), theta, y0, yn)
        low_r, high_r = low_r[0:1, :], high_r[0:1, :]
        low_c, high_c = line_parts(y_col, theta1, y0, yn)
        low_b, _ = line_parts(minus[0:1, :], theta1, y0, yn)
        _, high_t = line_parts(plus[0:1, :], theta1, y0, yn)
        g = k1 * jnp.where(y_past, high_r * low_c, low_r * high_c)
        ext = jnp.zeros((columns, lanes), F32)
        for e, values in enumerate((low_b * high_c * k1, high_t * low_c * k1, low_c, high_c)):
            ext = jnp.where(y_j == e * planes + z, values, ext)
        gy_ref[z, :, :lanes], gy_ref[planes + z, :, :lanes] = split(g)
        gy_ref[z, :, lanes:], gy_ref[planes + z, :, lanes:] = split(ext)
    lx[0] = packed

    total = planes * nz
    cond = [jnp.full((8, lanes), table[sheet[z]], F32) for z in range(total)]
    lead = [HEAT_SPREADING * STIFF * 0.5 * (cond[z] + cond[z + 1]) for z in range(total - 1)]
    lower = [jnp.ones((8, lanes), F32)]
    flux = HEAT_SPREADING * STIFF * cond[0]
    resist = [1.0 / value for value in lead]
    for z in range(total - 1):
        flux = flux + lower[z]
        lower.append(lower[z] + flux * resist[z])
    weight = 1.0 / (flux + lower[total - 1])
    upper = [None] * total
    upper[total - 1] = weight
    flux = jnp.zeros((8, lanes), F32)
    for z in range(total - 2, -1, -1):
        flux = flux + upper[z + 1]
        upper[z] = upper[z + 1] + flux * resist[z]
    zero = jnp.zeros((8, lanes), F32)
    z_scr[0], z_scr[total + 3] = zero, zero
    z_scr[total + 1], z_scr[total + 2] = zero, zero
    for z in range(total):
        z_scr[1 + z] = lower[z]
        z_scr[total + 3 + z] = upper[z]
    z_scr[2 * total + 3] = zero
    mine = gz * planes
    for z in range(planes + 2):
        phz[z] = z_scr[mine + z]
        psz[z] = jnp.where(mine + z == 0, zero, z_scr[total + 2 + mine + z])

    low_lane, high_lane = zero, zero
    for z in range(planes):
        low_lane = jnp.where(lane_z == z, phz[z + 1], low_lane)
        high_lane = jnp.where(lane_z == z, psz[z + 1], high_lane)
    row_p, lane_p = iota((planes, lanes), 0), iota((planes, lanes), 1)
    low_rows, high_rows = jnp.zeros((planes, lanes), F32), jnp.zeros((planes, lanes), F32)
    for z in range(planes):
        low_rows = jnp.where(row_p == z, phz[z + 1][0:1, :], low_rows)
        high_rows = jnp.where(row_p == z, psz[z + 1][0:1, :], high_rows)
    blocks, ends = [], []
    for e in range(2):
        g = jnp.where(
            lane_p % planes >= row_p,
            low_rows * high_lane[0:1, :],
            high_rows * low_lane[0:1, :],
        )
        blocks.append(jnp.where(lane_p // planes == e, g, 0.0))
        ends.append(
            jnp.where(lane_p == e, low_rows, jnp.where(lane_p == 2 + e, high_rows, 0.0))
        )
    rest = jnp.zeros((lanes - 2 * planes, lanes), F32)
    mz[0] = jnp.concatenate(blocks + [rest], axis=0)
    mz[1] = jnp.concatenate(ends + [rest], axis=0)
    row8 = iota((8, lanes), 0)
    wz[0] = jnp.where(
        (row8 < 2) & (lane_e == row8),
        high_lane,
        jnp.where((row8 >= 2) & (row8 < 4) & (lane_e == row8 - 2), low_lane, 0.0),
    )


def slopes(
    counts, idx, sheet, table, scaling, u_ref, kind_ref, xr0, xr1, yr0, yr1, zr0, zr1,
    ux, uy, uz, kx0, kx1, ky0, ky1, kz,
):
    planes, rows, columns = u_ref.shape
    even = [idx[d] % 2 == 0 for d in range(3)]
    at_low = [idx[d] == 0 for d in range(3)]
    at_high = [idx[d] == counts[d] - 1 for d in range(3)]
    row, lane = iota((rows, columns), 0), iota((rows, columns), 1)

    def ends(first, second, d):
        return jnp.where(even[d], second, first), jnp.where(even[d], first, second)

    low, high = ends(xr0[0], xr1[0], 0)
    ux[...] = jnp.zeros(ux.shape, F32)
    for z in range(planes):
        ux[z, 0:1, :] = low[z : z + 1, :]
        ux[z, 1:2, :] = high[z : z + 1, :]
    x_low, x_high = ends(xr0[1], xr1[1], 0)
    low, high = ends(yr0[...], yr1[...], 1)
    kind = iota((rows, 128), 1) // planes
    uy[...] = jnp.zeros(uy.shape, F32)
    uy[:rows, :] = jnp.where(
        kind == 0, low, jnp.where(kind == 1, pltpu.roll(high, planes, 1), 0.0)
    )
    low, high = ends(zr0[0], zr1[0], 2)
    uz[0] = jnp.where(at_low[2], 0.0, low)
    uz[1] = high
    z_low, z_high = ends(zr0[1], zr1[1], 2)
    half = 0.5 * HEAT_SPREADING
    y_low, y_high = ends(yr0[...], yr1[...], 1)
    c_before = None
    for z in range(planes):
        c = conductance(z, idx, sheet, table, scaling, kind_ref)
        first = jnp.where(at_low[0], -c[0:1, :], x_low[z : z + 1, :])
        final = jnp.where(at_high[0], -c[rows - 1 :, :], x_high[z : z + 1, :])
        kx0[z] = half * (c + jnp.where(row == 0, first, pltpu.roll(c, 1, 0)))
        kx1[z] = half * (c + jnp.where(row == rows - 1, final, pltpu.roll(c, rows - 1, 0)))
        first = jnp.where(at_low[1], -c, pltpu.roll(y_low, columns - planes - z, 1))
        final = jnp.where(at_high[1], -c, pltpu.roll(y_high, columns - 1 - planes - z, 1))
        ky0[z] = half * (c + jnp.where(lane == 0, first, pltpu.roll(c, 1, 1)))
        ky1[z] = half * (c + jnp.where(lane == columns - 1, final, pltpu.roll(c, columns - 1, 1)))
        if z == 0:
            kz[z] = half * (c + jnp.where(at_low[2], c, z_low))
        else:
            kz[z] = half * (c + c_before)
        c_before = c
        if z == planes - 1:
            kz[planes] = half * jnp.where(at_high[2], 0.0, c + z_high)


def outflow(z, u_ref, ux, uy, uz, kx0, kx1, ky0, ky1, kz):
    planes, rows, columns = u_ref.shape
    u = u_ref[z]
    row, lane = iota((rows, columns), 0), iota((rows, columns), 1)
    edge = uy[:rows, :]
    edge_low = pltpu.roll(edge, columns - z, 1) if z else edge
    edge_high = pltpu.roll(edge, columns - 1 - planes - z, 1)
    below = uz[0] if z == 0 else u_ref[z - 1]
    above = uz[1] if z == planes - 1 else u_ref[z + 1]
    total = kx0[z] * (jnp.where(row == 0, ux[z, 0:1, :], pltpu.roll(u, 1, 0)) - u)
    total += kx1[z] * (
        jnp.where(row == rows - 1, ux[z, 1:2, :], pltpu.roll(u, rows - 1, 0)) - u
    )
    total += ky0[z] * (jnp.where(lane == 0, edge_low, pltpu.roll(u, 1, 1)) - u)
    total += ky1[z] * (
        jnp.where(lane == columns - 1, edge_high, pltpu.roll(u, columns - 1, 1)) - u
    )
    return total + kz[z] * (below - u) + kz[z + 1] * (above - u)


def advance(idx, source_of, gx_ref, gy_ref, phz, psz, t_ref, e_ref, z_send, x_sends):
    planes, extent, columns = t_ref.shape
    rows = extent - EXTRA
    sums = jnp.zeros((extent, 128), F32)
    below, above = jnp.zeros((rows, columns), F32), jnp.zeros((rows, columns), F32)
    for z in range(planes):
        high, low = split(source_of(z))
        out = mm(gx_ref[z], jnp.concatenate([high, low], axis=1))
        t = out[:extent, :columns] + (out[:extent, columns:] + out[extent:, :columns])
        high, low = split(t)
        twice = jnp.concatenate([gy_ref[z], gy_ref[z]], axis=0)
        out = mm(jnp.concatenate([high, low], axis=1), twice) + mm(high, gy_ref[planes + z])
        t_ref[z] = out[:, :columns]
        sums += out[:, columns:]
        main = out[:rows, :columns]
        below += phz[z + 1][0:1, :] * main
        above += psz[z + 1][0:1, :] * main
    e_ref[...] = sums
    for b, send in enumerate(x_sends):
        take = jnp.where((idx[0] >> b) % 2 == 0, 0, 1)
        for z in range(planes):
            pair = t_ref[z, rows + 2 : rows + 4, :]
            send[z : z + 1, :] = jnp.where(take == 0, pair[0:1], pair[1:2])
        pair = sums[rows + 2 : rows + 4, :]
        send[planes:, :] = jnp.broadcast_to(
            jnp.where(take == 0, pair[0:1], pair[1:2]), (8, 128)
        )
    z_send[0], z_send[1] = below, above


def start_kernel(sizes, idx, sheet, table, scaling, xr0, xr1, yr0, yr1,
                 got_in, u_in, kind_in, zr0_in, zr1_in, gx_ref, gy_ref, co, ux, uy, uz, kx0, kx1, ky0, ky1, kz,
                 joule, t_ref, e_ref, *rest):
    sends, scratch = rest[:-9], rest[-9:]
    r_scr, k_scr, z_scr, got, u_ref, kind_ref, zr0, zr1, sems = scratch
    started = copies(
        [
            (got_in.at[:, 0, :], got), (u_in, u_ref), (kind_in, kind_ref),
            (zr0_in, zr0), (zr1_in, zr1),
        ],
        sems,
    )
    for copy in started:
        copy.start()
    phz, psz = groups_of(sizes, co, "phz", "psz")
    coefficients(sizes, idx, sheet, table, gx_ref, gy_ref, co, z_scr)
    started[0].wait()
    joule_into(got, joule, r_scr, k_scr)
    for copy in started[1:]:
        copy.wait()
    slopes(
        sizes[3:], idx, sheet, table, scaling, u_ref, kind_ref, xr0, xr1, yr0, yr1, zr0, zr1,
        ux, uy, uz, kx0, kx1, ky0, ky1, kz,
    )

    def source_of(z):
        out = outflow(z, u_ref, ux, uy, uz, kx0, kx1, ky0, ky1, kz)
        return out + OHMIC_POWER * ((1.0 + WARMING_SLOPE * u_ref[z]) * joule[z])

    advance(
        idx, source_of, gx_ref, gy_ref, phz, psz, t_ref, e_ref, sends[0], sends[1:]
    )


def x_kernel(sizes, idx, e_ref, co, pair, near, *rest):
    planes, nx = sizes[0], sizes[3]
    gots, (e_out, f_out, send), far = rest[: nx - 1], rest[nx - 1 : nx + 2], rest[nx + 2 :]
    for out in far:
        out[...] = jnp.where((idx[2] >> 1) % 2 == 0, pair[0] + near[0], pair[1] + near[1])
    dx, dxl, lx = groups_of(sizes, co, "dx", "dxl", "lx")
    me = idx[0]
    sums = [[jnp.zeros((planes, 128), F32), jnp.zeros((8, 128), F32)] for _ in range(2)]
    for k, got in zip(range(1, nx), gots):
        other = partner(me, k, nx)
        far = jnp.abs(me - other)
        pair = got[:planes, :] * dx[far], got[planes:, :] * dxl[far]
        for side, keep in ((0, other < me), (1, other > me)):
            for part in range(2):
                sums[side][part] += jnp.where(keep, pair[part], 0.0)
    f_out[:planes, :], f_out[planes:, :] = sums[0][0], sums[1][0]
    row, lane = iota((planes, 128), 0), iota((planes, 128), 1)
    own = lane % planes == row
    ext = jnp.concatenate(
        [jnp.where(own, sums[0][1][0:1, :], 0.0), jnp.where(own, sums[1][1][0:1, :], 0.0)],
        axis=0,
    )
    e = e_ref[...] + stacked(lx[0][:, : 2 * planes], ext)
    e_out[...] = e
    send[...] = e.T[2 * planes : 4 * planes]


def four(rows):
    return jnp.concatenate([rows] * 4, axis=0)


def weights(ref, planes):
    row = iota((planes, 128), 0)
    values = jnp.zeros((planes, 128), F32)
    for z in range(planes):
        values = jnp.where(row == z, ref[z + 1][0:1, :], values)
    return values


def y_kernel(sizes, final, idx, t_ref, e_ref, f_ref, co, *rest):
    ny = sizes[4]
    dy, lx, by, cg, phz, psz, mz = groups_of(
        sizes, co, "dy", "lx", "by", "cg", "phz", "psz", "mz"
    )
    gots, rest = rest[: ny - 1], rest[ny - 1 :]
    l_ref, b_ref = rest[:2]
    sends, q_ref = (rest[2:], None) if final else (rest[3:], rest[2])
    planes, extent, columns = t_ref.shape
    rows = extent - EXTRA
    me = idx[1]
    row = iota((2 * planes, extent), 0)
    across = jnp.zeros((2 * planes, extent), F32)
    for k, got in zip(range(1, ny), gots):
        other = partner(me, k, ny)
        far = jnp.concatenate([dy[jnp.abs(me - other)][:, 0:1]] * 2, axis=0)
        keep = (row < planes) == (other < me)
        across += jnp.where(keep, got[...] * far, 0.0)
    others = jnp.concatenate(
        [
            jnp.zeros((2 * planes, extent), F32),
            across,
            jnp.zeros((128 - 4 * planes, extent), F32),
        ],
        axis=0,
    ).T
    left = lx[0] + others
    l_ref[...] = left
    right = jnp.concatenate([f_ref[...], by[idx[2]]], axis=0)
    b_ref[...] = right
    low, high = weights(phz, planes), weights(psz, planes)
    if final:
        edge, g_low, g_high = jnp.zeros((8, rows), F32), 0.0, 0.0
    else:
        lane = iota((extent, 128), 1)
        q = jnp.where(lane < 2 * planes, e_ref[...], 0.0) + stacked(others, cg[0])
        q_ref[...] = q
        edge = stacked(q[:rows], mz[1]).T
        ghost = slice(rows, rows + 8)
        both = jnp.concatenate([right * four(low), right * four(high)], axis=1)
        ghosts = stacked(left[ghost, : 4 * planes], both)
        g_low, g_high = ghosts[:, :128], ghosts[:, 128:]
        for z in range(planes):
            value = t_ref[z, ghost, :]
            g_low += phz[z + 1][0:1, :] * value
            g_high += psz[z + 1][0:1, :] * value
    for b, send in enumerate(sends):
        lower = (idx[2] >> b) % 2 == 0
        scale = jnp.where(lower, low, high)
        twice = jnp.concatenate([scale] * 2, axis=0)
        send[:8, :] = jnp.broadcast_to(jnp.where(lower, g_low, g_high), (8, 128))
        send[8 : 8 + 2 * planes, :] = f_ref[...] * twice
        at = 8 + 2 * planes
        for part in range(rows // 128):
            cols = slice(part * 128, (part + 1) * 128)
            send[at : at + 8, :] = edge[0:8, cols]
            send[at + 8 : at + 8 + 2 * planes, :] = across[:, cols] * twice
            at += 8 + 2 * planes


def carried(nz, idx, bigs, smalls, ax, by, rows, ghosts):
    me = idx[2]
    planes = by.each // 2
    at_top = me % 2 == 1
    below = jnp.where(at_top, bigs[0][0], 0.0)
    above = jnp.where(at_top, 0.0, bigs[0][1])
    for b, big in enumerate(bigs[1:], 1):
        at_top = (me >> b) % 2 == 1
        below += jnp.where(at_top, big[...], 0.0)
        above += jnp.where(at_top, 0.0, big[...])
    g_below = g_above = edges = 0.0
    lefts, rights = [], []
    sub = iota((8, rows), 0)
    for k, small in zip(range(1, nz), smalls):
        other = partner(me, k, nz)
        lower = other < me

        at, stride = 8 + 2 * planes, 8 + 2 * planes
        parts = [at + p * stride for p in range(rows // 128)]
        across = jnp.concatenate([small[p + 8 : p + stride, :] for p in parts], axis=1)
        halves = rows // 128
        near = [ax[other * halves + half] for half in range(halves)]
        lefts += [jnp.concatenate(near, axis=1), across]
        right = jnp.concatenate([small[8:at, :], by[other]], axis=0)
        rights.append(
            jnp.concatenate(
                [jnp.where(lower, right, 0.0), jnp.where(lower, 0.0, right)], axis=1
            )
        )
        if ghosts:
            g_below += jnp.where(lower, small[:8, :], 0.0)
            g_above += jnp.where(lower, 0.0, small[:8, :])
            value = jnp.concatenate([small[p : p + 8, :] for p in parts], axis=1)
            edges += jnp.where(sub // 2 == jnp.where(lower, 0, 1), value, 0.0)
    more = exact(
        jnp.concatenate(lefts, axis=0), jnp.concatenate(rights, axis=0), ((0,), (0,))
    )
    below, above = below + more[:, :128], above + more[:, 128:]
    return below, above, g_below, g_above, edges


def whole_planes(t_ref, l_ref, b_ref, second, extent):
    planes, _, columns = t_ref.shape
    high, low = split(l_ref[:extent, : 4 * planes])
    left = jnp.concatenate([high, low, high], axis=1)
    right = b_ref[...]
    row = iota(right.shape, 0) % planes
    for z in range(0, planes, 2):
        own = [jnp.where(row == z + k, right, 0.0) for k in range(2)]
        r_high, r_low = split(jnp.concatenate(own, axis=1))
        out = mm(left, jnp.concatenate([r_high, r_high, r_low], axis=0))
        for k in range(2):
            second[z + k] = t_ref[z + k, :extent, :] + out[:, k * columns : (k + 1) * columns]


def change(outside, second, phz, psz, below, above, emit):
    planes = second.shape[0]
    tails = [above]
    for z in range(planes - 1, -1, -1):
        tails.append(tails[-1] + psz[z + 1][0:1, :] * second[z])
    tails = tails[::-1]
    if outside:
        emit(-1, psz[0][0:1, :] * below + phz[0][0:1, :] * tails[0])
    head = below
    for z in range(planes):
        head = head + phz[z + 1][0:1, :] * second[z]
        emit(z, psz[z + 1][0:1, :] * head + phz[z + 1][0:1, :] * tails[z + 1])
    if outside:
        emit(planes, psz[planes + 1][0:1, :] * head + phz[planes + 1][0:1, :] * above)


def rise_kernel(sizes, idx, t_in, l_ref, b_ref, q_ref, co,
                u_ref, ux, uy, uz, kx0, kx1, ky0, ky1, kz, joule, gx_ref, gy_ref, *rest):
    nz = sizes[5]
    phz, psz, mz, wz, ax, by = groups_of(sizes, co, "phz", "psz", "mz", "wz", "ax", "by")
    deep = (nz - 1).bit_length()
    bigs, smalls, rest = rest[:deep], rest[deep : deep + nz - 1], rest[deep + nz - 1 :]
    u_out, ux_out, uy_out, uz_out, t_ref, e_ref = rest[:6]
    sends, second = rest[6:-1], rest[-1]
    planes, rows, columns = u_ref.shape
    whole_planes(t_in, l_ref, b_ref, second, rows + 8)
    below, above, g_below, g_above, edges = carried(nz, idx, bigs, smalls, ax, by, rows, True)

    def emit(z, value):
        if z == -1:
            uz_out[0] = uz[0] + value[:rows]
        elif z == planes:
            uz_out[1] = uz[1] + value[:rows]
        else:
            u_out[z] = u_ref[z] + value[:rows]
            ux_out[z] = ux[z] + value[rows:]

    change(
        True, second, phz, psz,
        jnp.concatenate([below, g_below], axis=0),
        jnp.concatenate([above, g_above], axis=0),
        emit,
    )
    grown = stacked(q_ref[:rows, :], mz[0]) + exact(edges, wz[0], ((0,), (0,)))
    uy_out[...] = uy[...]
    uy_out[:rows, :] = uy[:rows, :] + grown

    def source_of(z):
        out = outflow(z, u_out, ux_out, uy_out, uz_out, kx0, kx1, ky0, ky1, kz)
        return out + OHMIC_POWER * ((1.0 + WARMING_SLOPE * u_out[z]) * joule[z])

    advance(
        idx, source_of, gx_ref, gy_ref, phz, psz, t_ref, e_ref, sends[0], sends[1:]
    )


def finish_kernel(sizes, idx, t_in, l_ref, b_ref, co, u_ref, joule, *rest):
    nz = sizes[5]
    phz, psz, ax, by = groups_of(sizes, co, "phz", "psz", "ax", "by")
    deep = (nz - 1).bit_length()
    bigs, smalls, rest = rest[:deep], rest[deep : deep + nz - 1], rest[deep + nz - 1 :]
    u_out, heat_out, u_scr, heat_scr, second, sems = rest
    rows = u_ref.shape[1]
    started = []
    whole_planes(t_in, l_ref, b_ref, second, rows)
    below, above, _, _, _ = carried(nz, idx, bigs, smalls, ax, by, rows, False)

    def emit(z, value):
        u = u_ref[z] + value
        u_scr[z] = u
        heat_scr[z] = (1.0 + WARMING_SLOPE * u) * joule[z]
        for k, (src, dst) in enumerate(((u_scr, u_out), (heat_scr, heat_out))):
            started.append(pltpu.make_async_copy(src.at[z], dst.at[z], sems.at[k, z]))
            started[-1].start()

    change(False, second, phz, psz, below, above, emit)
    for copy in started:
        copy.wait()


def per_device(
    starting_warmth,
    sheet_stratum_number,
    stratum_heat_conduction,
    substance_kind,
    substance_kind_scaling,
    wire_piece_amperes,
    wire_piece_ohms_base,
    wire_piece_tile,
    wire_piece_voxel,
):
    planes, rows, columns = starting_warmth.shape
    counts = tuple(lax.axis_size(axis) for axis in ("gx", "gy", "gz"))
    nx, ny, nz = counts
    bits = [(n - 1).bit_length() for n in counts]
    devices = nx * ny * nz
    extent = rows + EXTRA
    idx = jnp.stack([lax.axis_index(axis) for axis in ("gx", "gy", "gz")]).astype(jnp.int32)
    block = shaped(planes, rows, columns)
    tables = sheet_stratum_number, stratum_heat_conduction, substance_kind_scaling

    count = wire_piece_amperes.shape[0]
    capacity = 2 * count // devices
    lanes = 128
    chunks = count // lanes
    segments = tuple(
        part.reshape(chunks, lanes)
        for part in (
            wire_piece_amperes, wire_piece_ohms_base, wire_piece_tile, wire_piece_voxel
        )
    )
    share, spare = shares(capacity)
    slots = planes * share + spare
    send, xs0, xs1, ys0, ys1, zs0, zs1 = call(
        functools.partial(first_kernel, devices, planes, rows * columns, capacity),
        [shaped(devices, 1, 2 * slots)]
        + [shaped(2, planes, columns)] * 2
        + [shaped(rows, 128)] * 2
        + [shaped(2, rows, columns)] * 2,
        (idx, *tables, *segments, starting_warmth, substance_kind),
        smem=4,
        far=6,
        vmem=60,
        scratch=[pltpu.VMEM((chunks, lanes), part.dtype) for part in segments]
        + [
            pltpu.VMEM((5 * devices, count), BF16),
            pltpu.VMEM((max(planes * share, spare), count), BF16),
            pltpu.VMEM((devices * planes, lanes), F32),
            pltpu.VMEM((chunks, lanes), jnp.int32),
            pltpu.VMEM(block.shape, F32),
            pltpu.VMEM(block.shape, jnp.int32),
            pltpu.SemaphoreType.DMA((4,)),
            pltpu.SemaphoreType.DMA((2, planes)),
        ],
    )
    got = lax.all_to_all(send, ("gx", "gy", "gz"), split_axis=0, concat_axis=0, tiled=True)

    zr = next_pairs(zs0, zs1, "gz")
    xr = next_pairs(xs0, xs1, "gx")
    yr = next_pairs(ys0, ys1, "gy")
    sizes = (planes, rows, columns, nx, ny, nz)
    parts = [
        shaped(planes, 2 * extent, rows, dtype=BF16),
        shaped(2 * planes, columns, 256, dtype=BF16),
        shaped(table_rows(*sizes)[1], lanes),
    ]
    step_out = [shaped(planes, extent, columns), shaped(extent, 128)]
    step_out += [shaped(2, rows, columns)] + [shaped(planes + 8, columns)] * bits[0]
    total = devices * spare
    ghosts = [shaped(planes, 8, columns), shaped(extent, 128), shaped(2, rows, columns)]
    gx_m, gy_m, co, ux, uy, uz, *rest = call(
        functools.partial(start_kernel, sizes),
        parts + ghosts + [block] * 4 + [shaped(planes + 1, rows, columns), block] + step_out,
        (idx, *tables, *xr, *yr, got, starting_warmth, substance_kind, *zr),
        smem=4,
        far=5,
        vmem=36,
        scratch=[
            pltpu.VMEM((2 * columns, total), BF16),
            pltpu.VMEM((8, total), jnp.int32),
            pltpu.VMEM((2 * planes * nz + 4, 8, lanes), F32),
            pltpu.VMEM((devices, 2 * slots), F32),
            pltpu.VMEM(block.shape, F32),
            pltpu.VMEM(block.shape, jnp.int32),
            pltpu.VMEM((2, rows, columns), F32),
            pltpu.VMEM((2, rows, columns), F32),
            pltpu.SemaphoreType.DMA((5,)),
        ],
    )
    conduct, (joule, t, e, *sends) = rest[:5], rest[5:]
    u = starting_warmth
    small = shaped(8 + 2 * planes + (8 + 2 * planes) * (rows // 128), 128)
    for repeat in range(STEPS):
        pair, *sends = sends
        gots = all_pairs(sends, "gx")
        near = crossed(pair, 1, "gz")
        e, f, send, *far = call(
            functools.partial(x_kernel, sizes),
            [shaped(extent, 128), shaped(2 * planes, columns), shaped(2 * planes, extent)]
            + [shaped(rows, columns)] * (bits[2] - 1),
            (idx, e, co, pair, near, *gots),
            smem=1,
        )
        bigs = [near] + [crossed(array, 2, "gz") for array in far]
        gots = all_pairs([send] * bits[1], "gy")
        final = repeat == STEPS - 1
        q = [] if final else [shaped(extent, 128)]
        left, right, *sends = call(
            functools.partial(y_kernel, sizes, final),
            [shaped(extent, 128), shaped(4 * planes, columns)] + q + [small] * bits[2],
            (idx, t, e, f, co, *gots),
            smem=1,
        )
        if final:
            smalls = all_pairs(sends, "gz")
        else:
            q, *sends = sends
            smalls = all_pairs(sends, "gz")
            u, ux, uy, uz, t, e, *sends = call(
                functools.partial(rise_kernel, sizes),
                [block, shaped(planes, 8, columns), shaped(extent, 128)]
                + [shaped(2, rows, columns)]
                + step_out,
                (idx, t, left, right, q, co, u, ux, uy, uz, *conduct)
                + (joule, gx_m, gy_m, *bigs, *smalls),
                smem=1,
                scratch=[pltpu.VMEM((planes, rows + 8, columns), F32)],
            )
    return tuple(
        call(
            functools.partial(finish_kernel, sizes),
            [block, block],
            (idx, t, left, right, co, u, joule, *bigs, *smalls),
            smem=1,
            scratch=[pltpu.VMEM((planes, rows, columns), F32)] * 3
            + [pltpu.SemaphoreType.DMA((2, planes))],
            far_out=True,
        )
    )


def solution(mesh):
    return jax.shard_map(
        per_device,
        mesh=mesh,
        in_specs=(
            P("gz", "gx", "gy"),
            P(),
            P(),
            P("gz", "gx", "gy"),
            P(),
            P(("gx", "gy", "gz")),
            P(("gx", "gy", "gz")),
            P(("gx", "gy", "gz"), None),
            P(("gx", "gy", "gz")),
        ),
        out_specs=(P("gz", "gx", "gy"), P("gz", "gx", "gy")),
        check_vma=False,
    )
```

```python
import functools

import jax
import jax.numpy as jnp
from jax import lax
from jax.experimental import pallas as pl
from jax.experimental.pallas import tpu as pltpu
from jax.sharding import PartitionSpec as P

STEPS = 2
HEAT_SPREADING = 1000.0
STIFF = 1.5
WARMING_SLOPE = 0.1
OHMIC_POWER = 8.0

F32 = jnp.float32
BF16 = jnp.bfloat16
EXTRA = 16
EXACT = lax.Precision.HIGHEST


def call(kernel, out_shapes, args, scratch=(), vmem=24, far=0, far_out=False):
    specs = [pl.BlockSpec(memory_space=pltpu.VMEM)] * (len(args) - far)
    specs += [pl.BlockSpec(memory_space=pl.ANY)] * far
    return pl.pallas_call(
        kernel,
        out_shape=out_shapes,
        in_specs=specs,
        out_specs=[pl.BlockSpec(memory_space=pl.ANY if far_out else pltpu.VMEM)]
        * len(out_shapes),
        scratch_shapes=list(scratch),
        compiler_params=pltpu.CompilerParams(vmem_limit_bytes=vmem * 2**20),
        cost_estimate=pl.CostEstimate(flops=0, bytes_accessed=1, transcendentals=0),
    )(*args)


def shaped(*shape, dtype=F32):
    return jax.ShapeDtypeStruct(shape, dtype)


def split(x):
    high = x.astype(BF16)
    return high, (x - high.astype(F32)).astype(BF16)


def iota(shape, dim):
    return lax.broadcasted_iota(jnp.int32, shape, dim)


def place():
    return [lax.axis_index(axis) for axis in ("gx", "gy", "gz")]


def copies(pairs, sems):
    return [
        pltpu.make_async_copy(src, dst, sems.at[k]) for k, (src, dst) in enumerate(pairs)
    ]


def plane_copies(pairs, sems):
    started = [
        [
            pltpu.make_async_copy(src.at[z], dst.at[z], sems.at[k, z])
            for z in range(dst.shape[0])
        ]
        for k, (src, dst) in enumerate(pairs)
    ]
    for copies_of_plane in zip(*started):
        for copy in copies_of_plane:
            copy.start()
    return started


def mm(a, b):
    return jnp.dot(a, b, preferred_element_type=F32)


def exact(a, b, dims=((1,), (0,))):
    return lax.dot_general(a, b, (dims, ((), ())), precision=EXACT, preferred_element_type=F32)


def stacked(a, b):
    (a_high, a_low), (b_high, b_low) = split(a), split(b)
    return mm(
        jnp.concatenate([a_high, a_low, a_high], axis=1),
        jnp.concatenate([b_high, b_high, b_low], axis=0),
    )


def mm_nt(a, b):
    return lax.dot_general(a, b, (((1,), (1,)), ((), ())), preferred_element_type=F32)


def table_rows(planes, rows, columns, nx, ny, nz, classes):
    at, places = 0, {}
    for name, items, each in (
        ("lx", 1, rows + EXTRA),
        ("ax", nz * (rows // 128), 2 * planes),
        ("by", nz, 2 * planes),
        ("dx", nx, planes),
        ("dxl", nx, 8),
        ("dy", ny, planes),
        ("cg", 1, 128),
        ("phz", planes + 2, 8),
        ("psz", planes + 2, 8),
        ("mz", 2, 128),
        ("wz", 1, 8),
        ("cond", planes, 8),
        ("kinds", classes, 8),
    ):
        places[name] = (at, each)
        at += items * each
    return places, at


class Group:
    def __init__(self, ref, place):
        self.ref, (self.at, self.each) = ref, place

    def rows(self, k):
        at = self.at + k * self.each
        return pl.ds(at if isinstance(at, int) else pl.multiple_of(at, 8), self.each)

    def __getitem__(self, k):
        return self.ref[self.rows(k), :]

    def __setitem__(self, k, value):
        self.ref[self.rows(k), :] = value


def groups_of(sizes, ref, *names):
    places, _ = table_rows(*sizes)
    return [Group(ref, places[name]) for name in names]


def partner(me, k, n):
    return me ^ k


def groups(n):
    return [k.bit_length() - 1 for k in range(1, n)]


def all_pairs(arrays, axis):
    n = lax.axis_size(axis)
    return [
        lax.ppermute(arrays[b], axis, [(i, i ^ k) for i in range(n)])
        for k, b in zip(range(1, n), groups(n))
    ]


def crossed(array, k, axis):
    return lax.ppermute(array, axis, [(i, i ^ k) for i in range(lax.axis_size(axis))])


def next_pairs(even, odd, axis):
    n = lax.axis_size(axis)
    first = lax.ppermute(even, axis, [(i, i ^ 1) for i in range(n)])
    if n == 2:
        return first, first
    pairs = [(i, i + 1) for i in range(1, n - 1, 2)]
    return first, lax.ppermute(odd, axis, pairs + [(b, a) for a, b in pairs])


def conductance(kind, own, scales):
    factor = jnp.zeros(kind.shape, F32)
    for category, scale in enumerate(scales):
        factor = jnp.where(kind == category, scale, factor)
    return own * factor


def faces(
    idx, sheet, table, scaling, u_ref, kind_ref, started, xs0, xs1, ys0, ys1, zs0, zs1
):
    planes, rows, columns = u_ref.shape
    own = [table[sheet[idx[2] * planes + z]] for z in range(planes)]
    scales = [scaling[category] for category in range(scaling.shape[0])]
    even = [idx[d] % 2 == 0 for d in range(3)]
    lane = iota((rows, columns), 1)
    low = jnp.zeros((rows, columns), F32)
    high = jnp.zeros((rows, columns), F32)
    for z in range(planes):
        started[0][z].wait()
        started[1][z].wait()
        u, c = u_ref[z], conductance(kind_ref[z], own[z], scales)
        if z == 0:
            zs0[1], zs1[1] = c, c
        elif z == planes - 1:
            zs0[1] = jnp.where(even[2], c, zs0[1])
            zs1[1] = jnp.where(even[2], zs1[1], c)
        for slot, values in ((0, u), (1, c)):
            at = slot * planes + z
            low = jnp.where(lane == at, pltpu.roll(values, at, 1) if at else values, low)
            high = jnp.where(lane == at, pltpu.roll(values, at + 1, 1), high)
            first, last = values[0:1, :], values[rows - 1 : rows, :]
            xs0[slot, z : z + 1, :] = jnp.where(even[0], last, first)
            xs1[slot, z : z + 1, :] = jnp.where(even[0], first, last)
    ys0[...] = jnp.where(even[1], high, low)
    ys1[...] = jnp.where(even[1], low, high)
    zs0[0] = jnp.where(even[2], u_ref[planes - 1], u_ref[0])
    zs1[0] = jnp.where(even[2], u_ref[0], u_ref[planes - 1])


def shares(capacity):
    return capacity // 4, capacity - capacity // 4


def first_kernel(blocks, planes, area, capacity,
                 sheet_in, table_in, scaling_in, amps_in, ohms_in, tile_in, cell_in,
                 u_in, kind_in,
                 send, xs0, xs1, ys0, ys1, zs0, zs1,
                 amps, ohms, tiles, cells, a_scr, b_scr, z_scr, k_scr, u_ref, kind_ref,
                 sheet, table, scaling, sems, plane_sems):
    started = copies(
        [
            (amps_in, amps), (ohms_in, ohms), (tile_in, tiles), (cell_in, cells),
            (sheet_in, sheet), (table_in, table), (scaling_in, scaling),
        ],
        sems,
    )
    for copy in started:
        copy.start()
    loads = plane_copies([(u_in, u_ref), (kind_in, kind_ref)], plane_sems)
    for copy in started:
        copy.wait()
    dispatch(
        blocks, planes, area, capacity, amps, ohms, tiles, cells, send,
        a_scr, b_scr, z_scr, k_scr,
    )
    faces(
        place(), sheet, table, scaling, u_ref, kind_ref, loads, xs0, xs1, ys0, ys1, zs0, zs1
    )


def dispatch(blocks, planes, area, capacity, amps, ohms, tiles, cells, send,
             a_scr, b_scr, z_scr, k_scr):
    chunks, lanes = amps.shape
    share, spare = shares(capacity)
    keys, main = blocks * planes, planes * share
    power = amps[...] * amps[...] * ohms[...]
    tile, cell = tiles[...], cells[...]
    plane, within = cell // area, cell % area
    key = tile * planes + plane
    p_high, p_low = split(power)
    pieces = [
        p_high.astype(F32),
        p_low.astype(F32),
        (within >> 8).astype(F32),
        (within & 255).astype(F32),
        plane.astype(F32),
    ]
    key_row, block_row = iota((keys, lanes), 0), iota((blocks, lanes), 0)
    place = iota((main, lanes), 0)
    pair = 2 * lanes
    ahead = jnp.where(iota((pair, pair), 0) < iota((pair, pair), 1), 1.0, 0.0).astype(BF16)
    base = jnp.zeros((keys, lanes), F32)
    for c in range(0, chunks, 2):
        hits = [key_row == key[c + k : c + k + 1, :] for k in range(2)]
        ones = [jnp.where(hit, 1.0, 0.0) for hit in hits]
        counted = mm(jnp.concatenate(ones, axis=1).astype(BF16), ahead)
        for k in range(2):
            row, cols = slice(c + k, c + k + 1), slice((c + k) * lanes, (c + k + 1) * lanes)
            order = counted[:, k * lanes : (k + 1) * lanes] + base
            rank = jnp.sum(jnp.where(hits[k], order, 0.0), axis=0, keepdims=True)
            rank = rank.astype(jnp.int32)
            k_scr[row, :] = rank
            slot = jnp.where(rank < share, plane[row, :] * share + rank, -1)
            b_scr[:main, cols] = jnp.where(place == slot, 1.0, 0.0).astype(BF16)
            hit = block_row == tile[row, :]
            for n, piece in enumerate(pieces):
                a_scr[n * blocks : (n + 1) * blocks, cols] = jnp.where(
                    hit, piece[row, :], 0.0
                ).astype(BF16)
        base = base + (counted[:, pair - 1 :] + ones[1][:, lanes - 1 :])
    out = mm_nt(a_scr[: 4 * blocks, :], b_scr[:main, :])
    r = [out[k * blocks : (k + 1) * blocks] for k in range(4)]
    total = main + spare
    send[:, 0, :main] = r[0] + r[1]
    send[:, 0, total : total + main] = r[2] * 256.0 + r[3]
    send[:, 0, main:total] = jnp.zeros((blocks, spare), F32)
    send[:, 0, total + main :] = jnp.zeros((blocks, spare), F32)
    z_scr[...] = jnp.maximum(base - float(share), 0.0)

    @pl.when(jnp.max(z_scr[...]) > 0.0)
    def _():
        step = min(keys, 256)
        r, n = iota((step, step), 0), iota((step, step), 1)
        earlier = jnp.where((r // planes == n // planes) & (n < r), 1.0, 0.0).astype(BF16)
        for at in range(0, keys, step):
            part = slice(at, at + step)
            z_scr[part, :] = mm(earlier, z_scr[part, :].astype(BF16))
        place = iota((spare, lanes), 0)
        for c in range(chunks):
            row, cols = slice(c, c + 1), slice(c * lanes, (c + 1) * lanes)
            hit = key_row == key[row, :]
            first = jnp.sum(jnp.where(hit, z_scr[...], 0.0), axis=0, keepdims=True)
            rank = k_scr[row, :]
            slot = jnp.where(rank < share, -1, rank - share + first.astype(jnp.int32))
            b_scr[:spare, cols] = jnp.where(place == slot, 1.0, 0.0).astype(BF16)
        out = mm_nt(a_scr[...], b_scr[:spare, :])
        r = [out[k * blocks : (k + 1) * blocks] for k in range(5)]
        send[:, 0, main:total] = r[0] + r[1]
        send[:, 0, total + main :] = r[2] * 256.0 + r[3] + r[4] * float(area)


def joule_into(got, joule, r_scr, k_scr):
    planes, rows, columns = joule.shape
    sources, total = got.shape[0], got.shape[1] // 2
    spare = r_scr.shape[1] // sources
    main = total - spare
    share = main // planes
    lanes = 128
    per = lanes // share
    each = sources // per
    lane = iota((each, lanes), 1) // share
    row = iota((rows, lanes), 0).astype(F32).astype(BF16)
    column = iota((columns, lanes), 0).astype(F32).astype(BF16)
    one, none = jnp.ones((rows, lanes), BF16), jnp.zeros((rows, lanes), BF16)
    blank = jnp.zeros((columns, lanes), BF16)

    def gathered(values, h):
        out = values[:each]
        for g in range(per):
            part = values[g * each : (g + 1) * each]
            by = (g - h) * share % lanes
            part = pltpu.roll(part, by, 1) if by else part
            out = part if g == 0 else jnp.where(lane == g, part, out)
        return out

    for z in range(planes):
        at = z * share // lanes * lanes
        power = gathered(got[:, at : at + lanes], z % per)
        cell = gathered(got[:, total + at : total + at + lanes], z % per).astype(jnp.int32)
        high, low = split(power)
        high, low = high.astype(F32), low.astype(F32)
        x = (cell // columns).astype(F32)
        y = (cell % columns).astype(F32)
        lefts, rights = [], []
        for s in range(each):
            part = slice(s, s + 1)
            lefts.append(jnp.where(row == x[part, :].astype(BF16), one, none))
            hit = column == y[part, :].astype(BF16)
            rights.append(
                jnp.concatenate(
                    [
                        jnp.where(hit, high[part, :].astype(BF16), blank),
                        jnp.where(hit, low[part, :].astype(BF16), blank),
                    ],
                    axis=0,
                )
            )
        sums = mm_nt(jnp.concatenate(lefts, axis=1), jnp.concatenate(rights, axis=1))
        joule[z] = sums[:, :columns] + sums[:, columns:]

    @pl.when(jnp.max(got[:, main:total]) > 0.0)
    def _():
        column = iota((columns, spare), 0)
        for s in range(sources):
            power = got[s : s + 1, main:total]
            cell = got[s : s + 1, total + main :].astype(jnp.int32)
            part = slice(s * spare, (s + 1) * spare)
            high, low = split(power)
            hit = column == cell % columns
            r_scr[:columns, part] = jnp.where(hit, high.astype(F32), 0.0).astype(BF16)
            r_scr[columns:, part] = jnp.where(hit, low.astype(F32), 0.0).astype(BF16)
            k_scr[:, part] = jnp.broadcast_to(cell // columns, (8, spare))
        width = sources * spare
        step = 2048 if width % 2048 == 0 else width
        row = iota((rows, step), 0)

        def plane(z, carry):
            sums = jnp.zeros((rows, 2 * columns), F32)
            for at in range(0, width, step):
                hit = row == k_scr[0:1, at : at + step] - z * rows
                onehot = jnp.where(hit, 1.0, 0.0).astype(BF16)
                sums = sums + mm_nt(onehot, r_scr[:, at : at + step])
            joule[z] += sums[:, :columns] + sums[:, columns:]
            return carry

        lax.fori_loop(0, planes, plane, 0)


def line_parts(position, theta, start, cells):
    growing, falling = jnp.exp(position * theta), jnp.exp(-position * theta)
    lower = growing + falling * jnp.exp(-(2.0 * start + 1.0) * theta)
    upper = falling + growing * jnp.exp(-(2.0 * (cells - start) - 1.0) * theta)
    return lower, upper


def line(conduct, cells):
    lead = HEAT_SPREADING * STIFF * conduct
    t = 0.5 / jnp.sqrt(lead)
    theta = 2.0 * jnp.log1p(t + t * t / (1.0 + jnp.sqrt(1.0 + t * t)))
    scale = 1.0 / (jnp.sqrt(4.0 * lead + 1.0) * (1.0 - jnp.exp(-2.0 * cells * theta)))
    return theta, scale


def coefficients(sizes, idx, sheet, table, scaling, gx_ref, gy_ref, co, z_scr):
    planes, rows, columns, nx, ny, nz, classes = sizes
    lanes = 128
    extent = rows + EXTRA
    lx, ax, by, dx, dxl, dy, cg, phz, psz, mz, wz, cond_rows, kind_rows = groups_of(
        sizes, co, "lx", "ax", "by", "dx", "dxl", "dy", "cg", "phz", "psz", "mz", "wz",
        "cond", "kinds",
    )
    for category in range(classes):
        kind_rows[category] = jnp.full((8, lanes), scaling[category], F32)
    gx, gy, gz = idx[0], idx[1], idx[2]
    x0, xn = (gx * rows).astype(F32), float(nx * rows)
    y0, yn = (gy * columns).astype(F32), float(ny * columns)

    def wide(array, width):
        return jnp.concatenate([array] * (width // lanes), axis=1)

    def rows_of(first):
        value = jnp.ones((planes, lanes), F32)
        for z in range(planes):
            one = table[sheet[first + z]]
            value = jnp.where(iota((planes, lanes), 0) == z, one, value)
        return value

    lane_z = iota((8, lanes), 1) % planes
    lane_e = iota((8, lanes), 1) // planes
    by_lane = jnp.ones((8, lanes), F32)
    own = []
    for z in range(planes):
        value = table[sheet[gz * planes + z]]
        own.append(value)
        cond_rows[z] = jnp.full((8, lanes), value, F32)
        by_lane = jnp.where(lane_z == z, value, by_lane)
    theta_lane, scale_lane = line(by_lane, yn)
    theta_rows, _ = line(rows_of(gz * planes), 1.0)
    for k in range(nx):
        dx[k] = jnp.exp(-float(k * rows) * theta_rows)
        dxl[k] = jnp.exp(-float(k * rows) * theta_lane)
    for k in range(ny):
        dy[k] = jnp.exp(-float(k * columns) * theta_rows)

    for part in range(nz):
        conduct = rows_of(part * planes)
        theta, scale = line(conduct, xn)
        low, high = line_parts(
            iota((planes, rows), 1).astype(F32), wide(theta, rows), x0, xn
        )
        both = jnp.concatenate([high * wide(scale, rows), low * wide(scale, rows)], axis=0)
        for half in range(rows // lanes):
            ax[part * (rows // lanes) + half] = both[:, half * lanes : (half + 1) * lanes]
        theta, scale = line(conduct, yn)
        low, high = line_parts(iota((planes, columns), 1).astype(F32), theta, y0, yn)
        by[part] = jnp.concatenate([high * scale, low * scale], axis=0)

    minus, plus = jnp.full((8, lanes), -1.0, F32), jnp.full((8, lanes), float(columns), F32)
    low_b, high_b = line_parts(minus, theta_lane, y0, yn)
    low_t, high_t = line_parts(plus, theta_lane, y0, yn)
    r, n = iota((lanes, lanes), 0), iota((lanes, lanes), 1)
    same = r % planes == n % planes
    kind = jnp.where(same, (r // planes) * 4 + n // planes, -1)
    cg[0] = jnp.where(
        kind == 8, (high_b * scale_lane)[0:1, :],
        jnp.where(
            kind == 9, (high_t * scale_lane)[0:1, :],
            jnp.where(
                kind == 12, (low_b * scale_lane)[0:1, :],
                jnp.where(kind == 13, (low_t * scale_lane)[0:1, :], 0.0),
            ),
        ),
    )

    order = iota((extent, lanes), 0)
    index = jnp.where(order == rows, -1, jnp.where(order == rows + 1, rows, order))
    position = index.astype(F32)
    real = order < rows + 2
    index_w, order_w = wide(index, rows), wide(order, rows)
    at_or_past = index_w >= iota((extent, rows), 1)
    lane = iota((extent, lanes), 1)
    packed = jnp.zeros((extent, lanes), F32)
    y_col = iota((columns, columns), 0).astype(F32)
    y_i, y_j = iota((columns, columns), 0), iota((columns, columns), 1)
    y_past = y_j >= y_i
    for z in range(planes):
        theta, k_x = line(jnp.full((8, lanes), own[z], F32), xn)
        theta1, k1 = theta[0:1, :], k_x[0:1, :]
        low_c, high_c = line_parts(position, theta1, x0, xn)
        low_c = jnp.where(real, low_c * k1, 0.0)
        high_c = jnp.where(real, high_c * k1, 0.0)
        packed = jnp.where(lane == z, high_c, jnp.where(lane == planes + z, low_c, packed))
        low_r, high_r = line_parts(
            iota((8, rows), 1).astype(F32), wide(theta, rows), x0, xn
        )
        low_r, high_r = low_r[0:1, :], high_r[0:1, :]
        g = jnp.where(at_or_past, wide(high_c, rows) * low_r, wide(low_c, rows) * high_r)
        g = jnp.where(order_w == rows + 2, low_r, jnp.where(order_w == rows + 3, high_r, g))
        gx_ref[z, :extent, :], gx_ref[z, extent:, :] = split(g)

        theta, k_y = line(jnp.full((8, lanes), own[z], F32), yn)
        theta1, k1 = theta[0:1, :], k_y[0:1, :]
        low_r, high_r = line_parts(iota((8, columns), 1).astype(F32), theta, y0, yn)
        low_r, high_r = low_r[0:1, :], high_r[0:1, :]
        low_c, high_c = line_parts(y_col, theta1, y0, yn)
        low_b, _ = line_parts(minus[0:1, :], theta1, y0, yn)
        _, high_t = line_parts(plus[0:1, :], theta1, y0, yn)
        g = k1 * jnp.where(y_past, high_r * low_c, low_r * high_c)
        ext = jnp.zeros((columns, lanes), F32)
        for e, values in enumerate((low_b * high_c * k1, high_t * low_c * k1, low_c, high_c)):
            ext = jnp.where(y_j == e * planes + z, values, ext)
        gy_ref[z, :, :lanes], gy_ref[planes + z, :, :lanes] = split(g)
        gy_ref[z, :, lanes:], gy_ref[planes + z, :, lanes:] = split(ext)
    lx[0] = packed

    total = planes * nz
    cond = [jnp.full((8, lanes), table[sheet[z]], F32) for z in range(total)]
    lead = [HEAT_SPREADING * STIFF * 0.5 * (cond[z] + cond[z + 1]) for z in range(total - 1)]
    lower = [jnp.ones((8, lanes), F32)]
    flux = HEAT_SPREADING * STIFF * cond[0]
    resist = [1.0 / value for value in lead]
    for z in range(total - 1):
        flux = flux + lower[z]
        lower.append(lower[z] + flux * resist[z])
    weight = 1.0 / (flux + lower[total - 1])
    upper = [None] * total
    upper[total - 1] = weight
    flux = jnp.zeros((8, lanes), F32)
    for z in range(total - 2, -1, -1):
        flux = flux + upper[z + 1]
        upper[z] = upper[z + 1] + flux * resist[z]
    zero = jnp.zeros((8, lanes), F32)
    z_scr[0], z_scr[total + 3] = zero, zero
    z_scr[total + 1], z_scr[total + 2] = zero, zero
    for z in range(total):
        z_scr[1 + z] = lower[z]
        z_scr[total + 3 + z] = upper[z]
    z_scr[2 * total + 3] = zero
    mine = gz * planes
    for z in range(planes + 2):
        phz[z] = z_scr[mine + z]
        psz[z] = jnp.where(mine + z == 0, zero, z_scr[total + 2 + mine + z])

    low_lane, high_lane = zero, zero
    for z in range(planes):
        low_lane = jnp.where(lane_z == z, phz[z + 1], low_lane)
        high_lane = jnp.where(lane_z == z, psz[z + 1], high_lane)
    row_p, lane_p = iota((planes, lanes), 0), iota((planes, lanes), 1)
    low_rows, high_rows = jnp.zeros((planes, lanes), F32), jnp.zeros((planes, lanes), F32)
    for z in range(planes):
        low_rows = jnp.where(row_p == z, phz[z + 1][0:1, :], low_rows)
        high_rows = jnp.where(row_p == z, psz[z + 1][0:1, :], high_rows)
    blocks, ends = [], []
    for e in range(2):
        g = jnp.where(
            lane_p % planes >= row_p,
            low_rows * high_lane[0:1, :],
            high_rows * low_lane[0:1, :],
        )
        blocks.append(jnp.where(lane_p // planes == e, g, 0.0))
        ends.append(
            jnp.where(lane_p == e, low_rows, jnp.where(lane_p == 2 + e, high_rows, 0.0))
        )
    rest = jnp.zeros((lanes - 2 * planes, lanes), F32)
    mz[0] = jnp.concatenate(blocks + [rest], axis=0)
    mz[1] = jnp.concatenate(ends + [rest], axis=0)
    row8 = iota((8, lanes), 0)
    wz[0] = jnp.where(
        (row8 < 2) & (lane_e == row8),
        high_lane,
        jnp.where((row8 >= 2) & (row8 < 4) & (lane_e == row8 - 2), low_lane, 0.0),
    )


def slopes(
    counts, idx, cond, scales, u_ref, kind_ref, xr0, xr1, yr0, yr1, zr0, zr1,
    ux, uy, uz, kx0, kx1, ky0, ky1, kz,
):
    planes, rows, columns = u_ref.shape
    even = [idx[d] % 2 == 0 for d in range(3)]
    at_low = [idx[d] == 0 for d in range(3)]
    at_high = [idx[d] == counts[d] - 1 for d in range(3)]
    row, lane = iota((rows, columns), 0), iota((rows, columns), 1)

    def ends(first, second, d):
        return jnp.where(even[d], second, first), jnp.where(even[d], first, second)

    low, high = ends(xr0[0], xr1[0], 0)
    ux[...] = jnp.zeros(ux.shape, F32)
    for z in range(planes):
        ux[z, 0:1, :] = low[z : z + 1, :]
        ux[z, 1:2, :] = high[z : z + 1, :]
    x_low, x_high = ends(xr0[1], xr1[1], 0)
    low, high = ends(yr0[...], yr1[...], 1)
    kind = iota((rows, 128), 1) // planes
    uy[...] = jnp.zeros(uy.shape, F32)
    uy[:rows, :] = jnp.where(
        kind == 0, low, jnp.where(kind == 1, pltpu.roll(high, planes, 1), 0.0)
    )
    low, high = ends(zr0[0], zr1[0], 2)
    uz[0] = jnp.where(at_low[2], 0.0, low)
    uz[1] = high
    z_low, z_high = ends(zr0[1], zr1[1], 2)
    half = 0.5 * HEAT_SPREADING
    y_low, y_high = ends(yr0[...], yr1[...], 1)
    c_before = None
    for z in range(planes):
        c = conductance(kind_ref[z], cond[z][0:1, :], scales)
        first = jnp.where(at_low[0], -c[0:1, :], x_low[z : z + 1, :])
        final = jnp.where(at_high[0], -c[rows - 1 :, :], x_high[z : z + 1, :])
        kx0[z] = half * (c + jnp.where(row == 0, first, pltpu.roll(c, 1, 0)))
        kx1[z] = half * (c + jnp.where(row == rows - 1, final, pltpu.roll(c, rows - 1, 0)))
        first = jnp.where(at_low[1], -c, pltpu.roll(y_low, columns - planes - z, 1))
        final = jnp.where(at_high[1], -c, pltpu.roll(y_high, columns - 1 - planes - z, 1))
        ky0[z] = half * (c + jnp.where(lane == 0, first, pltpu.roll(c, 1, 1)))
        ky1[z] = half * (c + jnp.where(lane == columns - 1, final, pltpu.roll(c, columns - 1, 1)))
        if z == 0:
            kz[z] = half * (c + jnp.where(at_low[2], c, z_low))
        else:
            kz[z] = half * (c + c_before)
        c_before = c
        if z == planes - 1:
            kz[planes] = half * jnp.where(at_high[2], 0.0, c + z_high)


def outflow(z, u_ref, ux, uy, uz, kx0, kx1, ky0, ky1, kz):
    planes, rows, columns = u_ref.shape
    u = u_ref[z]
    row, lane = iota((rows, columns), 0), iota((rows, columns), 1)
    edge = uy[:rows, :]
    edge_low = pltpu.roll(edge, columns - z, 1) if z else edge
    edge_high = pltpu.roll(edge, columns - 1 - planes - z, 1)
    below = uz[0] if z == 0 else u_ref[z - 1]
    above = uz[1] if z == planes - 1 else u_ref[z + 1]
    total = kx0[z] * (jnp.where(row == 0, ux[z, 0:1, :], pltpu.roll(u, 1, 0)) - u)
    total += kx1[z] * (
        jnp.where(row == rows - 1, ux[z, 1:2, :], pltpu.roll(u, rows - 1, 0)) - u
    )
    total += ky0[z] * (jnp.where(lane == 0, edge_low, pltpu.roll(u, 1, 1)) - u)
    total += ky1[z] * (
        jnp.where(lane == columns - 1, edge_high, pltpu.roll(u, columns - 1, 1)) - u
    )
    return total + kz[z] * (below - u) + kz[z + 1] * (above - u)


def advance(idx, source_of, gx_ref, gy_ref, phz, psz, t_ref, e_ref, z_send, x_sends):
    planes, extent, columns = t_ref.shape
    rows = extent - EXTRA
    sums = jnp.zeros((extent, 128), F32)
    below, above = jnp.zeros((rows, columns), F32), jnp.zeros((rows, columns), F32)
    for z in range(planes):
        high, low = split(source_of(z))
        out = mm(gx_ref[z], jnp.concatenate([high, low], axis=1))
        t = out[:extent, :columns] + (out[:extent, columns:] + out[extent:, :columns])
        high, low = split(t)
        twice = jnp.concatenate([gy_ref[z], gy_ref[z]], axis=0)
        out = mm(jnp.concatenate([high, low], axis=1), twice) + mm(high, gy_ref[planes + z])
        t_ref[z] = out[:, :columns]
        sums += out[:, columns:]
        main = out[:rows, :columns]
        below += phz[z + 1][0:1, :] * main
        above += psz[z + 1][0:1, :] * main
    e_ref[...] = sums
    for b, send in enumerate(x_sends):
        take = jnp.where((idx[0] >> b) % 2 == 0, 0, 1)
        for z in range(planes):
            pair = t_ref[z, rows + 2 : rows + 4, :]
            send[z : z + 1, :] = jnp.where(take == 0, pair[0:1], pair[1:2])
        pair = sums[rows + 2 : rows + 4, :]
        send[planes:, :] = jnp.broadcast_to(
            jnp.where(take == 0, pair[0:1], pair[1:2]), (8, 128)
        )
    z_send[0], z_send[1] = below, above


def joule_kernel(sizes, sheet_in, table_in, scaling_in, got_in, gx_ref, gy_ref, co, joule,
                 r_scr, k_scr, z_scr, got, sheet, table, scaling, sems):
    started = copies(
        [
            (sheet_in, sheet), (table_in, table), (scaling_in, scaling),
            (got_in.at[:, 0, :], got),
        ],
        sems,
    )
    for copy in started:
        copy.start()
    for copy in started[:3]:
        copy.wait()
    coefficients(sizes, place(), sheet, table, scaling, gx_ref, gy_ref, co, z_scr)
    started[3].wait()
    joule_into(got, joule, r_scr, k_scr)


def start_kernel(sizes, xr0, xr1, yr0, yr1, zr0, zr1,
                 u_ref, kind_ref, gx_ref, gy_ref, co, joule,
                 ux, uy, uz, kx0, kx1, ky0, ky1, kz, t_ref, e_ref, *sends):
    idx = place()
    phz, psz, cond, kinds = groups_of(sizes, co, "phz", "psz", "cond", "kinds")
    scales = [kinds[category][0:1, :] for category in range(sizes[6])]
    slopes(
        sizes[3:], idx, cond, scales, u_ref, kind_ref, xr0, xr1, yr0, yr1, zr0, zr1,
        ux, uy, uz, kx0, kx1, ky0, ky1, kz,
    )

    def source_of(z):
        out = outflow(z, u_ref, ux, uy, uz, kx0, kx1, ky0, ky1, kz)
        return out + OHMIC_POWER * ((1.0 + WARMING_SLOPE * u_ref[z]) * joule[z])

    advance(
        idx, source_of, gx_ref, gy_ref, phz, psz, t_ref, e_ref, sends[0], sends[1:]
    )


def x_kernel(sizes, e_ref, co, pair, near, *rest):
    idx = place()
    planes, nx = sizes[0], sizes[3]
    gots, (e_out, f_out, send), far = rest[: nx - 1], rest[nx - 1 : nx + 2], rest[nx + 2 :]
    for out in far:
        out[...] = jnp.where((idx[2] >> 1) % 2 == 0, pair[0] + near[0], pair[1] + near[1])
    dx, dxl, lx = groups_of(sizes, co, "dx", "dxl", "lx")
    me = idx[0]
    sums = [[jnp.zeros((planes, 128), F32), jnp.zeros((8, 128), F32)] for _ in range(2)]
    for k, got in zip(range(1, nx), gots):
        other = partner(me, k, nx)
        far = jnp.abs(me - other)
        pair = got[:planes, :] * dx[far], got[planes:, :] * dxl[far]
        for side, keep in ((0, other < me), (1, other > me)):
            for part in range(2):
                sums[side][part] += jnp.where(keep, pair[part], 0.0)
    f_out[:planes, :], f_out[planes:, :] = sums[0][0], sums[1][0]
    row, lane = iota((planes, 128), 0), iota((planes, 128), 1)
    own = lane % planes == row
    ext = jnp.concatenate(
        [jnp.where(own, sums[0][1][0:1, :], 0.0), jnp.where(own, sums[1][1][0:1, :], 0.0)],
        axis=0,
    )
    e = e_ref[...] + stacked(lx[0][:, : 2 * planes], ext)
    e_out[...] = e
    send[...] = e.T[2 * planes : 4 * planes]


def four(rows):
    return jnp.concatenate([rows] * 4, axis=0)


def weights(ref, planes):
    row = iota((planes, 128), 0)
    values = jnp.zeros((planes, 128), F32)
    for z in range(planes):
        values = jnp.where(row == z, ref[z + 1][0:1, :], values)
    return values


def y_kernel(sizes, final, t_ref, e_ref, f_ref, co, *rest):
    idx = place()
    ny = sizes[4]
    dy, lx, by, cg, phz, psz, mz = groups_of(
        sizes, co, "dy", "lx", "by", "cg", "phz", "psz", "mz"
    )
    gots, rest = rest[: ny - 1], rest[ny - 1 :]
    l_ref, b_ref = rest[:2]
    sends, q_ref = (rest[2:], None) if final else (rest[3:], rest[2])
    planes, extent, columns = t_ref.shape
    rows = extent - EXTRA
    me = idx[1]
    row = iota((2 * planes, extent), 0)
    across = jnp.zeros((2 * planes, extent), F32)
    for k, got in zip(range(1, ny), gots):
        other = partner(me, k, ny)
        far = jnp.concatenate([dy[jnp.abs(me - other)][:, 0:1]] * 2, axis=0)
        keep = (row < planes) == (other < me)
        across += jnp.where(keep, got[...] * far, 0.0)
    others = jnp.concatenate(
        [
            jnp.zeros((2 * planes, extent), F32),
            across,
            jnp.zeros((128 - 4 * planes, extent), F32),
        ],
        axis=0,
    ).T
    left = lx[0] + others
    l_ref[...] = left
    right = jnp.concatenate([f_ref[...], by[idx[2]]], axis=0)
    b_ref[...] = right
    low, high = weights(phz, planes), weights(psz, planes)
    if not final:
        lane = iota((extent, 128), 1)
        q = jnp.where(lane < 2 * planes, e_ref[...], 0.0) + stacked(others, cg[0])
        q_ref[...] = q
        edge = stacked(q[:rows], mz[1]).T
        ghost = slice(rows, rows + 8)
        both = jnp.concatenate([right * four(low), right * four(high)], axis=1)
        ghosts = stacked(left[ghost, : 4 * planes], both)
        g_low, g_high = ghosts[:, :128], ghosts[:, 128:]
        for z in range(planes):
            value = t_ref[z, ghost, :]
            g_low += phz[z + 1][0:1, :] * value
            g_high += psz[z + 1][0:1, :] * value
    if ny == 2:
        across = jnp.where(me == 1, across[:planes], across[planes:])
    for b, send in enumerate(sends):
        lower = (idx[2] >> b) % 2 == 0
        scale = jnp.where(lower, low, high)
        at = 0
        if not final:
            send[:2, :] = jnp.where(lower, g_low[:2], g_high[:2])
            ends = jnp.where(lower, edge[:2], edge[2:4])
            for part in range(rows // 128):
                send[2 + 2 * part : 4 + 2 * part, :] = ends[:, part * 128 : (part + 1) * 128]
            at = 8
        send[at : at + 2 * planes, :] = f_ref[...] * jnp.concatenate([scale] * 2, axis=0)
        at += 2 * planes
        many = across.shape[0]
        scale = jnp.concatenate([scale] * (many // planes), axis=0)
        for part in range(rows // 128):
            send[at : at + many, :] = across[:, part * 128 : (part + 1) * 128] * scale
            at += many


def carried(nz, idx, bigs, smalls, ax, by, rows, ghosts):
    me = idx[2]
    planes = by.each // 2
    at_top = me % 2 == 1
    below = jnp.where(at_top, bigs[0][0], 0.0)
    above = jnp.where(at_top, 0.0, bigs[0][1])
    for b, big in enumerate(bigs[1:], 1):
        at_top = (me >> b) % 2 == 1
        below += jnp.where(at_top, big[...], 0.0)
        above += jnp.where(at_top, 0.0, big[...])
    g_below = g_above = 0.0
    ends = [0.0, 0.0]
    lefts, rights = [], []
    for k, small in zip(range(1, nz), smalls):
        other = partner(me, k, nz)
        lower = other < me
        at = 0
        halves = rows // 128
        if ghosts:
            g_below += jnp.where(lower, small[:2, :], 0.0)
            g_above += jnp.where(lower, 0.0, small[:2, :])
            value = jnp.concatenate(
                [small[2 + 2 * p : 4 + 2 * p, :] for p in range(halves)], axis=1
            )
            ends[0] += jnp.where(lower, value, 0.0)
            ends[1] += jnp.where(lower, 0.0, value)
            at = 8
        both = at + 2 * planes
        many = (small.shape[0] - both) // halves
        across = [small[both + p * many : both + (p + 1) * many, :] for p in range(halves)]
        near = [ax[other * halves + half] for half in range(halves)]
        lefts += [jnp.concatenate(near, axis=1), jnp.concatenate(across, axis=1)]
        lines = by[other]
        if many == planes:
            lines = jnp.where(idx[1] == 1, lines[:planes], lines[planes:])
        right = jnp.concatenate([small[at:both, :], lines], axis=0)
        rights.append(
            jnp.concatenate(
                [jnp.where(lower, right, 0.0), jnp.where(lower, 0.0, right)], axis=1
            )
        )
    edges = None
    if ghosts:
        edges = jnp.concatenate(ends + [jnp.zeros((4, rows), F32)], axis=0)
        none = jnp.zeros((6, 128), F32)
        g_below = jnp.concatenate([g_below, none], axis=0)
        g_above = jnp.concatenate([g_above, none], axis=0)
    more = exact(
        jnp.concatenate(lefts, axis=0), jnp.concatenate(rights, axis=0), ((0,), (0,))
    )
    below, above = below + more[:, :128], above + more[:, 128:]
    return below, above, g_below, g_above, edges


def whole_planes(t_ref, l_ref, b_ref, second, extent):
    planes, _, columns = t_ref.shape
    high, low = split(l_ref[:extent, : 4 * planes])
    left = jnp.concatenate([high, low, high], axis=1)
    right = b_ref[...]
    row = iota(right.shape, 0) % planes
    for z in range(0, planes, 2):
        own = [jnp.where(row == z + k, right, 0.0) for k in range(2)]
        r_high, r_low = split(jnp.concatenate(own, axis=1))
        out = mm(left, jnp.concatenate([r_high, r_high, r_low], axis=0))
        for k in range(2):
            second[z + k] = t_ref[z + k, :extent, :] + out[:, k * columns : (k + 1) * columns]


def change(outside, second, phz, psz, below, above, emit):
    planes = second.shape[0]
    tails = [above]
    for z in range(planes - 1, -1, -1):
        tails.append(tails[-1] + psz[z + 1][0:1, :] * second[z])
    tails = tails[::-1]
    if outside:
        emit(-1, psz[0][0:1, :] * below + phz[0][0:1, :] * tails[0])
    head = below
    for z in range(planes):
        head = head + phz[z + 1][0:1, :] * second[z]
        emit(z, psz[z + 1][0:1, :] * head + phz[z + 1][0:1, :] * tails[z + 1])
    if outside:
        emit(planes, psz[planes + 1][0:1, :] * head + phz[planes + 1][0:1, :] * above)


def rise_kernel(sizes, t_in, l_ref, b_ref, q_ref, co,
                u_ref, ux, uy, uz, kx0, kx1, ky0, ky1, kz, joule, gx_ref, gy_ref, *rest):
    idx = place()
    nz = sizes[5]
    phz, psz, mz, wz, ax, by = groups_of(sizes, co, "phz", "psz", "mz", "wz", "ax", "by")
    deep = (nz - 1).bit_length()
    bigs, smalls, rest = rest[:deep], rest[deep : deep + nz - 1], rest[deep + nz - 1 :]
    u_out, ux_out, uy_out, uz_out, t_ref, e_ref = rest[:6]
    sends, second = rest[6:-1], rest[-1]
    planes, rows, columns = u_ref.shape
    whole_planes(t_in, l_ref, b_ref, second, rows + 8)
    below, above, g_below, g_above, edges = carried(nz, idx, bigs, smalls, ax, by, rows, True)

    def emit(z, value):
        if z == -1:
            uz_out[0] = uz[0] + value[:rows]
        elif z == planes:
            uz_out[1] = uz[1] + value[:rows]
        else:
            u_out[z] = u_ref[z] + value[:rows]
            ux_out[z] = ux[z] + value[rows:]

    change(
        True, second, phz, psz,
        jnp.concatenate([below, g_below], axis=0),
        jnp.concatenate([above, g_above], axis=0),
        emit,
    )
    grown = stacked(q_ref[:rows, :], mz[0]) + exact(edges, wz[0], ((0,), (0,)))
    uy_out[...] = uy[...]
    uy_out[:rows, :] = uy[:rows, :] + grown

    def source_of(z):
        out = outflow(z, u_out, ux_out, uy_out, uz_out, kx0, kx1, ky0, ky1, kz)
        return out + OHMIC_POWER * ((1.0 + WARMING_SLOPE * u_out[z]) * joule[z])

    advance(
        idx, source_of, gx_ref, gy_ref, phz, psz, t_ref, e_ref, sends[0], sends[1:]
    )


def finish_kernel(sizes, t_in, l_ref, b_ref, co, u_ref, joule, *rest):
    idx = place()
    nz = sizes[5]
    phz, psz, ax, by = groups_of(sizes, co, "phz", "psz", "ax", "by")
    deep = (nz - 1).bit_length()
    bigs, smalls, rest = rest[:deep], rest[deep : deep + nz - 1], rest[deep + nz - 1 :]
    u_out, heat_out, u_scr, heat_scr, second, sems = rest
    rows = u_ref.shape[1]
    started = []
    whole_planes(t_in, l_ref, b_ref, second, rows)
    below, above, _, _, _ = carried(nz, idx, bigs, smalls, ax, by, rows, False)

    def emit(z, value):
        u = u_ref[z] + value
        u_scr[z] = u
        heat_scr[z] = (1.0 + WARMING_SLOPE * u) * joule[z]
        for k, (src, dst) in enumerate(((u_scr, u_out), (heat_scr, heat_out))):
            started.append(pltpu.make_async_copy(src.at[z], dst.at[z], sems.at[k, z]))
            started[-1].start()

    change(False, second, phz, psz, below, above, emit)
    for copy in started:
        copy.wait()


def per_device(
    starting_warmth,
    sheet_stratum_number,
    stratum_heat_conduction,
    substance_kind,
    substance_kind_scaling,
    wire_piece_amperes,
    wire_piece_ohms_base,
    wire_piece_tile,
    wire_piece_voxel,
):
    planes, rows, columns = starting_warmth.shape
    counts = tuple(lax.axis_size(axis) for axis in ("gx", "gy", "gz"))
    nx, ny, nz = counts
    bits = [(n - 1).bit_length() for n in counts]
    devices = nx * ny * nz
    extent = rows + EXTRA
    block = shaped(planes, rows, columns)
    tables = sheet_stratum_number, stratum_heat_conduction, substance_kind_scaling
    scalars = [pltpu.SMEM(part.shape, part.dtype) for part in tables]

    count = wire_piece_amperes.shape[0]
    capacity = 2 * count // devices
    lanes = 128
    chunks = count // lanes
    segments = tuple(
        part.reshape(chunks, lanes)
        for part in (
            wire_piece_amperes, wire_piece_ohms_base, wire_piece_tile, wire_piece_voxel
        )
    )
    share, spare = shares(capacity)
    slots = planes * share + spare
    send, xs0, xs1, ys0, ys1, zs0, zs1 = call(
        functools.partial(first_kernel, devices, planes, rows * columns, capacity),
        [shaped(devices, 1, 2 * slots)]
        + [shaped(2, planes, columns)] * 2
        + [shaped(rows, 128)] * 2
        + [shaped(2, rows, columns)] * 2,
        (*tables, *segments, starting_warmth, substance_kind),
        far=9,
        vmem=60,
        scratch=[pltpu.VMEM((chunks, lanes), part.dtype) for part in segments]
        + [
            pltpu.VMEM((5 * devices, count), BF16),
            pltpu.VMEM((max(planes * share, spare), count), BF16),
            pltpu.VMEM((devices * planes, lanes), F32),
            pltpu.VMEM((chunks, lanes), jnp.int32),
            pltpu.VMEM(block.shape, F32),
            pltpu.VMEM(block.shape, jnp.int32),
            *scalars,
            pltpu.SemaphoreType.DMA((7,)),
            pltpu.SemaphoreType.DMA((2, planes)),
        ],
    )
    got = lax.all_to_all(send, ("gx", "gy", "gz"), split_axis=0, concat_axis=0, tiled=True)

    zr = next_pairs(zs0, zs1, "gz")
    xr = next_pairs(xs0, xs1, "gx")
    yr = next_pairs(ys0, ys1, "gy")
    sizes = (planes, rows, columns, nx, ny, nz, substance_kind_scaling.shape[0])
    parts = [
        shaped(planes, 2 * extent, rows, dtype=BF16),
        shaped(2 * planes, columns, 256, dtype=BF16),
        shaped(table_rows(*sizes)[1], lanes),
    ]
    step_out = [shaped(planes, extent, columns), shaped(extent, 128)]
    step_out += [shaped(2, rows, columns)] + [shaped(planes + 8, columns)] * bits[0]
    total = devices * spare
    ghosts = [shaped(planes, 8, columns), shaped(extent, 128), shaped(2, rows, columns)]
    gx_m, gy_m, co, joule = call(
        functools.partial(joule_kernel, sizes),
        parts + [block],
        (*tables, got),
        far=4,
        vmem=24,
        scratch=[
            pltpu.VMEM((2 * columns, total), BF16),
            pltpu.VMEM((8, total), jnp.int32),
            pltpu.VMEM((2 * planes * nz + 4, 8, lanes), F32),
            pltpu.VMEM((devices, 2 * slots), F32),
            *scalars,
            pltpu.SemaphoreType.DMA((4,)),
        ],
    )
    ux, uy, uz, *rest = call(
        functools.partial(start_kernel, sizes),
        ghosts + [block] * 4 + [shaped(planes + 1, rows, columns)] + step_out,
        (*xr, *yr, *zr, starting_warmth, substance_kind, gx_m, gy_m, co, joule),
    )
    conduct, (t, e, *sends) = rest[:5], rest[5:]
    u = starting_warmth
    lines = planes if ny == 2 else 2 * planes
    small_rows = 2 * planes + lines * (rows // 128)
    for repeat in range(STEPS):
        pair, *sends = sends
        gots = all_pairs(sends, "gx")
        near = crossed(pair, 1, "gz")
        e, f, send, *far = call(
            functools.partial(x_kernel, sizes),
            [shaped(extent, 128), shaped(2 * planes, columns), shaped(2 * planes, extent)]
            + [shaped(rows, columns)] * (bits[2] - 1),
            (e, co, pair, near, *gots),
        )
        bigs = [near] + [crossed(array, 2, "gz") for array in far]
        gots = all_pairs([send] * bits[1], "gy")
        final = repeat == STEPS - 1
        q = [] if final else [shaped(extent, 128)]
        small = shaped(small_rows + (0 if final else 8), 128)
        left, right, *sends = call(
            functools.partial(y_kernel, sizes, final),
            [shaped(extent, 128), shaped(4 * planes, columns)] + q + [small] * bits[2],
            (t, e, f, co, *gots),
        )
        if final:
            smalls = all_pairs(sends, "gz")
        else:
            q, *sends = sends
            smalls = all_pairs(sends, "gz")
            u, ux, uy, uz, t, e, *sends = call(
                functools.partial(rise_kernel, sizes),
                [block, shaped(planes, 8, columns), shaped(extent, 128)]
                + [shaped(2, rows, columns)]
                + step_out,
                (t, left, right, q, co, u, ux, uy, uz, *conduct)
                + (joule, gx_m, gy_m, *bigs, *smalls),
                scratch=[pltpu.VMEM((planes, rows + 8, columns), F32)],
            )
    return tuple(
        call(
            functools.partial(finish_kernel, sizes),
            [block, block],
            (t, left, right, co, u, joule, *bigs, *smalls),
            scratch=[pltpu.VMEM((planes, rows, columns), F32)] * 3
            + [pltpu.SemaphoreType.DMA((2, planes))],
            far_out=True,
        )
    )


def solution(mesh):
    return jax.shard_map(
        per_device,
        mesh=mesh,
        in_specs=(
            P("gz", "gx", "gy"),
            P(),
            P(),
            P("gz", "gx", "gy"),
            P(),
            P(("gx", "gy", "gz")),
            P(("gx", "gy", "gz")),
            P(("gx", "gy", "gz"), None),
            P(("gx", "gy", "gz")),
        ),
        out_specs=(P("gz", "gx", "gy"), P("gz", "gx", "gy")),
        check_vma=False,
    )
```

```python
import functools

import jax
import jax.numpy as jnp
from jax import lax
from jax.experimental import pallas as pl
from jax.experimental.pallas import tpu as pltpu
from jax.sharding import PartitionSpec as P

STEPS = 2
HEAT_SPREADING = 1000.0
STIFF = 1.5
WARMING_SLOPE = 0.1
OHMIC_POWER = 8.0

F32 = jnp.float32
BF16 = jnp.bfloat16
EXTRA = 16


def call(kernel, out_shapes, args, scratch=(), vmem=24, far=0, far_out=False):
    specs = [pl.BlockSpec(memory_space=pltpu.VMEM)] * (len(args) - far)
    specs += [pl.BlockSpec(memory_space=pl.ANY)] * far
    return pl.pallas_call(
        kernel,
        out_shape=out_shapes,
        in_specs=specs,
        out_specs=[pl.BlockSpec(memory_space=pl.ANY if far_out else pltpu.VMEM)]
        * len(out_shapes),
        scratch_shapes=list(scratch),
        compiler_params=pltpu.CompilerParams(vmem_limit_bytes=vmem * 2**20),
        cost_estimate=pl.CostEstimate(flops=0, bytes_accessed=1, transcendentals=0),
    )(*args)


def shaped(*shape, dtype=F32):
    return jax.ShapeDtypeStruct(shape, dtype)


def split(x):
    high = x.astype(BF16)
    return high, (x - high.astype(F32)).astype(BF16)


def iota(shape, dim):
    return lax.broadcasted_iota(jnp.int32, shape, dim)


def place():
    return [lax.axis_index(axis) for axis in ("gx", "gy", "gz")]


def copies(pairs, sems):
    return [
        pltpu.make_async_copy(src, dst, sems.at[k]) for k, (src, dst) in enumerate(pairs)
    ]


def plane_copies(pairs, sems):
    started = [
        [
            pltpu.make_async_copy(src.at[z], dst.at[z], sems.at[k, z])
            for z in range(dst.shape[0])
        ]
        for k, (src, dst) in enumerate(pairs)
    ]
    for copies_of_plane in zip(*started):
        for copy in copies_of_plane:
            copy.start()
    return started


def mm(a, b):
    return jnp.dot(a, b, preferred_element_type=F32)


def stacked(a, b):
    (a_high, a_low), (b_high, b_low) = split(a), split(b)
    return mm(
        jnp.concatenate([a_high, a_low, a_high], axis=1),
        jnp.concatenate([b_high, b_high, b_low], axis=0),
    )


def stacked_rows(a, b):
    more = -a.shape[0] % 16
    if more:
        a = jnp.concatenate([a, jnp.zeros((more, a.shape[1]), F32)], axis=0)
        b = jnp.concatenate([b, jnp.zeros((more, b.shape[1]), F32)], axis=0)
    (a_high, a_low), (b_high, b_low) = split(a), split(b)
    return lax.dot_general(
        jnp.concatenate([a_high, a_low, a_high], axis=0),
        jnp.concatenate([b_high, b_high, b_low], axis=0),
        (((0,), (0,)), ((), ())),
        preferred_element_type=F32,
    )


def mm_nt(a, b):
    return lax.dot_general(a, b, (((1,), (1,)), ((), ())), preferred_element_type=F32)


def table_rows(planes, rows, columns, nx, ny, nz, classes):
    at, places = 0, {}
    for name, items, each in (
        ("lx", 1, rows + EXTRA),
        ("ax", nz * (rows // 128), 2 * planes),
        ("by", nz, 2 * planes),
        ("dx", nx, planes),
        ("dxl", nx, 8),
        ("dy", ny, planes),
        ("cg", 1, 128),
        ("phz", planes + 2, 8),
        ("psz", planes + 2, 8),
        ("mz", 2, 128),
        ("wz", 1, 8),
        ("cond", planes, 8),
        ("kinds", classes, 8),
    ):
        places[name] = (at, each)
        at += items * each
    return places, at


class Group:
    def __init__(self, ref, place):
        self.ref, (self.at, self.each) = ref, place

    def rows(self, k):
        at = self.at + k * self.each
        return pl.ds(at if isinstance(at, int) else pl.multiple_of(at, 8), self.each)

    def __getitem__(self, k):
        return self.ref[self.rows(k), :]

    def __setitem__(self, k, value):
        self.ref[self.rows(k), :] = value


def groups_of(sizes, ref, *names):
    places, _ = table_rows(*sizes)
    return [Group(ref, places[name]) for name in names]


def partner(me, k, n):
    return me ^ k


def groups(n):
    return [k.bit_length() - 1 for k in range(1, n)]


def all_pairs(arrays, axis):
    n = lax.axis_size(axis)
    return [
        lax.ppermute(arrays[b], axis, [(i, i ^ k) for i in range(n)])
        for k, b in zip(range(1, n), groups(n))
    ]


def crossed(array, k, axis):
    return lax.ppermute(array, axis, [(i, i ^ k) for i in range(lax.axis_size(axis))])


def next_pairs(even, odd, axis):
    n = lax.axis_size(axis)
    first = lax.ppermute(even, axis, [(i, i ^ 1) for i in range(n)])
    if n == 2:
        return first, first
    pairs = [(i, i + 1) for i in range(1, n - 1, 2)]
    return first, lax.ppermute(odd, axis, pairs + [(b, a) for a, b in pairs])


def conductance(kind, own, scales):
    factor = jnp.zeros(kind.shape, F32)
    for category, scale in enumerate(scales):
        factor = jnp.where(kind == category, scale, factor)
    return own * factor


def faces(idx, own, scales, u_ref, kind_ref, zc, xs, ys):
    planes, rows, columns = u_ref.shape
    even = [idx[d] % 2 == 0 for d in range(2)]
    lane = iota((rows, columns), 1)
    kept = [jnp.zeros((rows, columns), F32) for _ in range(ys.shape[0])]
    for z in range(planes):
        u = u_ref[z]
        if z in (0, planes - 1):
            c = zc[min(z, 1)]
        else:
            c = conductance(kind_ref[z], own[z], scales)
        for slot, values in ((0, u), (1, c)):
            at = slot * planes + z
            for k in range(len(kept)):
                upper = even[1] if k == 0 else jnp.logical_not(even[1])
                turned = pltpu.roll(values, at + jnp.where(upper, 1, 0), 1)
                kept[k] = jnp.where(lane == at, turned, kept[k])
            first, last = values[0:1, :], values[rows - 1 : rows, :]
            xs[0, slot, z : z + 1, :] = jnp.where(even[0], last, first)
            xs[1, slot, z : z + 1, :] = jnp.where(even[0], first, last)
    for k, value in enumerate(kept):
        ys[k] = value


def shares(capacity):
    return capacity // 4, capacity - capacity // 4


def first_kernel(blocks, planes, area, capacity,
                 sheet_in, table_in, scaling_in, amps_in, ohms_in, tile_in, cell_in,
                 u_in, kind_in,
                 send_out, xs0_out, xs1_out, ys_out, zs0_out, zs1_out,
                 send, xs, ys, zc,
                 amps, ohms, tiles, cells, a_scr, b_scr, z_scr, k_scr, u_ref, kind_ref,
                 sheet, table, scaling, sems, plane_sems, out_sems):
    started = copies(
        [
            (amps_in, amps), (ohms_in, ohms), (tile_in, tiles), (cell_in, cells),
            (sheet_in, sheet), (table_in, table), (scaling_in, scaling),
        ],
        sems,
    )
    for copy in started:
        copy.start()
    loads = plane_copies([(u_in, u_ref), (kind_in, kind_ref)], plane_sems)
    for copy in started:
        copy.wait()
    dispatch(
        blocks, planes, area, capacity, amps, ohms, tiles, cells, send,
        a_scr, b_scr, z_scr, k_scr,
    )
    idx = place()
    even = idx[2] % 2 == 0
    top = u_ref.shape[0] - 1
    own = [table[sheet[idx[2] * planes + z]] for z in range(planes)]
    scales = [scaling[category] for category in range(scaling.shape[0])]
    stores = [(send, send_out)]
    for copies_of_plane in zip(*loads):
        for copy in copies_of_plane:
            copy.wait()
    zc[0] = conductance(kind_ref[0], own[0], scales)
    zc[1] = conductance(kind_ref[top], own[top], scales)
    for out, upper in ((zs0_out, even), (zs1_out, jnp.logical_not(even))):
        stores.append((u_ref.at[jnp.where(upper, top, 0)], out.at[0]))
        stores.append((zc.at[jnp.where(upper, 1, 0)], out.at[1]))
    stored = copies(stores, out_sems)
    for copy in stored:
        copy.start()
    faces(idx, own, scales, u_ref, kind_ref, zc, xs, ys)
    last = [
        pltpu.make_async_copy(src, dst, out_sems.at[len(stores) + k])
        for k, (src, dst) in enumerate(
            ((xs.at[0], xs0_out), (xs.at[1], xs1_out), (ys, ys_out))
        )
    ]
    for copy in last:
        copy.start()
    for copy in stored + last:
        copy.wait()


def dispatch(blocks, planes, area, capacity, amps, ohms, tiles, cells, send,
             a_scr, b_scr, z_scr, k_scr):
    chunks, lanes = amps.shape
    share, spare = shares(capacity)
    keys, main = blocks * planes, planes * share
    power = amps[...] * amps[...] * ohms[...]
    tile, cell = tiles[...], cells[...]
    plane, within = cell // area, cell % area
    key = tile * planes + plane
    p_high, p_low = split(power)
    pieces = [
        p_high.astype(F32),
        p_low.astype(F32),
        (within >> 8).astype(F32),
        (within & 255).astype(F32),
        plane.astype(F32),
    ]
    key_row, block_row = iota((keys, lanes), 0), iota((blocks, lanes), 0)
    place = iota((main, lanes), 0)
    pair = 2 * lanes
    ahead = jnp.where(iota((pair, pair), 0) < iota((pair, pair), 1), 1.0, 0.0).astype(BF16)
    base = jnp.zeros((keys, lanes), F32)
    for c in range(0, chunks, 2):
        hits = [key_row == key[c + k : c + k + 1, :] for k in range(2)]
        ones = [jnp.where(hit, 1.0, 0.0) for hit in hits]
        counted = mm(jnp.concatenate(ones, axis=1).astype(BF16), ahead)
        for k in range(2):
            row, cols = slice(c + k, c + k + 1), slice((c + k) * lanes, (c + k + 1) * lanes)
            order = counted[:, k * lanes : (k + 1) * lanes] + base
            rank = jnp.sum(jnp.where(hits[k], order, 0.0), axis=0, keepdims=True)
            rank = rank.astype(jnp.int32)
            k_scr[row, :] = rank
            slot = jnp.where(rank < share, plane[row, :] * share + rank, -1)
            b_scr[:main, cols] = jnp.where(place == slot, 1.0, 0.0).astype(BF16)
            hit = block_row == tile[row, :]
            for n, piece in enumerate(pieces):
                a_scr[n * blocks : (n + 1) * blocks, cols] = jnp.where(
                    hit, piece[row, :], 0.0
                ).astype(BF16)
        base = base + (counted[:, pair - 1 :] + ones[1][:, lanes - 1 :])
    out = mm_nt(a_scr[: 4 * blocks, :], b_scr[:main, :])
    r = [out[k * blocks : (k + 1) * blocks] for k in range(4)]
    total = main + spare
    send[:, 0, :main] = r[0] + r[1]
    send[:, 0, total : total + main] = r[2] * 256.0 + r[3]
    send[:, 0, main:total] = jnp.zeros((blocks, spare), F32)
    send[:, 0, total + main :] = jnp.zeros((blocks, spare), F32)
    z_scr[...] = jnp.maximum(base - float(share), 0.0)

    @pl.when(jnp.max(z_scr[...]) > 0.0)
    def _():
        step = min(keys, 256)
        r, n = iota((step, step), 0), iota((step, step), 1)
        earlier = jnp.where((r // planes == n // planes) & (n < r), 1.0, 0.0).astype(BF16)
        for at in range(0, keys, step):
            part = slice(at, at + step)
            z_scr[part, :] = mm(earlier, z_scr[part, :].astype(BF16))
        place = iota((spare, lanes), 0)
        for c in range(chunks):
            row, cols = slice(c, c + 1), slice(c * lanes, (c + 1) * lanes)
            hit = key_row == key[row, :]
            first = jnp.sum(jnp.where(hit, z_scr[...], 0.0), axis=0, keepdims=True)
            rank = k_scr[row, :]
            slot = jnp.where(rank < share, -1, rank - share + first.astype(jnp.int32))
            b_scr[:spare, cols] = jnp.where(place == slot, 1.0, 0.0).astype(BF16)
        out = mm_nt(a_scr[...], b_scr[:spare, :])
        r = [out[k * blocks : (k + 1) * blocks] for k in range(5)]
        send[:, 0, main:total] = r[0] + r[1]
        send[:, 0, total + main :] = r[2] * 256.0 + r[3] + r[4] * float(area)


def joule_into(got, joule, r_scr, k_scr):
    planes, rows, columns = joule.shape
    sources, total = got.shape[0], got.shape[1] // 2
    spare = r_scr.shape[1] // sources
    main = total - spare
    share = main // planes
    lanes = 128
    per = lanes // share
    each = sources // per
    lane = iota((each, lanes), 1) // share
    row = iota((rows, lanes), 0).astype(F32).astype(BF16)
    column = iota((columns, lanes), 0).astype(F32).astype(BF16)
    one, none = jnp.ones((rows, lanes), BF16), jnp.zeros((rows, lanes), BF16)
    blank = jnp.zeros((columns, lanes), BF16)

    def gathered(values, h):
        out = values[:each]
        for g in range(per):
            part = values[g * each : (g + 1) * each]
            by = (g - h) * share % lanes
            part = pltpu.roll(part, by, 1) if by else part
            out = part if g == 0 else jnp.where(lane == g, part, out)
        return out

    for z in range(planes):
        at = z * share // lanes * lanes
        power = gathered(got[:, at : at + lanes], z % per)
        cell = gathered(got[:, total + at : total + at + lanes], z % per).astype(jnp.int32)
        high, low = split(power)
        high, low = high.astype(F32), low.astype(F32)
        x = (cell // columns).astype(F32)
        y = (cell % columns).astype(F32)
        lefts, rights = [], []
        for s in range(each):
            part = slice(s, s + 1)
            lefts.append(jnp.where(row == x[part, :].astype(BF16), one, none))
            hit = column == y[part, :].astype(BF16)
            rights.append(
                jnp.concatenate(
                    [
                        jnp.where(hit, high[part, :].astype(BF16), blank),
                        jnp.where(hit, low[part, :].astype(BF16), blank),
                    ],
                    axis=0,
                )
            )
        sums = mm_nt(jnp.concatenate(lefts, axis=1), jnp.concatenate(rights, axis=1))
        joule[z] = sums[:, :columns] + sums[:, columns:]

    @pl.when(jnp.max(got[:, main:total]) > 0.0)
    def _():
        column = iota((columns, spare), 0)
        for s in range(sources):
            power = got[s : s + 1, main:total]
            cell = got[s : s + 1, total + main :].astype(jnp.int32)
            part = slice(s * spare, (s + 1) * spare)
            high, low = split(power)
            hit = column == cell % columns
            r_scr[:columns, part] = jnp.where(hit, high.astype(F32), 0.0).astype(BF16)
            r_scr[columns:, part] = jnp.where(hit, low.astype(F32), 0.0).astype(BF16)
            k_scr[:, part] = jnp.broadcast_to(cell // columns, (8, spare))
        width = sources * spare
        step = 2048 if width % 2048 == 0 else width
        row = iota((rows, step), 0)

        def plane(z, carry):
            sums = jnp.zeros((rows, 2 * columns), F32)
            for at in range(0, width, step):
                hit = row == k_scr[0:1, at : at + step] - z * rows
                onehot = jnp.where(hit, 1.0, 0.0).astype(BF16)
                sums = sums + mm_nt(onehot, r_scr[:, at : at + step])
            joule[z] += sums[:, :columns] + sums[:, columns:]
            return carry

        lax.fori_loop(0, planes, plane, 0)


def line_parts(position, theta, start, cells):
    growing, falling = jnp.exp(position * theta), jnp.exp(-position * theta)
    lower = growing + falling * jnp.exp(-(2.0 * start + 1.0) * theta)
    upper = falling + growing * jnp.exp(-(2.0 * (cells - start) - 1.0) * theta)
    return lower, upper


def line(conduct, cells):
    lead = HEAT_SPREADING * STIFF * conduct
    t = 0.5 / jnp.sqrt(lead)
    theta = 2.0 * jnp.log1p(t + t * t / (1.0 + jnp.sqrt(1.0 + t * t)))
    scale = 1.0 / (jnp.sqrt(4.0 * lead + 1.0) * (1.0 - jnp.exp(-2.0 * cells * theta)))
    return theta, scale


def coefficients(sizes, idx, sheet, table, scaling, gx_ref, gy_ref, co, z_scr):
    planes, rows, columns, nx, ny, nz, classes = sizes
    lanes = 128
    extent = rows + EXTRA
    lx, ax, by, dx, dxl, dy, cg, phz, psz, mz, wz, cond_rows, kind_rows = groups_of(
        sizes, co, "lx", "ax", "by", "dx", "dxl", "dy", "cg", "phz", "psz", "mz", "wz",
        "cond", "kinds",
    )
    for category in range(classes):
        kind_rows[category] = jnp.full((8, lanes), scaling[category], F32)
    gx, gy, gz = idx[0], idx[1], idx[2]
    x0, xn = (gx * rows).astype(F32), float(nx * rows)
    y0, yn = (gy * columns).astype(F32), float(ny * columns)

    def wide(array, width):
        return jnp.concatenate([array] * (width // lanes), axis=1)

    def rows_of(first):
        value = jnp.ones((planes, lanes), F32)
        for z in range(planes):
            one = table[sheet[first + z]]
            value = jnp.where(iota((planes, lanes), 0) == z, one, value)
        return value

    lane_z = iota((8, lanes), 1) % planes
    lane_e = iota((8, lanes), 1) // planes
    by_lane = jnp.ones((8, lanes), F32)
    own = []
    for z in range(planes):
        value = table[sheet[gz * planes + z]]
        own.append(value)
        cond_rows[z] = jnp.full((8, lanes), value, F32)
        by_lane = jnp.where(lane_z == z, value, by_lane)
    theta_lane, scale_lane = line(by_lane, yn)
    theta_rows, _ = line(rows_of(gz * planes), 1.0)
    for k in range(nx):
        dx[k] = jnp.exp(-float(k * rows) * theta_rows)
        dxl[k] = jnp.exp(-float(k * rows) * theta_lane)
    for k in range(ny):
        dy[k] = jnp.exp(-float(k * columns) * theta_rows)

    for part in range(nz):
        conduct = rows_of(part * planes)
        theta, scale = line(conduct, xn)
        low, high = line_parts(
            iota((planes, rows), 1).astype(F32), wide(theta, rows), x0, xn
        )
        both = jnp.concatenate([high * wide(scale, rows), low * wide(scale, rows)], axis=0)
        for half in range(rows // lanes):
            ax[part * (rows // lanes) + half] = both[:, half * lanes : (half + 1) * lanes]
        theta, scale = line(conduct, yn)
        low, high = line_parts(iota((planes, columns), 1).astype(F32), theta, y0, yn)
        by[part] = jnp.concatenate([high * scale, low * scale], axis=0)

    minus, plus = jnp.full((8, lanes), -1.0, F32), jnp.full((8, lanes), float(columns), F32)
    low_b, high_b = line_parts(minus, theta_lane, y0, yn)
    low_t, high_t = line_parts(plus, theta_lane, y0, yn)
    r, n = iota((lanes, lanes), 0), iota((lanes, lanes), 1)
    same = r % planes == n % planes
    kind = jnp.where(same, (r // planes) * 4 + n // planes, -1)
    cg[0] = jnp.where(
        kind == 8, (high_b * scale_lane)[0:1, :],
        jnp.where(
            kind == 9, (high_t * scale_lane)[0:1, :],
            jnp.where(
                kind == 12, (low_b * scale_lane)[0:1, :],
                jnp.where(kind == 13, (low_t * scale_lane)[0:1, :], 0.0),
            ),
        ),
    )

    order = iota((extent, lanes), 0)
    index = jnp.where(order == rows, -1, jnp.where(order == rows + 1, rows, order))
    position = index.astype(F32)
    real = order < rows + 2
    index_w, order_w = wide(index, rows), wide(order, rows)
    at_or_past = index_w >= iota((extent, rows), 1)
    lane = iota((extent, lanes), 1)
    packed = jnp.zeros((extent, lanes), F32)
    y_col = iota((columns, columns), 0).astype(F32)
    y_i, y_j = iota((columns, columns), 0), iota((columns, columns), 1)
    y_past = y_j >= y_i
    for z in range(planes):
        theta, k_x = line(jnp.full((8, lanes), own[z], F32), xn)
        theta1, k1 = theta[0:1, :], k_x[0:1, :]
        low_c, high_c = line_parts(position, theta1, x0, xn)
        low_c = jnp.where(real, low_c * k1, 0.0)
        high_c = jnp.where(real, high_c * k1, 0.0)
        packed = jnp.where(lane == z, high_c, jnp.where(lane == planes + z, low_c, packed))
        low_r, high_r = line_parts(
            iota((8, rows), 1).astype(F32), wide(theta, rows), x0, xn
        )
        low_r, high_r = low_r[0:1, :], high_r[0:1, :]
        g = jnp.where(at_or_past, wide(high_c, rows) * low_r, wide(low_c, rows) * high_r)
        g = jnp.where(order_w == rows + 2, low_r, jnp.where(order_w == rows + 3, high_r, g))
        gx_ref[z, :extent, :], gx_ref[z, extent:, :] = split(g)

        theta, k_y = line(jnp.full((8, lanes), own[z], F32), yn)
        theta1, k1 = theta[0:1, :], k_y[0:1, :]
        low_r, high_r = line_parts(iota((8, columns), 1).astype(F32), theta, y0, yn)
        low_r, high_r = low_r[0:1, :], high_r[0:1, :]
        low_c, high_c = line_parts(y_col, theta1, y0, yn)
        low_b, _ = line_parts(minus[0:1, :], theta1, y0, yn)
        _, high_t = line_parts(plus[0:1, :], theta1, y0, yn)
        g = k1 * jnp.where(y_past, high_r * low_c, low_r * high_c)
        ext = jnp.zeros((columns, lanes), F32)
        for e, values in enumerate((low_b * high_c * k1, high_t * low_c * k1, low_c, high_c)):
            ext = jnp.where(y_j == e * planes + z, values, ext)
        gy_ref[z, :, :lanes], gy_ref[planes + z, :, :lanes] = split(g)
        gy_ref[z, :, lanes:], gy_ref[planes + z, :, lanes:] = split(ext)
    lx[0] = packed

    total = planes * nz
    cond = [jnp.full((8, lanes), table[sheet[z]], F32) for z in range(total)]
    lead = [HEAT_SPREADING * STIFF * 0.5 * (cond[z] + cond[z + 1]) for z in range(total - 1)]
    lower = [jnp.ones((8, lanes), F32)]
    flux = HEAT_SPREADING * STIFF * cond[0]
    resist = [1.0 / value for value in lead]
    for z in range(total - 1):
        flux = flux + lower[z]
        lower.append(lower[z] + flux * resist[z])
    weight = 1.0 / (flux + lower[total - 1])
    upper = [None] * total
    upper[total - 1] = weight
    flux = jnp.zeros((8, lanes), F32)
    for z in range(total - 2, -1, -1):
        flux = flux + upper[z + 1]
        upper[z] = upper[z + 1] + flux * resist[z]
    zero = jnp.zeros((8, lanes), F32)
    z_scr[0], z_scr[total + 3] = zero, zero
    z_scr[total + 1], z_scr[total + 2] = zero, zero
    for z in range(total):
        z_scr[1 + z] = lower[z]
        z_scr[total + 3 + z] = upper[z]
    z_scr[2 * total + 3] = zero
    mine = gz * planes
    for z in range(planes + 2):
        phz[z] = z_scr[mine + z]
        psz[z] = jnp.where(mine + z == 0, zero, z_scr[total + 2 + mine + z])

    low_lane, high_lane = zero, zero
    for z in range(planes):
        low_lane = jnp.where(lane_z == z, phz[z + 1], low_lane)
        high_lane = jnp.where(lane_z == z, psz[z + 1], high_lane)
    row_p, lane_p = iota((planes, lanes), 0), iota((planes, lanes), 1)
    low_rows, high_rows = jnp.zeros((planes, lanes), F32), jnp.zeros((planes, lanes), F32)
    for z in range(planes):
        low_rows = jnp.where(row_p == z, phz[z + 1][0:1, :], low_rows)
        high_rows = jnp.where(row_p == z, psz[z + 1][0:1, :], high_rows)
    blocks, ends = [], []
    for e in range(2):
        g = jnp.where(
            lane_p % planes >= row_p,
            low_rows * high_lane[0:1, :],
            high_rows * low_lane[0:1, :],
        )
        blocks.append(jnp.where(lane_p // planes == e, g, 0.0))
        ends.append(
            jnp.where(lane_p == e, low_rows, jnp.where(lane_p == 2 + e, high_rows, 0.0))
        )
    rest = jnp.zeros((lanes - 2 * planes, lanes), F32)
    mz[0] = jnp.concatenate(blocks + [rest], axis=0)
    mz[1] = jnp.concatenate(ends + [rest], axis=0)
    row8 = iota((8, lanes), 0)
    wz[0] = jnp.where(
        (row8 < 2) & (lane_e == row8),
        high_lane,
        jnp.where((row8 >= 2) & (row8 < 4) & (lane_e == row8 - 2), low_lane, 0.0),
    )


def slopes(
    counts, idx, cond, scales, u_ref, kind_ref, xr0, xr1, yr0, yr1, zr0, zr1,
    ux, uy, uz, kx0, kx1, ky0, ky1, kz,
):
    planes, rows, columns = u_ref.shape
    even = [idx[d] % 2 == 0 for d in range(3)]
    at_low = [idx[d] == 0 for d in range(3)]
    at_high = [idx[d] == counts[d] - 1 for d in range(3)]
    row, lane = iota((rows, columns), 0), iota((rows, columns), 1)

    def ends(first, second, d):
        return jnp.where(even[d], second, first), jnp.where(even[d], first, second)

    low, high = ends(xr0[0], xr1[0], 0)
    ux[...] = jnp.zeros(ux.shape, F32)
    for z in range(planes):
        ux[z, 0:1, :] = low[z : z + 1, :]
        ux[z, 1:2, :] = high[z : z + 1, :]
    x_low, x_high = ends(xr0[1], xr1[1], 0)
    low, high = ends(yr0[...], yr1[...], 1)
    kind = iota((rows, 128), 1) // planes
    uy[...] = jnp.zeros(uy.shape, F32)
    uy[:rows, :] = jnp.where(
        kind == 0, low, jnp.where(kind == 1, pltpu.roll(high, planes, 1), 0.0)
    )
    low, high = ends(zr0[0], zr1[0], 2)
    uz[0] = jnp.where(at_low[2], 0.0, low)
    uz[1] = high
    z_low, z_high = ends(zr0[1], zr1[1], 2)
    half = 0.5 * HEAT_SPREADING
    y_low, y_high = ends(yr0[...], yr1[...], 1)
    c_before = None
    for z in range(planes):
        c = conductance(kind_ref[z], cond[z][0:1, :], scales)
        first = jnp.where(at_low[0], -c[0:1, :], x_low[z : z + 1, :])
        final = jnp.where(at_high[0], -c[rows - 1 :, :], x_high[z : z + 1, :])
        kx0[z] = half * (c + jnp.where(row == 0, first, pltpu.roll(c, 1, 0)))
        kx1[z] = half * (c + jnp.where(row == rows - 1, final, pltpu.roll(c, rows - 1, 0)))
        first = jnp.where(at_low[1], -c, pltpu.roll(y_low, columns - planes - z, 1))
        final = jnp.where(at_high[1], -c, pltpu.roll(y_high, columns - 1 - planes - z, 1))
        ky0[z] = half * (c + jnp.where(lane == 0, first, pltpu.roll(c, 1, 1)))
        ky1[z] = half * (c + jnp.where(lane == columns - 1, final, pltpu.roll(c, columns - 1, 1)))
        if z == 0:
            kz[z] = half * (c + jnp.where(at_low[2], c, z_low))
        else:
            kz[z] = half * (c + c_before)
        c_before = c
        if z == planes - 1:
            kz[planes] = half * jnp.where(at_high[2], 0.0, c + z_high)


def outflow(z, u_ref, ux, uy, uz, kx0, kx1, ky0, ky1, kz):
    planes, rows, columns = u_ref.shape
    u = u_ref[z]
    row, lane = iota((rows, columns), 0), iota((rows, columns), 1)
    edge = uy[:rows, :]
    edge_low = pltpu.roll(edge, columns - z, 1) if z else edge
    edge_high = pltpu.roll(edge, columns - 1 - planes - z, 1)
    below = uz[0] if z == 0 else u_ref[z - 1]
    above = uz[1] if z == planes - 1 else u_ref[z + 1]
    total = kx0[z] * (jnp.where(row == 0, ux[z, 0:1, :], pltpu.roll(u, 1, 0)) - u)
    total += kx1[z] * (
        jnp.where(row == rows - 1, ux[z, 1:2, :], pltpu.roll(u, rows - 1, 0)) - u
    )
    total += ky0[z] * (jnp.where(lane == 0, edge_low, pltpu.roll(u, 1, 1)) - u)
    total += ky1[z] * (
        jnp.where(lane == columns - 1, edge_high, pltpu.roll(u, columns - 1, 1)) - u
    )
    return total + kz[z] * (below - u) + kz[z + 1] * (above - u)


def advance(idx, source_of, gx_ref, gy_ref, phz, psz, t_ref, e_ref, z_send, x_sends):
    planes, extent, columns = t_ref.shape
    rows = extent - EXTRA
    sums = jnp.zeros((extent, 128), F32)
    below, above = jnp.zeros((rows, columns), F32), jnp.zeros((rows, columns), F32)
    for z in range(planes):
        high, low = split(source_of(z))
        out = mm(gx_ref[z], jnp.concatenate([high, low], axis=1))
        t = out[:extent, :columns] + (out[:extent, columns:] + out[extent:, :columns])
        high, low = split(t)
        twice = jnp.concatenate([gy_ref[z], gy_ref[z]], axis=0)
        out = mm(jnp.concatenate([high, low], axis=1), twice) + mm(high, gy_ref[planes + z])
        t_ref[z] = out[:, :columns]
        sums += out[:, columns:]
        main = out[:rows, :columns]
        below += phz[z + 1][0:1, :] * main
        above += psz[z + 1][0:1, :] * main
    e_ref[...] = sums
    for b, send in enumerate(x_sends):
        take = jnp.where((idx[0] >> b) % 2 == 0, 0, 1)
        for z in range(planes):
            pair = t_ref[z, rows + 2 : rows + 4, :]
            send[z : z + 1, :] = jnp.where(take == 0, pair[0:1], pair[1:2])
        pair = sums[rows + 2 : rows + 4, :]
        send[planes:, :] = jnp.broadcast_to(
            jnp.where(take == 0, pair[0:1], pair[1:2]), (8, 128)
        )
    z_send[0], z_send[1] = below, above


def joule_kernel(sizes, sheet_in, table_in, scaling_in, got_in, gx_ref, gy_ref, co, joule,
                 r_scr, k_scr, z_scr, got, sheet, table, scaling, sems):
    started = copies(
        [
            (sheet_in, sheet), (table_in, table), (scaling_in, scaling),
            (got_in.at[:, 0, :], got),
        ],
        sems,
    )
    for copy in started:
        copy.start()
    for copy in started[:3]:
        copy.wait()
    coefficients(sizes, place(), sheet, table, scaling, gx_ref, gy_ref, co, z_scr)
    started[3].wait()
    joule_into(got, joule, r_scr, k_scr)


def start_kernel(sizes, xr0, xr1, yr0, yr1, zr0, zr1,
                 u_ref, kind_ref, gx_ref, gy_ref, co, joule,
                 ux, uy, uz, kx0, kx1, ky0, ky1, kz, t_ref, e_ref, *sends):
    idx = place()
    phz, psz, cond, kinds = groups_of(sizes, co, "phz", "psz", "cond", "kinds")
    scales = [kinds[category][0:1, :] for category in range(sizes[6])]
    slopes(
        sizes[3:], idx, cond, scales, u_ref, kind_ref, xr0, xr1, yr0, yr1, zr0, zr1,
        ux, uy, uz, kx0, kx1, ky0, ky1, kz,
    )

    def source_of(z):
        out = outflow(z, u_ref, ux, uy, uz, kx0, kx1, ky0, ky1, kz)
        return out + OHMIC_POWER * ((1.0 + WARMING_SLOPE * u_ref[z]) * joule[z])

    advance(
        idx, source_of, gx_ref, gy_ref, phz, psz, t_ref, e_ref, sends[0], sends[1:]
    )


def x_kernel(sizes, e_ref, co, pair, near, *rest):
    idx = place()
    planes, nx = sizes[0], sizes[3]
    gots, (e_out, f_out, send), far = rest[: nx - 1], rest[nx - 1 : nx + 2], rest[nx + 2 :]
    for out in far:
        out[...] = jnp.where((idx[2] >> 1) % 2 == 0, pair[0] + near[0], pair[1] + near[1])
    dx, dxl, lx = groups_of(sizes, co, "dx", "dxl", "lx")
    me = idx[0]
    sums = [[jnp.zeros((planes, 128), F32), jnp.zeros((8, 128), F32)] for _ in range(2)]
    for k, got in zip(range(1, nx), gots):
        other = partner(me, k, nx)
        far = jnp.abs(me - other)
        pair = got[:planes, :] * dx[far], got[planes:, :] * dxl[far]
        for side, keep in ((0, other < me), (1, other > me)):
            for part in range(2):
                sums[side][part] += jnp.where(keep, pair[part], 0.0)
    f_out[:planes, :], f_out[planes:, :] = sums[0][0], sums[1][0]
    row, lane = iota((planes, 128), 0), iota((planes, 128), 1)
    own = lane % planes == row
    ext = jnp.concatenate(
        [jnp.where(own, sums[0][1][0:1, :], 0.0), jnp.where(own, sums[1][1][0:1, :], 0.0)],
        axis=0,
    )
    e = e_ref[...] + stacked(lx[0][:, : 2 * planes], ext)
    e_out[...] = e
    send[...] = e.T[2 * planes : 4 * planes]


def four(rows):
    return jnp.concatenate([rows] * 4, axis=0)


def weights(ref, planes):
    row = iota((planes, 128), 0)
    values = jnp.zeros((planes, 128), F32)
    for z in range(planes):
        values = jnp.where(row == z, ref[z + 1][0:1, :], values)
    return values


def y_kernel(sizes, final, t_ref, e_ref, f_ref, co, *rest):
    idx = place()
    ny = sizes[4]
    dy, lx, by, cg, phz, psz, mz = groups_of(
        sizes, co, "dy", "lx", "by", "cg", "phz", "psz", "mz"
    )
    gots, rest = rest[: ny - 1], rest[ny - 1 :]
    l_ref, b_ref = rest[:2]
    sends, q_ref = (rest[2:], None) if final else (rest[3:], rest[2])
    planes, extent, columns = t_ref.shape
    rows = extent - EXTRA
    me = idx[1]
    row = iota((2 * planes, extent), 0)
    across = jnp.zeros((2 * planes, extent), F32)
    for k, got in zip(range(1, ny), gots):
        other = partner(me, k, ny)
        far = jnp.concatenate([dy[jnp.abs(me - other)][:, 0:1]] * 2, axis=0)
        keep = (row < planes) == (other < me)
        across += jnp.where(keep, got[...] * far, 0.0)
    others = jnp.concatenate(
        [
            jnp.zeros((2 * planes, extent), F32),
            across,
            jnp.zeros((128 - 4 * planes, extent), F32),
        ],
        axis=0,
    ).T
    left = lx[0] + others
    l_ref[...] = left
    right = jnp.concatenate([f_ref[...], by[idx[2]]], axis=0)
    b_ref[...] = right
    low, high = weights(phz, planes), weights(psz, planes)
    if not final:
        lane = iota((extent, 128), 1)
        q = jnp.where(lane < 2 * planes, e_ref[...], 0.0) + stacked(others, cg[0])
        q_ref[...] = q
        edge = stacked(q[:rows], mz[1]).T
        ghost = slice(rows, rows + 8)
        both = jnp.concatenate([right * four(low), right * four(high)], axis=1)
        ghosts = stacked(left[ghost, : 4 * planes], both)
        g_low, g_high = ghosts[:, :128], ghosts[:, 128:]
        for z in range(planes):
            value = t_ref[z, ghost, :]
            g_low += phz[z + 1][0:1, :] * value
            g_high += psz[z + 1][0:1, :] * value
    if ny == 2:
        across = jnp.where(me == 1, across[:planes], across[planes:])
    for b, send in enumerate(sends):
        lower = (idx[2] >> b) % 2 == 0
        scale = jnp.where(lower, low, high)
        at = 0
        if not final:
            send[:2, :] = jnp.where(lower, g_low[:2], g_high[:2])
            ends = jnp.where(lower, edge[:2], edge[2:4])
            for part in range(rows // 128):
                send[2 + 2 * part : 4 + 2 * part, :] = ends[:, part * 128 : (part + 1) * 128]
            at = 8
        send[at : at + 2 * planes, :] = f_ref[...] * jnp.concatenate([scale] * 2, axis=0)
        at += 2 * planes
        many = across.shape[0]
        scale = jnp.concatenate([scale] * (many // planes), axis=0)
        for part in range(rows // 128):
            send[at : at + many, :] = across[:, part * 128 : (part + 1) * 128] * scale
            at += many


def carried(nz, idx, bigs, smalls, ax, by, rows, ghosts):
    me = idx[2]
    planes = by.each // 2
    at_top = me % 2 == 1
    below = jnp.where(at_top, bigs[0][0], 0.0)
    above = jnp.where(at_top, 0.0, bigs[0][1])
    for b, big in enumerate(bigs[1:], 1):
        at_top = (me >> b) % 2 == 1
        below += jnp.where(at_top, big[...], 0.0)
        above += jnp.where(at_top, 0.0, big[...])
    g_below = g_above = 0.0
    ends = [0.0, 0.0]
    lefts, rights = [], []
    for k, small in zip(range(1, nz), smalls):
        other = partner(me, k, nz)
        lower = other < me
        at = 0
        halves = rows // 128
        if ghosts:
            g_below += jnp.where(lower, small[:2, :], 0.0)
            g_above += jnp.where(lower, 0.0, small[:2, :])
            value = jnp.concatenate(
                [small[2 + 2 * p : 4 + 2 * p, :] for p in range(halves)], axis=1
            )
            ends[0] += jnp.where(lower, value, 0.0)
            ends[1] += jnp.where(lower, 0.0, value)
            at = 8
        both = at + 2 * planes
        many = (small.shape[0] - both) // halves
        across = [small[both + p * many : both + (p + 1) * many, :] for p in range(halves)]
        near = [ax[other * halves + half] for half in range(halves)]
        lefts += [jnp.concatenate(near, axis=1), jnp.concatenate(across, axis=1)]
        lines = by[other]
        if many == planes:
            lines = jnp.where(idx[1] == 1, lines[:planes], lines[planes:])
        right = jnp.concatenate([small[at:both, :], lines], axis=0)
        rights.append(
            jnp.concatenate(
                [jnp.where(lower, right, 0.0), jnp.where(lower, 0.0, right)], axis=1
            )
        )
    edges = None
    if ghosts:
        edges = jnp.concatenate(ends + [jnp.zeros((4, rows), F32)], axis=0)
        none = jnp.zeros((6, 128), F32)
        g_below = jnp.concatenate([g_below, none], axis=0)
        g_above = jnp.concatenate([g_above, none], axis=0)
    more = stacked_rows(jnp.concatenate(lefts, axis=0), jnp.concatenate(rights, axis=0))
    below, above = below + more[:, :128], above + more[:, 128:]
    return below, above, g_below, g_above, edges


def whole_planes(t_ref, l_ref, b_ref, second, extent):
    planes, _, columns = t_ref.shape
    high, low = split(l_ref[:extent, : 4 * planes])
    left = jnp.concatenate([high, low, high], axis=1)
    right = b_ref[...]
    row = iota(right.shape, 0) % planes
    for z in range(0, planes, 2):
        own = [jnp.where(row == z + k, right, 0.0) for k in range(2)]
        r_high, r_low = split(jnp.concatenate(own, axis=1))
        out = mm(left, jnp.concatenate([r_high, r_high, r_low], axis=0))
        for k in range(2):
            second[z + k] = t_ref[z + k, :extent, :] + out[:, k * columns : (k + 1) * columns]


def change(outside, second, phz, psz, below, above, emit):
    planes = second.shape[0]
    tails = [above]
    for z in range(planes - 1, -1, -1):
        tails.append(tails[-1] + psz[z + 1][0:1, :] * second[z])
    tails = tails[::-1]
    if outside:
        emit(-1, psz[0][0:1, :] * below + phz[0][0:1, :] * tails[0])
    head = below
    for z in range(planes):
        head = head + phz[z + 1][0:1, :] * second[z]
        emit(z, psz[z + 1][0:1, :] * head + phz[z + 1][0:1, :] * tails[z + 1])
    if outside:
        emit(planes, psz[planes + 1][0:1, :] * head + phz[planes + 1][0:1, :] * above)


def rise_kernel(sizes, t_in, l_ref, b_ref, q_ref, co,
                u_ref, ux, uy, uz, kx0, kx1, ky0, ky1, kz, joule, gx_ref, gy_ref, *rest):
    idx = place()
    nz = sizes[5]
    phz, psz, mz, wz, ax, by = groups_of(sizes, co, "phz", "psz", "mz", "wz", "ax", "by")
    deep = (nz - 1).bit_length()
    bigs, smalls, rest = rest[:deep], rest[deep : deep + nz - 1], rest[deep + nz - 1 :]
    u_out, ux_out, uy_out, uz_out, t_ref, e_ref = rest[:6]
    sends, second = rest[6:-1], rest[-1]
    planes, rows, columns = u_ref.shape
    whole_planes(t_in, l_ref, b_ref, second, rows + 8)
    below, above, g_below, g_above, edges = carried(nz, idx, bigs, smalls, ax, by, rows, True)

    def emit(z, value):
        if z == -1:
            uz_out[0] = uz[0] + value[:rows]
        elif z == planes:
            uz_out[1] = uz[1] + value[:rows]
        else:
            u_out[z] = u_ref[z] + value[:rows]
            ux_out[z] = ux[z] + value[rows:]

    change(
        True, second, phz, psz,
        jnp.concatenate([below, g_below], axis=0),
        jnp.concatenate([above, g_above], axis=0),
        emit,
    )
    grown = stacked(q_ref[:rows, :], mz[0]) + stacked_rows(edges, wz[0])
    uy_out[...] = uy[...]
    uy_out[:rows, :] = uy[:rows, :] + grown

    def source_of(z):
        out = outflow(z, u_out, ux_out, uy_out, uz_out, kx0, kx1, ky0, ky1, kz)
        return out + OHMIC_POWER * ((1.0 + WARMING_SLOPE * u_out[z]) * joule[z])

    advance(
        idx, source_of, gx_ref, gy_ref, phz, psz, t_ref, e_ref, sends[0], sends[1:]
    )


def finish_kernel(sizes, t_in, l_ref, b_ref, co, u_ref, joule, *rest):
    idx = place()
    nz = sizes[5]
    phz, psz, ax, by = groups_of(sizes, co, "phz", "psz", "ax", "by")
    deep = (nz - 1).bit_length()
    bigs, smalls, rest = rest[:deep], rest[deep : deep + nz - 1], rest[deep + nz - 1 :]
    u_out, heat_out, u_scr, heat_scr, second, sems = rest
    rows = u_ref.shape[1]
    started = []
    whole_planes(t_in, l_ref, b_ref, second, rows)
    below, above, _, _, _ = carried(nz, idx, bigs, smalls, ax, by, rows, False)

    def emit(z, value):
        u = u_ref[z] + value
        u_scr[z] = u
        heat_scr[z] = (1.0 + WARMING_SLOPE * u) * joule[z]
        for k, (src, dst) in enumerate(((u_scr, u_out), (heat_scr, heat_out))):
            started.append(pltpu.make_async_copy(src.at[z], dst.at[z], sems.at[k, z]))
            started[-1].start()

    change(False, second, phz, psz, below, above, emit)
    for copy in started:
        copy.wait()


def per_device(
    starting_warmth,
    sheet_stratum_number,
    stratum_heat_conduction,
    substance_kind,
    substance_kind_scaling,
    wire_piece_amperes,
    wire_piece_ohms_base,
    wire_piece_tile,
    wire_piece_voxel,
):
    planes, rows, columns = starting_warmth.shape
    counts = tuple(lax.axis_size(axis) for axis in ("gx", "gy", "gz"))
    nx, ny, nz = counts
    bits = [(n - 1).bit_length() for n in counts]
    devices = nx * ny * nz
    extent = rows + EXTRA
    block = shaped(planes, rows, columns)
    tables = sheet_stratum_number, stratum_heat_conduction, substance_kind_scaling
    scalars = [pltpu.SMEM(part.shape, part.dtype) for part in tables]

    count = wire_piece_amperes.shape[0]
    capacity = 2 * count // devices
    lanes = 128
    chunks = count // lanes
    segments = tuple(
        part.reshape(chunks, lanes)
        for part in (
            wire_piece_amperes, wire_piece_ohms_base, wire_piece_tile, wire_piece_voxel
        )
    )
    share, spare = shares(capacity)
    slots = planes * share + spare
    y_faces = 1 if ny == 2 else 2
    send, xs0, xs1, ys, zs0, zs1 = call(
        functools.partial(first_kernel, devices, planes, rows * columns, capacity),
        [
            shaped(devices, 1, 2 * slots),
            shaped(2, planes, columns),
            shaped(2, planes, columns),
            shaped(y_faces, rows, 128),
            shaped(2, rows, columns),
            shaped(2, rows, columns),
        ],
        (*tables, *segments, starting_warmth, substance_kind),
        far=9,
        far_out=True,
        vmem=60,
        scratch=[
            pltpu.VMEM((devices, 1, 2 * slots), F32),
            pltpu.VMEM((2, 2, planes, columns), F32),
            pltpu.VMEM((y_faces, rows, 128), F32),
            pltpu.VMEM((2, rows, columns), F32),
        ]
        + [pltpu.VMEM((chunks, lanes), part.dtype) for part in segments]
        + [
            pltpu.VMEM((5 * devices, count), BF16),
            pltpu.VMEM((max(planes * share, spare), count), BF16),
            pltpu.VMEM((devices * planes, lanes), F32),
            pltpu.VMEM((chunks, lanes), jnp.int32),
            pltpu.VMEM(block.shape, F32),
            pltpu.VMEM(block.shape, jnp.int32),
            *scalars,
            pltpu.SemaphoreType.DMA((7,)),
            pltpu.SemaphoreType.DMA((2, planes)),
            pltpu.SemaphoreType.DMA((8,)),
        ],
    )
    got = lax.all_to_all(send, ("gx", "gy", "gz"), split_axis=0, concat_axis=0, tiled=True)

    zr = next_pairs(zs0, zs1, "gz")
    xr = next_pairs(xs0, xs1, "gx")
    yr = next_pairs(ys[0], ys[-1], "gy")
    sizes = (planes, rows, columns, nx, ny, nz, substance_kind_scaling.shape[0])
    parts = [
        shaped(planes, 2 * extent, rows, dtype=BF16),
        shaped(2 * planes, columns, 256, dtype=BF16),
        shaped(table_rows(*sizes)[1], lanes),
    ]
    step_out = [shaped(planes, extent, columns), shaped(extent, 128)]
    step_out += [shaped(2, rows, columns)] + [shaped(planes + 8, columns)] * bits[0]
    total = devices * spare
    ghosts = [shaped(planes, 8, columns), shaped(extent, 128), shaped(2, rows, columns)]
    gx_m, gy_m, co, joule = call(
        functools.partial(joule_kernel, sizes),
        parts + [block],
        (*tables, got),
        far=4,
        vmem=24,
        scratch=[
            pltpu.VMEM((2 * columns, total), BF16),
            pltpu.VMEM((8, total), jnp.int32),
            pltpu.VMEM((2 * planes * nz + 4, 8, lanes), F32),
            pltpu.VMEM((devices, 2 * slots), F32),
            *scalars,
            pltpu.SemaphoreType.DMA((4,)),
        ],
    )
    ux, uy, uz, *rest = call(
        functools.partial(start_kernel, sizes),
        ghosts + [block] * 4 + [shaped(planes + 1, rows, columns)] + step_out,
        (*xr, *yr, *zr, starting_warmth, substance_kind, gx_m, gy_m, co, joule),
    )
    conduct, (t, e, *sends) = rest[:5], rest[5:]
    u = starting_warmth
    lines = planes if ny == 2 else 2 * planes
    small_rows = 2 * planes + lines * (rows // 128)
    for repeat in range(STEPS):
        pair, *sends = sends
        gots = all_pairs(sends, "gx")
        near = crossed(pair, 1, "gz")
        e, f, send, *far = call(
            functools.partial(x_kernel, sizes),
            [shaped(extent, 128), shaped(2 * planes, columns), shaped(2 * planes, extent)]
            + [shaped(rows, columns)] * (bits[2] - 1),
            (e, co, pair, near, *gots),
        )
        bigs = [near] + [crossed(array, 2, "gz") for array in far]
        gots = all_pairs([send] * bits[1], "gy")
        final = repeat == STEPS - 1
        q = [] if final else [shaped(extent, 128)]
        small = shaped(small_rows + (0 if final else 8), 128)
        left, right, *sends = call(
            functools.partial(y_kernel, sizes, final),
            [shaped(extent, 128), shaped(4 * planes, columns)] + q + [small] * bits[2],
            (t, e, f, co, *gots),
        )
        if final:
            smalls = all_pairs(sends, "gz")
        else:
            q, *sends = sends
            smalls = all_pairs(sends, "gz")
            u, ux, uy, uz, t, e, *sends = call(
                functools.partial(rise_kernel, sizes),
                [block, shaped(planes, 8, columns), shaped(extent, 128)]
                + [shaped(2, rows, columns)]
                + step_out,
                (t, left, right, q, co, u, ux, uy, uz, *conduct)
                + (joule, gx_m, gy_m, *bigs, *smalls),
                scratch=[pltpu.VMEM((planes, rows + 8, columns), F32)],
            )
    return tuple(
        call(
            functools.partial(finish_kernel, sizes),
            [block, block],
            (t, left, right, co, u, joule, *bigs, *smalls),
            scratch=[pltpu.VMEM((planes, rows, columns), F32)] * 3
            + [pltpu.SemaphoreType.DMA((2, planes))],
            far_out=True,
        )
    )


def solution(mesh):
    return jax.shard_map(
        per_device,
        mesh=mesh,
        in_specs=(
            P("gz", "gx", "gy"),
            P(),
            P(),
            P("gz", "gx", "gy"),
            P(),
            P(("gx", "gy", "gz")),
            P(("gx", "gy", "gz")),
            P(("gx", "gy", "gz"), None),
            P(("gx", "gy", "gz")),
        ),
        out_specs=(P("gz", "gx", "gy"), P("gz", "gx", "gy")),
        check_vma=False,
    )
```

```python
import functools

import jax
import jax.numpy as jnp
from jax import lax
from jax.experimental import pallas as pl
from jax.experimental.pallas import tpu as pltpu
from jax.sharding import PartitionSpec as P

STEPS = 2
HEAT_SPREADING = 1000.0
STIFF = 1.5
WARMING_SLOPE = 0.1
OHMIC_POWER = 8.0

F32 = jnp.float32
BF16 = jnp.bfloat16
EXTRA = 16


def call(kernel, out_shapes, args, scratch=(), vmem=24, far=0, far_out=False):
    specs = [pl.BlockSpec(memory_space=pltpu.VMEM)] * (len(args) - far)
    specs += [pl.BlockSpec(memory_space=pl.ANY)] * far
    return pl.pallas_call(
        kernel,
        out_shape=out_shapes,
        in_specs=specs,
        out_specs=[pl.BlockSpec(memory_space=pl.ANY if far_out else pltpu.VMEM)]
        * len(out_shapes),
        scratch_shapes=list(scratch),
        compiler_params=pltpu.CompilerParams(vmem_limit_bytes=vmem * 2**20),
        cost_estimate=pl.CostEstimate(flops=0, bytes_accessed=1, transcendentals=0),
    )(*args)


def shaped(*shape, dtype=F32):
    return jax.ShapeDtypeStruct(shape, dtype)


def split(x):
    high = x.astype(BF16)
    return high, (x - high.astype(F32)).astype(BF16)


def iota(shape, dim):
    return lax.broadcasted_iota(jnp.int32, shape, dim)


def place():
    return [lax.axis_index(axis) for axis in ("gx", "gy", "gz")]


def copies(pairs, sems):
    return [
        pltpu.make_async_copy(src, dst, sems.at[k]) for k, (src, dst) in enumerate(pairs)
    ]


def plane_copies(pairs, sems):
    started = [
        [
            pltpu.make_async_copy(src.at[z], dst.at[z], sems.at[k, z])
            for z in range(dst.shape[0])
        ]
        for k, (src, dst) in enumerate(pairs)
    ]
    for copies_of_plane in zip(*started):
        for copy in copies_of_plane:
            copy.start()
    return started


def mm(a, b):
    return jnp.dot(a, b, preferred_element_type=F32)


def stacked(a, b):
    (a_high, a_low), (b_high, b_low) = split(a), split(b)
    return mm(
        jnp.concatenate([a_high, a_low, a_high], axis=1),
        jnp.concatenate([b_high, b_high, b_low], axis=0),
    )


def stacked_rows(a, b):
    more = -a.shape[0] % 16
    if more:
        a = jnp.concatenate([a, jnp.zeros((more, a.shape[1]), F32)], axis=0)
        b = jnp.concatenate([b, jnp.zeros((more, b.shape[1]), F32)], axis=0)
    (a_high, a_low), (b_high, b_low) = split(a), split(b)
    return lax.dot_general(
        jnp.concatenate([a_high, a_low, a_high], axis=0),
        jnp.concatenate([b_high, b_high, b_low], axis=0),
        (((0,), (0,)), ((), ())),
        preferred_element_type=F32,
    )


def mm_nt(a, b):
    return lax.dot_general(a, b, (((1,), (1,)), ((), ())), preferred_element_type=F32)


def table_rows(planes, rows, columns, nx, ny, nz, classes):
    at, places = 0, {}
    for name, items, each in (
        ("lx", 1, rows + EXTRA),
        ("ax", nz * (rows // 128), 2 * planes),
        ("by", nz, 2 * planes),
        ("dx", nx, planes),
        ("dxl", nx, 8),
        ("dy", ny, planes),
        ("cg", 1, 128),
        ("phz", planes + 2, 8),
        ("psz", planes + 2, 8),
        ("mz", 2, 128),
        ("wz", 1, 8),
        ("cond", planes, 8),
        ("kinds", classes, 8),
    ):
        places[name] = (at, each)
        at += items * each
    return places, at


class Group:
    def __init__(self, ref, place):
        self.ref, (self.at, self.each) = ref, place

    def rows(self, k):
        at = self.at + k * self.each
        return pl.ds(at if isinstance(at, int) else pl.multiple_of(at, 8), self.each)

    def __getitem__(self, k):
        return self.ref[self.rows(k), :]

    def __setitem__(self, k, value):
        self.ref[self.rows(k), :] = value


def groups_of(sizes, ref, *names):
    places, _ = table_rows(*sizes)
    return [Group(ref, places[name]) for name in names]


def partner(me, k, n):
    return me ^ k


def groups(n):
    return [k.bit_length() - 1 for k in range(1, n)]


def all_pairs(arrays, axis):
    n = lax.axis_size(axis)
    return [
        lax.ppermute(arrays[b], axis, [(i, i ^ k) for i in range(n)])
        for k, b in zip(range(1, n), groups(n))
    ]


def crossed(array, k, axis):
    return lax.ppermute(array, axis, [(i, i ^ k) for i in range(lax.axis_size(axis))])


def next_pairs(even, odd, axis):
    n = lax.axis_size(axis)
    first = lax.ppermute(even, axis, [(i, i ^ 1) for i in range(n)])
    if n == 2:
        return first, first
    pairs = [(i, i + 1) for i in range(1, n - 1, 2)]
    return first, lax.ppermute(odd, axis, pairs + [(b, a) for a, b in pairs])


def conductance(kind, own, scales):
    factor = jnp.zeros(kind.shape, F32)
    for category, scale in enumerate(scales):
        factor = jnp.where(kind == category, scale, factor)
    return own * factor


def faces(idx, own, scales, u_ref, kind_ref, zc, xs, ys):
    planes, rows, columns = u_ref.shape
    even = [idx[d] % 2 == 0 for d in range(2)]
    lane = iota((rows, columns), 1)
    kept = [jnp.zeros((rows, columns), F32) for _ in range(ys.shape[0])]
    for z in range(planes):
        u = u_ref[z]
        if z in (0, planes - 1):
            c = zc[min(z, 1)]
        else:
            c = conductance(kind_ref[z], own[z], scales)
        for slot, values in ((0, u), (1, c)):
            at = 2 * (slot * planes + z)
            for k in range(len(kept)):
                upper = even[1] if k == 0 else jnp.logical_not(even[1])
                turned = pltpu.roll(values, at + jnp.where(upper, 1, 0), 1)
                kept[k] = jnp.where(lane == at, turned, kept[k])
            first, last = values[0:1, :], values[rows - 1 : rows, :]
            xs[0, slot, z : z + 1, :] = jnp.where(even[0], last, first)
            xs[1, slot, z : z + 1, :] = jnp.where(even[0], first, last)
    for k, value in enumerate(kept):
        ys[k] = value


def shares(capacity):
    return capacity // 4, capacity - capacity // 4


def first_kernel(blocks, planes, area, capacity,
                 sheet_in, table_in, scaling_in, amps_in, ohms_in, tile_in, cell_in,
                 u_in, kind_in,
                 send_out, xs0_out, xs1_out, ys_out, zs0_out, zs1_out,
                 send, xs, ys, zc,
                 amps, ohms, tiles, cells, a_scr, b_scr, z_scr, k_scr, u_ref, kind_ref,
                 sheet, table, scaling, sems, plane_sems, out_sems):
    started = copies(
        [
            (amps_in, amps), (ohms_in, ohms), (tile_in, tiles), (cell_in, cells),
            (sheet_in, sheet), (table_in, table), (scaling_in, scaling),
        ],
        sems,
    )
    for copy in started:
        copy.start()
    loads = plane_copies([(u_in, u_ref), (kind_in, kind_ref)], plane_sems)
    for copy in started:
        copy.wait()
    dispatch(
        blocks, planes, area, capacity, amps, ohms, tiles, cells, send,
        a_scr, b_scr, z_scr, k_scr,
    )
    idx = place()
    even = idx[2] % 2 == 0
    top = u_ref.shape[0] - 1
    own = [table[sheet[idx[2] * planes + z]] for z in range(planes)]
    scales = [scaling[category] for category in range(scaling.shape[0])]
    stores = [(send, send_out)]
    for copies_of_plane in zip(*loads):
        for copy in copies_of_plane:
            copy.wait()
    zc[0] = conductance(kind_ref[0], own[0], scales)
    zc[1] = conductance(kind_ref[top], own[top], scales)
    for out, upper in ((zs0_out, even), (zs1_out, jnp.logical_not(even))):
        stores.append((u_ref.at[jnp.where(upper, top, 0)], out.at[0]))
        stores.append((zc.at[jnp.where(upper, 1, 0)], out.at[1]))
    stored = copies(stores, out_sems)
    for copy in stored:
        copy.start()
    faces(idx, own, scales, u_ref, kind_ref, zc, xs, ys)
    last = [
        pltpu.make_async_copy(src, dst, out_sems.at[len(stores) + k])
        for k, (src, dst) in enumerate(
            ((xs.at[0], xs0_out), (xs.at[1], xs1_out), (ys, ys_out))
        )
    ]
    for copy in last:
        copy.start()
    for copy in stored + last:
        copy.wait()


def dispatch(blocks, planes, area, capacity, amps, ohms, tiles, cells, send,
             a_scr, b_scr, z_scr, k_scr):
    chunks, lanes = amps.shape
    share, spare = shares(capacity)
    keys, main = blocks * planes, planes * share
    power = amps[...] * amps[...] * ohms[...]
    tile, cell = tiles[...], cells[...]
    plane, within = cell // area, cell % area
    key = tile * planes + plane
    p_high, p_low = split(power)
    pieces = [
        p_high.astype(F32),
        p_low.astype(F32),
        (within >> 8).astype(F32),
        (within & 255).astype(F32),
        plane.astype(F32),
    ]
    key_row, block_row = iota((keys, lanes), 0), iota((blocks, lanes), 0)
    place = iota((main, lanes), 0).astype(jnp.int16)
    one, none = jnp.ones((main, lanes), BF16), jnp.zeros((main, lanes), BF16)
    pair = 2 * lanes
    ahead = jnp.where(iota((pair, pair), 0) < iota((pair, pair), 1), 1.0, 0.0).astype(BF16)
    base = jnp.zeros((keys, lanes), F32)
    for c in range(0, chunks, 2):
        hits = [key_row == key[c + k : c + k + 1, :] for k in range(2)]
        ones = [jnp.where(hit, 1.0, 0.0) for hit in hits]
        counted = mm(jnp.concatenate(ones, axis=1).astype(BF16), ahead)
        for k in range(2):
            row, cols = slice(c + k, c + k + 1), slice((c + k) * lanes, (c + k + 1) * lanes)
            order = counted[:, k * lanes : (k + 1) * lanes] + base
            rank = jnp.sum(jnp.where(hits[k], order, 0.0), axis=0, keepdims=True)
            rank = rank.astype(jnp.int32)
            k_scr[row, :] = rank
            slot = jnp.where(rank < share, plane[row, :] * share + rank, -1)
            b_scr[:main, cols] = jnp.where(place == slot.astype(jnp.int16), one, none)
            hit = block_row == tile[row, :]
            for n, piece in enumerate(pieces):
                a_scr[n * blocks : (n + 1) * blocks, cols] = jnp.where(
                    hit, piece[row, :], 0.0
                ).astype(BF16)
        base = base + (counted[:, pair - 1 :] + ones[1][:, lanes - 1 :])
    out = mm_nt(a_scr[: 4 * blocks, :], b_scr[:main, :])
    r = [out[k * blocks : (k + 1) * blocks] for k in range(4)]
    total = main + spare
    send[:, 0, :main] = r[0] + r[1]
    send[:, 0, total : total + main] = r[2] * 256.0 + r[3]
    send[:, 0, main:total] = jnp.zeros((blocks, spare), F32)
    send[:, 0, total + main :] = jnp.zeros((blocks, spare), F32)
    z_scr[...] = jnp.maximum(base - float(share), 0.0)

    @pl.when(jnp.max(z_scr[...]) > 0.0)
    def _():
        step = min(keys, 256)
        r, n = iota((step, step), 0), iota((step, step), 1)
        earlier = jnp.where((r // planes == n // planes) & (n < r), 1.0, 0.0).astype(BF16)
        for at in range(0, keys, step):
            part = slice(at, at + step)
            z_scr[part, :] = mm(earlier, z_scr[part, :].astype(BF16))
        place = iota((spare, lanes), 0)
        for c in range(chunks):
            row, cols = slice(c, c + 1), slice(c * lanes, (c + 1) * lanes)
            hit = key_row == key[row, :]
            first = jnp.sum(jnp.where(hit, z_scr[...], 0.0), axis=0, keepdims=True)
            rank = k_scr[row, :]
            slot = jnp.where(rank < share, -1, rank - share + first.astype(jnp.int32))
            b_scr[:spare, cols] = jnp.where(place == slot, 1.0, 0.0).astype(BF16)
        out = mm_nt(a_scr[...], b_scr[:spare, :])
        r = [out[k * blocks : (k + 1) * blocks] for k in range(5)]
        send[:, 0, main:total] = r[0] + r[1]
        send[:, 0, total + main :] = r[2] * 256.0 + r[3] + r[4] * float(area)


def joule_into(got, joule, r_scr, k_scr):
    planes, rows, columns = joule.shape
    sources, total = got.shape[0], got.shape[1] // 2
    spare = r_scr.shape[1] // sources
    main = total - spare
    share = main // planes
    lanes = 128
    per = lanes // share
    each = sources // per
    lane = iota((each, lanes), 1) // share
    row = iota((rows, lanes), 0).astype(F32).astype(BF16)
    column = iota((columns, lanes), 0).astype(F32).astype(BF16)
    one, none = jnp.ones((rows, lanes), BF16), jnp.zeros((rows, lanes), BF16)
    blank = jnp.zeros((columns, lanes), BF16)

    def gathered(values, h):
        out = values[:each]
        for g in range(per):
            part = values[g * each : (g + 1) * each]
            by = (g - h) * share % lanes
            part = pltpu.roll(part, by, 1) if by else part
            out = part if g == 0 else jnp.where(lane == g, part, out)
        return out

    for z in range(planes):
        at = z * share // lanes * lanes
        power = gathered(got[:, at : at + lanes], z % per)
        cell = gathered(got[:, total + at : total + at + lanes], z % per).astype(jnp.int32)
        high, low = split(power)
        high, low = high.astype(F32), low.astype(F32)
        x = (cell // columns).astype(F32)
        y = (cell % columns).astype(F32)
        lefts, rights = [], []
        for s in range(each):
            part = slice(s, s + 1)
            lefts.append(jnp.where(row == x[part, :].astype(BF16), one, none))
            hit = column == y[part, :].astype(BF16)
            rights.append(
                jnp.concatenate(
                    [
                        jnp.where(hit, high[part, :].astype(BF16), blank),
                        jnp.where(hit, low[part, :].astype(BF16), blank),
                    ],
                    axis=0,
                )
            )
        sums = mm_nt(jnp.concatenate(lefts, axis=1), jnp.concatenate(rights, axis=1))
        joule[z] = sums[:, :columns] + sums[:, columns:]

    @pl.when(jnp.max(got[:, main:total]) > 0.0)
    def _():
        column = iota((columns, spare), 0)
        for s in range(sources):
            power = got[s : s + 1, main:total]
            cell = got[s : s + 1, total + main :].astype(jnp.int32)
            part = slice(s * spare, (s + 1) * spare)
            high, low = split(power)
            hit = column == cell % columns
            r_scr[:columns, part] = jnp.where(hit, high.astype(F32), 0.0).astype(BF16)
            r_scr[columns:, part] = jnp.where(hit, low.astype(F32), 0.0).astype(BF16)
            k_scr[:, part] = jnp.broadcast_to(cell // columns, (8, spare))
        width = sources * spare
        step = 2048 if width % 2048 == 0 else width
        row = iota((rows, step), 0)

        def plane(z, carry):
            sums = jnp.zeros((rows, 2 * columns), F32)
            for at in range(0, width, step):
                hit = row == k_scr[0:1, at : at + step] - z * rows
                onehot = jnp.where(hit, 1.0, 0.0).astype(BF16)
                sums = sums + mm_nt(onehot, r_scr[:, at : at + step])
            joule[z] += sums[:, :columns] + sums[:, columns:]
            return carry

        lax.fori_loop(0, planes, plane, 0)


def line_parts(position, theta, start, cells):
    growing, falling = jnp.exp(position * theta), jnp.exp(-position * theta)
    lower = growing + falling * jnp.exp(-(2.0 * start + 1.0) * theta)
    upper = falling + growing * jnp.exp(-(2.0 * (cells - start) - 1.0) * theta)
    return lower, upper


def line(conduct, cells):
    lead = HEAT_SPREADING * STIFF * conduct
    t = 0.5 / jnp.sqrt(lead)
    theta = 2.0 * jnp.log1p(t + t * t / (1.0 + jnp.sqrt(1.0 + t * t)))
    scale = 1.0 / (jnp.sqrt(4.0 * lead + 1.0) * (1.0 - jnp.exp(-2.0 * cells * theta)))
    return theta, scale


def coefficients(sizes, idx, sheet, table, scaling, gx_ref, gy_ref, co, z_scr):
    planes, rows, columns, nx, ny, nz, classes = sizes
    lanes = 128
    extent = rows + EXTRA
    lx, ax, by, dx, dxl, dy, cg, phz, psz, mz, wz, cond_rows, kind_rows = groups_of(
        sizes, co, "lx", "ax", "by", "dx", "dxl", "dy", "cg", "phz", "psz", "mz", "wz",
        "cond", "kinds",
    )
    for category in range(classes):
        kind_rows[category] = jnp.full((8, lanes), scaling[category], F32)
    gx, gy, gz = idx[0], idx[1], idx[2]
    x0, xn = (gx * rows).astype(F32), float(nx * rows)
    y0, yn = (gy * columns).astype(F32), float(ny * columns)

    def wide(array, width):
        return jnp.concatenate([array] * (width // lanes), axis=1)

    def rows_of(first):
        value = jnp.ones((planes, lanes), F32)
        for z in range(planes):
            one = table[sheet[first + z]]
            value = jnp.where(iota((planes, lanes), 0) == z, one, value)
        return value

    lane_z = iota((8, lanes), 1) % planes
    by_lane = jnp.ones((8, lanes), F32)
    own = []
    for z in range(planes):
        value = table[sheet[gz * planes + z]]
        own.append(value)
        cond_rows[z] = jnp.full((8, lanes), value, F32)
        by_lane = jnp.where(lane_z == z, value, by_lane)
    theta_lane, scale_lane = line(by_lane, yn)
    theta_rows, _ = line(rows_of(gz * planes), 1.0)
    for k in range(nx):
        dx[k] = jnp.exp(-float(k * rows) * theta_rows)
        dxl[k] = jnp.exp(-float(k * rows) * theta_lane)
    for k in range(ny):
        dy[k] = jnp.exp(-float(k * columns) * theta_rows)

    for part in range(nz):
        conduct = rows_of(part * planes)
        theta, scale = line(conduct, xn)
        low, high = line_parts(
            iota((planes, rows), 1).astype(F32), wide(theta, rows), x0, xn
        )
        both = jnp.concatenate([high * wide(scale, rows), low * wide(scale, rows)], axis=0)
        for half in range(rows // lanes):
            ax[part * (rows // lanes) + half] = both[:, half * lanes : (half + 1) * lanes]
        theta, scale = line(conduct, yn)
        low, high = line_parts(iota((planes, columns), 1).astype(F32), theta, y0, yn)
        by[part] = jnp.concatenate([high * scale, low * scale], axis=0)

    minus, plus = jnp.full((8, lanes), -1.0, F32), jnp.full((8, lanes), float(columns), F32)
    low_b, high_b = line_parts(minus, theta_lane, y0, yn)
    low_t, high_t = line_parts(plus, theta_lane, y0, yn)
    r, n = iota((lanes, lanes), 0), iota((lanes, lanes), 1)
    same = r % planes == n % planes
    kind = jnp.where(same, (r // planes) * 4 + n // planes, -1)
    cg[0] = jnp.where(
        kind == 8, (high_b * scale_lane)[0:1, :],
        jnp.where(
            kind == 9, (high_t * scale_lane)[0:1, :],
            jnp.where(
                kind == 12, (low_b * scale_lane)[0:1, :],
                jnp.where(kind == 13, (low_t * scale_lane)[0:1, :], 0.0),
            ),
        ),
    )

    order = iota((extent, lanes), 0)
    index = jnp.where(order == rows, -1, jnp.where(order == rows + 1, rows, order))
    position = index.astype(F32)
    real = order < rows + 2
    index_w, order_w = wide(index, rows), wide(order, rows)
    at_or_past = index_w >= iota((extent, rows), 1)
    lane = iota((extent, lanes), 1)
    packed = jnp.zeros((extent, lanes), F32)
    y_col = iota((columns, columns), 0).astype(F32)
    y_i, y_j = iota((columns, columns), 0), iota((columns, columns), 1)
    y_past = y_j >= y_i
    for z in range(planes):
        theta, k_x = line(jnp.full((8, lanes), own[z], F32), xn)
        theta1, k1 = theta[0:1, :], k_x[0:1, :]
        low_c, high_c = line_parts(position, theta1, x0, xn)
        low_c = jnp.where(real, low_c * k1, 0.0)
        high_c = jnp.where(real, high_c * k1, 0.0)
        packed = jnp.where(lane == z, high_c, jnp.where(lane == planes + z, low_c, packed))
        low_r, high_r = line_parts(
            iota((8, rows), 1).astype(F32), wide(theta, rows), x0, xn
        )
        low_r, high_r = low_r[0:1, :], high_r[0:1, :]
        g = jnp.where(at_or_past, wide(high_c, rows) * low_r, wide(low_c, rows) * high_r)
        g = jnp.where(order_w == rows + 2, low_r, jnp.where(order_w == rows + 3, high_r, g))
        gx_ref[z, :extent, :], gx_ref[z, extent:, :] = split(g)

        theta, k_y = line(jnp.full((8, lanes), own[z], F32), yn)
        theta1, k1 = theta[0:1, :], k_y[0:1, :]
        low_r, high_r = line_parts(iota((8, columns), 1).astype(F32), theta, y0, yn)
        low_r, high_r = low_r[0:1, :], high_r[0:1, :]
        low_c, high_c = line_parts(y_col, theta1, y0, yn)
        low_b, _ = line_parts(minus[0:1, :], theta1, y0, yn)
        _, high_t = line_parts(plus[0:1, :], theta1, y0, yn)
        g = k1 * jnp.where(y_past, high_r * low_c, low_r * high_c)
        ext = jnp.zeros((columns, lanes), F32)
        for e, values in enumerate((low_b * high_c * k1, high_t * low_c * k1, low_c, high_c)):
            ext = jnp.where(y_j == e * planes + z, values, ext)
        gy_ref[z, :, :lanes], gy_ref[planes + z, :, :lanes] = split(g)
        gy_ref[z, :, lanes:], gy_ref[planes + z, :, lanes:] = split(ext)
    lx[0] = packed

    total = planes * nz
    cond = [jnp.full((8, lanes), table[sheet[z]], F32) for z in range(total)]
    lead = [HEAT_SPREADING * STIFF * 0.5 * (cond[z] + cond[z + 1]) for z in range(total - 1)]
    lower = [jnp.ones((8, lanes), F32)]
    flux = HEAT_SPREADING * STIFF * cond[0]
    resist = [1.0 / value for value in lead]
    for z in range(total - 1):
        flux = flux + lower[z]
        lower.append(lower[z] + flux * resist[z])
    weight = 1.0 / (flux + lower[total - 1])
    upper = [None] * total
    upper[total - 1] = weight
    flux = jnp.zeros((8, lanes), F32)
    for z in range(total - 2, -1, -1):
        flux = flux + upper[z + 1]
        upper[z] = upper[z + 1] + flux * resist[z]
    zero = jnp.zeros((8, lanes), F32)
    z_scr[0], z_scr[total + 3] = zero, zero
    z_scr[total + 1], z_scr[total + 2] = zero, zero
    for z in range(total):
        z_scr[1 + z] = lower[z]
        z_scr[total + 3 + z] = upper[z]
    z_scr[2 * total + 3] = zero
    mine = gz * planes
    for z in range(planes + 2):
        phz[z] = z_scr[mine + z]
        psz[z] = jnp.where(mine + z == 0, zero, z_scr[total + 2 + mine + z])

    low_lane, high_lane = zero, zero
    pair_z = iota((8, lanes), 1) // 2
    side = jnp.where(pair_z < planes, 1 - iota((8, lanes), 1) % 2, -1)
    for z in range(planes):
        low_lane = jnp.where(pair_z == z, phz[z + 1], low_lane)
        high_lane = jnp.where(pair_z == z, psz[z + 1], high_lane)
    row_p, lane_p = iota((planes, lanes), 0), iota((planes, lanes), 1)
    low_rows, high_rows = jnp.zeros((planes, lanes), F32), jnp.zeros((planes, lanes), F32)
    for z in range(planes):
        low_rows = jnp.where(row_p == z, phz[z + 1][0:1, :], low_rows)
        high_rows = jnp.where(row_p == z, psz[z + 1][0:1, :], high_rows)
    blocks, ends = [], []
    for e in range(2):
        g = jnp.where(
            lane_p // 2 >= row_p,
            low_rows * high_lane[0:1, :],
            high_rows * low_lane[0:1, :],
        )
        blocks.append(jnp.where(side[0:1, :] == e, g, 0.0))
        ends.append(
            jnp.where(lane_p == e, low_rows, jnp.where(lane_p == 2 + e, high_rows, 0.0))
        )
    rest = jnp.zeros((lanes - 2 * planes, lanes), F32)
    mz[0] = jnp.concatenate(blocks + [rest], axis=0)
    mz[1] = jnp.concatenate(ends + [rest], axis=0)
    row8 = iota((8, lanes), 0)
    wz[0] = jnp.where(
        (row8 < 2) & (side == row8),
        high_lane,
        jnp.where((row8 >= 2) & (row8 < 4) & (side == row8 - 2), low_lane, 0.0),
    )


def slopes(
    counts, idx, cond, scales, u_ref, kind_ref, xr0, xr1, yr0, yr1, zr0, zr1,
    ux, uy, uz, kx0, kx1, ky0, ky1, kz,
):
    planes, rows, columns = u_ref.shape
    even = [idx[d] % 2 == 0 for d in range(3)]
    at_low = [idx[d] == 0 for d in range(3)]
    at_high = [idx[d] == counts[d] - 1 for d in range(3)]
    row, lane = iota((rows, columns), 0), iota((rows, columns), 1)

    def ends(first, second, d):
        return jnp.where(even[d], second, first), jnp.where(even[d], first, second)

    low, high = ends(xr0[0], xr1[0], 0)
    ux[...] = jnp.zeros(ux.shape, F32)
    for z in range(planes):
        ux[z, 0:1, :] = low[z : z + 1, :]
        ux[z, 1:2, :] = high[z : z + 1, :]
    x_low, x_high = ends(xr0[1], xr1[1], 0)
    low, high = ends(yr0[...], yr1[...], 1)
    both = jnp.where(lane % 2 == 0, high, pltpu.roll(low, 1, 1))
    uy[...] = jnp.zeros(uy.shape, F32)
    uy[:rows, :] = jnp.where(lane < 2 * planes, both, 0.0)
    low, high = ends(zr0[0], zr1[0], 2)
    uz[0] = jnp.where(at_low[2], 0.0, low)
    uz[1] = high
    z_low, z_high = ends(zr0[1], zr1[1], 2)
    half = 0.5 * HEAT_SPREADING
    c_before = None
    for z in range(planes):
        c = conductance(kind_ref[z], cond[z][0:1, :], scales)
        first = jnp.where(at_low[0], -c[0:1, :], x_low[z : z + 1, :])
        final = jnp.where(at_high[0], -c[rows - 1 :, :], x_high[z : z + 1, :])
        kx0[z] = half * (c + jnp.where(row == 0, first, pltpu.roll(c, 1, 0)))
        kx1[z] = half * (c + jnp.where(row == rows - 1, final, pltpu.roll(c, rows - 1, 0)))
        edge = pltpu.roll(both, columns - 1 - 2 * (planes + z), 1)
        first = jnp.where(at_low[1], -c, edge)
        final = jnp.where(at_high[1], -c, edge)
        ky0[z] = half * (c + jnp.where(lane == 0, first, pltpu.roll(c, 1, 1)))
        ky1[z] = half * (c + jnp.where(lane == columns - 1, final, pltpu.roll(c, columns - 1, 1)))
        if z == 0:
            kz[z] = half * (c + jnp.where(at_low[2], c, z_low))
        else:
            kz[z] = half * (c + c_before)
        c_before = c
        if z == planes - 1:
            kz[planes] = half * jnp.where(at_high[2], 0.0, c + z_high)


def outflow(z, u_ref, ux, uy, uz, kx0, kx1, ky0, ky1, kz):
    planes, rows, columns = u_ref.shape
    u = u_ref[z]
    row, lane = iota((rows, columns), 0), iota((rows, columns), 1)
    edge = pltpu.roll(uy[:rows, :], columns - 1 - 2 * z, 1)
    below = uz[0] if z == 0 else u_ref[z - 1]
    above = uz[1] if z == planes - 1 else u_ref[z + 1]
    total = kx0[z] * (jnp.where(row == 0, ux[z, 0:1, :], pltpu.roll(u, 1, 0)) - u)
    total += kx1[z] * (
        jnp.where(row == rows - 1, ux[z, 1:2, :], pltpu.roll(u, rows - 1, 0)) - u
    )
    total += ky0[z] * (jnp.where(lane == 0, edge, pltpu.roll(u, 1, 1)) - u)
    total += ky1[z] * (
        jnp.where(lane == columns - 1, edge, pltpu.roll(u, columns - 1, 1)) - u
    )
    return total + kz[z] * (below - u) + kz[z + 1] * (above - u)


def advance(idx, source_of, gx_ref, gy_ref, phz, psz, t_ref, e_ref, z_send, x_sends):
    planes, extent, columns = t_ref.shape
    rows = extent - EXTRA
    sums = jnp.zeros((extent, 128), F32)
    below, above = jnp.zeros((rows, columns), F32), jnp.zeros((rows, columns), F32)
    for z in range(planes):
        high, low = split(source_of(z))
        out = mm(gx_ref[z], jnp.concatenate([high, low], axis=1))
        t = out[:extent, :columns] + (out[:extent, columns:] + out[extent:, :columns])
        high, low = split(t)
        twice = jnp.concatenate([gy_ref[z], gy_ref[z]], axis=0)
        out = mm(jnp.concatenate([high, low], axis=1), twice) + mm(high, gy_ref[planes + z])
        t_ref[z] = out[:, :columns]
        sums += out[:, columns:]
        main = out[:rows, :columns]
        below += phz[z + 1][0:1, :] * main
        above += psz[z + 1][0:1, :] * main
    e_ref[...] = sums
    for b, send in enumerate(x_sends):
        take = jnp.where((idx[0] >> b) % 2 == 0, 0, 1)
        for z in range(planes):
            pair = t_ref[z, rows + 2 : rows + 4, :]
            send[z : z + 1, :] = jnp.where(take == 0, pair[0:1], pair[1:2])
        pair = sums[rows + 2 : rows + 4, :]
        send[planes:, :] = jnp.broadcast_to(
            jnp.where(take == 0, pair[0:1], pair[1:2]), (8, 128)
        )
    z_send[0], z_send[1] = below, above


def joule_kernel(sizes, sheet_in, table_in, scaling_in, got_in, gx_ref, gy_ref, co, joule,
                 r_scr, k_scr, z_scr, got, sheet, table, scaling, sems):
    started = copies(
        [
            (sheet_in, sheet), (table_in, table), (scaling_in, scaling),
            (got_in.at[:, 0, :], got),
        ],
        sems,
    )
    for copy in started:
        copy.start()
    for copy in started[:3]:
        copy.wait()
    coefficients(sizes, place(), sheet, table, scaling, gx_ref, gy_ref, co, z_scr)
    started[3].wait()
    joule_into(got, joule, r_scr, k_scr)


def start_kernel(sizes, xr0, xr1, yr0, yr1, zr0, zr1,
                 u_ref, kind_ref, gx_ref, gy_ref, co, joule,
                 ux, uy, uz, kx0, kx1, ky0, ky1, kz, t_ref, e_ref, *sends):
    idx = place()
    phz, psz, cond, kinds = groups_of(sizes, co, "phz", "psz", "cond", "kinds")
    scales = [kinds[category][0:1, :] for category in range(sizes[6])]
    slopes(
        sizes[3:], idx, cond, scales, u_ref, kind_ref, xr0, xr1, yr0, yr1, zr0, zr1,
        ux, uy, uz, kx0, kx1, ky0, ky1, kz,
    )

    def source_of(z):
        out = outflow(z, u_ref, ux, uy, uz, kx0, kx1, ky0, ky1, kz)
        return out + OHMIC_POWER * ((1.0 + WARMING_SLOPE * u_ref[z]) * joule[z])

    advance(
        idx, source_of, gx_ref, gy_ref, phz, psz, t_ref, e_ref, sends[0], sends[1:]
    )


def x_kernel(sizes, e_ref, co, pair, near, *rest):
    idx = place()
    planes, nx = sizes[0], sizes[3]
    gots, (e_out, f_out, send), far = rest[: nx - 1], rest[nx - 1 : nx + 2], rest[nx + 2 :]
    for out in far:
        out[...] = jnp.where((idx[2] >> 1) % 2 == 0, pair[0] + near[0], pair[1] + near[1])
    dx, dxl, lx = groups_of(sizes, co, "dx", "dxl", "lx")
    me = idx[0]
    sums = [[jnp.zeros((planes, 128), F32), jnp.zeros((8, 128), F32)] for _ in range(2)]
    for k, got in zip(range(1, nx), gots):
        other = partner(me, k, nx)
        far = jnp.abs(me - other)
        pair = got[:planes, :] * dx[far], got[planes:, :] * dxl[far]
        for side, keep in ((0, other < me), (1, other > me)):
            for part in range(2):
                sums[side][part] += jnp.where(keep, pair[part], 0.0)
    f_out[:planes, :], f_out[planes:, :] = sums[0][0], sums[1][0]
    row, lane = iota((planes, 128), 0), iota((planes, 128), 1)
    own = lane % planes == row
    ext = jnp.concatenate(
        [jnp.where(own, sums[0][1][0:1, :], 0.0), jnp.where(own, sums[1][1][0:1, :], 0.0)],
        axis=0,
    )
    e = e_ref[...] + stacked(lx[0][:, : 2 * planes], ext)
    e_out[...] = e
    send[...] = e.T[2 * planes : 4 * planes]


def four(rows):
    return jnp.concatenate([rows] * 4, axis=0)


def weights(ref, planes):
    row = iota((planes, 128), 0)
    values = jnp.zeros((planes, 128), F32)
    for z in range(planes):
        values = jnp.where(row == z, ref[z + 1][0:1, :], values)
    return values


def y_kernel(sizes, final, t_ref, e_ref, f_ref, co, *rest):
    idx = place()
    ny = sizes[4]
    dy, lx, by, cg, phz, psz, mz = groups_of(
        sizes, co, "dy", "lx", "by", "cg", "phz", "psz", "mz"
    )
    gots, rest = rest[: ny - 1], rest[ny - 1 :]
    l_ref, b_ref = rest[:2]
    sends, q_ref = (rest[2:], None) if final else (rest[3:], rest[2])
    planes, extent, columns = t_ref.shape
    rows = extent - EXTRA
    me = idx[1]
    row = iota((2 * planes, extent), 0)
    across = jnp.zeros((2 * planes, extent), F32)
    for k, got in zip(range(1, ny), gots):
        other = partner(me, k, ny)
        far = jnp.concatenate([dy[jnp.abs(me - other)][:, 0:1]] * 2, axis=0)
        keep = (row < planes) == (other < me)
        across += jnp.where(keep, got[...] * far, 0.0)
    others = jnp.concatenate(
        [
            jnp.zeros((2 * planes, extent), F32),
            across,
            jnp.zeros((128 - 4 * planes, extent), F32),
        ],
        axis=0,
    ).T
    left = lx[0] + others
    l_ref[...] = left
    right = jnp.concatenate([f_ref[...], by[idx[2]]], axis=0)
    b_ref[...] = right
    low, high = weights(phz, planes), weights(psz, planes)
    if not final:
        lane = iota((extent, 128), 1)
        q = jnp.where(lane < 2 * planes, e_ref[...], 0.0) + stacked(others, cg[0])
        q_ref[...] = q
        edge = stacked(q[:rows], mz[1]).T
        ghost = slice(rows, rows + 8)
        both = jnp.concatenate([right * four(low), right * four(high)], axis=1)
        ghosts = stacked(left[ghost, : 4 * planes], both)
        g_low, g_high = ghosts[:, :128], ghosts[:, 128:]
        for z in range(planes):
            value = t_ref[z, ghost, :]
            g_low += phz[z + 1][0:1, :] * value
            g_high += psz[z + 1][0:1, :] * value
    if ny == 2:
        across = jnp.where(me == 1, across[:planes], across[planes:])
    for b, send in enumerate(sends):
        lower = (idx[2] >> b) % 2 == 0
        scale = jnp.where(lower, low, high)
        at = 0
        if not final:
            send[:2, :] = jnp.where(lower, g_low[:2], g_high[:2])
            ends = jnp.where(lower, edge[:2], edge[2:4])
            for part in range(rows // 128):
                send[2 + 2 * part : 4 + 2 * part, :] = ends[:, part * 128 : (part + 1) * 128]
            at = 8
        send[at : at + 2 * planes, :] = f_ref[...] * jnp.concatenate([scale] * 2, axis=0)
        at += 2 * planes
        many = across.shape[0]
        scale = jnp.concatenate([scale] * (many // planes), axis=0)
        for part in range(rows // 128):
            send[at : at + many, :] = across[:, part * 128 : (part + 1) * 128] * scale
            at += many


def carried(nz, idx, bigs, smalls, ax, by, rows, ghosts):
    me = idx[2]
    planes = by.each // 2
    at_top = me % 2 == 1
    below = jnp.where(at_top, bigs[0][0], 0.0)
    above = jnp.where(at_top, 0.0, bigs[0][1])
    for b, big in enumerate(bigs[1:], 1):
        at_top = (me >> b) % 2 == 1
        below += jnp.where(at_top, big[...], 0.0)
        above += jnp.where(at_top, 0.0, big[...])
    g_below = g_above = 0.0
    ends = [0.0, 0.0]
    lefts, rights = [], []
    for k, small in zip(range(1, nz), smalls):
        other = partner(me, k, nz)
        lower = other < me
        at = 0
        halves = rows // 128
        if ghosts:
            g_below += jnp.where(lower, small[:2, :], 0.0)
            g_above += jnp.where(lower, 0.0, small[:2, :])
            value = jnp.concatenate(
                [small[2 + 2 * p : 4 + 2 * p, :] for p in range(halves)], axis=1
            )
            ends[0] += jnp.where(lower, value, 0.0)
            ends[1] += jnp.where(lower, 0.0, value)
            at = 8
        both = at + 2 * planes
        many = (small.shape[0] - both) // halves
        across = [small[both + p * many : both + (p + 1) * many, :] for p in range(halves)]
        near = [ax[other * halves + half] for half in range(halves)]
        lefts += [jnp.concatenate(near, axis=1), jnp.concatenate(across, axis=1)]
        lines = by[other]
        if many == planes:
            lines = jnp.where(idx[1] == 1, lines[:planes], lines[planes:])
        right = jnp.concatenate([small[at:both, :], lines], axis=0)
        rights.append(
            jnp.concatenate(
                [jnp.where(lower, right, 0.0), jnp.where(lower, 0.0, right)], axis=1
            )
        )
    edges = None
    if ghosts:
        edges = jnp.concatenate(ends + [jnp.zeros((4, rows), F32)], axis=0)
        none = jnp.zeros((6, 128), F32)
        g_below = jnp.concatenate([g_below, none], axis=0)
        g_above = jnp.concatenate([g_above, none], axis=0)
    more = stacked_rows(jnp.concatenate(lefts, axis=0), jnp.concatenate(rights, axis=0))
    below, above = below + more[:, :128], above + more[:, 128:]
    return below, above, g_below, g_above, edges


def whole_planes(t_ref, l_ref, b_ref, second, extent):
    planes, _, columns = t_ref.shape
    high, low = split(l_ref[:extent, : 4 * planes])
    left = jnp.concatenate([high, low, high], axis=1)
    right = b_ref[...]
    row = iota(right.shape, 0) % planes
    for z in range(0, planes, 2):
        own = [jnp.where(row == z + k, right, 0.0) for k in range(2)]
        r_high, r_low = split(jnp.concatenate(own, axis=1))
        out = mm(left, jnp.concatenate([r_high, r_high, r_low], axis=0))
        for k in range(2):
            second[z + k] = t_ref[z + k, :extent, :] + out[:, k * columns : (k + 1) * columns]


def change(outside, second, phz, psz, below, above, emit):
    planes = second.shape[0]
    tails = [above]
    for z in range(planes - 1, -1, -1):
        tails.append(tails[-1] + psz[z + 1][0:1, :] * second[z])
    tails = tails[::-1]
    if outside:
        emit(-1, psz[0][0:1, :] * below + phz[0][0:1, :] * tails[0])
    head = below
    for z in range(planes):
        head = head + phz[z + 1][0:1, :] * second[z]
        emit(z, psz[z + 1][0:1, :] * head + phz[z + 1][0:1, :] * tails[z + 1])
    if outside:
        emit(planes, psz[planes + 1][0:1, :] * head + phz[planes + 1][0:1, :] * above)


def rise_kernel(sizes, t_in, l_ref, b_ref, q_ref, co,
                u_ref, ux, uy, uz, kx0, kx1, ky0, ky1, kz, joule, gx_ref, gy_ref, *rest):
    idx = place()
    nz = sizes[5]
    phz, psz, mz, wz, ax, by = groups_of(sizes, co, "phz", "psz", "mz", "wz", "ax", "by")
    deep = (nz - 1).bit_length()
    bigs, smalls, rest = rest[:deep], rest[deep : deep + nz - 1], rest[deep + nz - 1 :]
    u_out, ux_out, uy_out, uz_out, t_ref, e_ref = rest[:6]
    sends, second = rest[6:-1], rest[-1]
    planes, rows, columns = u_ref.shape
    whole_planes(t_in, l_ref, b_ref, second, rows + 8)
    below, above, g_below, g_above, edges = carried(nz, idx, bigs, smalls, ax, by, rows, True)

    def emit(z, value):
        if z == -1:
            uz_out[0] = uz[0] + value[:rows]
        elif z == planes:
            uz_out[1] = uz[1] + value[:rows]
        else:
            u_out[z] = u_ref[z] + value[:rows]
            ux_out[z] = ux[z] + value[rows:]

    change(
        True, second, phz, psz,
        jnp.concatenate([below, g_below], axis=0),
        jnp.concatenate([above, g_above], axis=0),
        emit,
    )
    grown = stacked(q_ref[:rows, :], mz[0]) + stacked_rows(edges, wz[0])
    uy_out[...] = uy[...]
    uy_out[:rows, :] = uy[:rows, :] + grown

    def source_of(z):
        out = outflow(z, u_out, ux_out, uy_out, uz_out, kx0, kx1, ky0, ky1, kz)
        return out + OHMIC_POWER * ((1.0 + WARMING_SLOPE * u_out[z]) * joule[z])

    advance(
        idx, source_of, gx_ref, gy_ref, phz, psz, t_ref, e_ref, sends[0], sends[1:]
    )


def finish_kernel(sizes, t_in, l_ref, b_ref, co, u_ref, joule, *rest):
    idx = place()
    nz = sizes[5]
    phz, psz, ax, by = groups_of(sizes, co, "phz", "psz", "ax", "by")
    deep = (nz - 1).bit_length()
    bigs, smalls, rest = rest[:deep], rest[deep : deep + nz - 1], rest[deep + nz - 1 :]
    u_out, heat_out, u_scr, heat_scr, second, sems = rest
    rows = u_ref.shape[1]
    started = []
    whole_planes(t_in, l_ref, b_ref, second, rows)
    below, above, _, _, _ = carried(nz, idx, bigs, smalls, ax, by, rows, False)

    def emit(z, value):
        u = u_ref[z] + value
        u_scr[z] = u
        heat_scr[z] = (1.0 + WARMING_SLOPE * u) * joule[z]
        for k, (src, dst) in enumerate(((u_scr, u_out), (heat_scr, heat_out))):
            started.append(pltpu.make_async_copy(src.at[z], dst.at[z], sems.at[k, z]))
            started[-1].start()

    change(False, second, phz, psz, below, above, emit)
    for copy in started:
        copy.wait()


def per_device(
    starting_warmth,
    sheet_stratum_number,
    stratum_heat_conduction,
    substance_kind,
    substance_kind_scaling,
    wire_piece_amperes,
    wire_piece_ohms_base,
    wire_piece_tile,
    wire_piece_voxel,
):
    planes, rows, columns = starting_warmth.shape
    counts = tuple(lax.axis_size(axis) for axis in ("gx", "gy", "gz"))
    nx, ny, nz = counts
    bits = [(n - 1).bit_length() for n in counts]
    devices = nx * ny * nz
    extent = rows + EXTRA
    block = shaped(planes, rows, columns)
    tables = sheet_stratum_number, stratum_heat_conduction, substance_kind_scaling
    scalars = [pltpu.SMEM(part.shape, part.dtype) for part in tables]

    count = wire_piece_amperes.shape[0]
    capacity = 2 * count // devices
    lanes = 128
    chunks = count // lanes
    segments = tuple(
        part.reshape(chunks, lanes)
        for part in (
            wire_piece_amperes, wire_piece_ohms_base, wire_piece_tile, wire_piece_voxel
        )
    )
    share, spare = shares(capacity)
    slots = planes * share + spare
    y_faces = 1 if ny == 2 else 2
    send, xs0, xs1, ys, zs0, zs1 = call(
        functools.partial(first_kernel, devices, planes, rows * columns, capacity),
        [
            shaped(devices, 1, 2 * slots),
            shaped(2, planes, columns),
            shaped(2, planes, columns),
            shaped(y_faces, rows, 128),
            shaped(2, rows, columns),
            shaped(2, rows, columns),
        ],
        (*tables, *segments, starting_warmth, substance_kind),
        far=9,
        far_out=True,
        vmem=60,
        scratch=[
            pltpu.VMEM((devices, 1, 2 * slots), F32),
            pltpu.VMEM((2, 2, planes, columns), F32),
            pltpu.VMEM((y_faces, rows, 128), F32),
            pltpu.VMEM((2, rows, columns), F32),
        ]
        + [pltpu.VMEM((chunks, lanes), part.dtype) for part in segments]
        + [
            pltpu.VMEM((5 * devices, count), BF16),
            pltpu.VMEM((max(planes * share, spare), count), BF16),
            pltpu.VMEM((devices * planes, lanes), F32),
            pltpu.VMEM((chunks, lanes), jnp.int32),
            pltpu.VMEM(block.shape, F32),
            pltpu.VMEM(block.shape, jnp.int32),
            *scalars,
            pltpu.SemaphoreType.DMA((7,)),
            pltpu.SemaphoreType.DMA((2, planes)),
            pltpu.SemaphoreType.DMA((8,)),
        ],
    )
    got = lax.all_to_all(send, ("gx", "gy", "gz"), split_axis=0, concat_axis=0, tiled=True)

    zr = next_pairs(zs0, zs1, "gz")
    xr = next_pairs(xs0, xs1, "gx")
    yr = next_pairs(ys[0], ys[-1], "gy")
    sizes = (planes, rows, columns, nx, ny, nz, substance_kind_scaling.shape[0])
    parts = [
        shaped(planes, 2 * extent, rows, dtype=BF16),
        shaped(2 * planes, columns, 256, dtype=BF16),
        shaped(table_rows(*sizes)[1], lanes),
    ]
    step_out = [shaped(planes, extent, columns), shaped(extent, 128)]
    step_out += [shaped(2, rows, columns)] + [shaped(planes + 8, columns)] * bits[0]
    total = devices * spare
    ghosts = [shaped(planes, 8, columns), shaped(extent, 128), shaped(2, rows, columns)]
    gx_m, gy_m, co, joule = call(
        functools.partial(joule_kernel, sizes),
        parts + [block],
        (*tables, got),
        far=4,
        vmem=24,
        scratch=[
            pltpu.VMEM((2 * columns, total), BF16),
            pltpu.VMEM((8, total), jnp.int32),
            pltpu.VMEM((2 * planes * nz + 4, 8, lanes), F32),
            pltpu.VMEM((devices, 2 * slots), F32),
            *scalars,
            pltpu.SemaphoreType.DMA((4,)),
        ],
    )
    ux, uy, uz, *rest = call(
        functools.partial(start_kernel, sizes),
        ghosts + [block] * 4 + [shaped(planes + 1, rows, columns)] + step_out,
        (*xr, *yr, *zr, starting_warmth, substance_kind, gx_m, gy_m, co, joule),
    )
    conduct, (t, e, *sends) = rest[:5], rest[5:]
    u = starting_warmth
    lines = planes if ny == 2 else 2 * planes
    small_rows = 2 * planes + lines * (rows // 128)
    for repeat in range(STEPS):
        pair, *sends = sends
        gots = all_pairs(sends, "gx")
        near = crossed(pair, 1, "gz")
        e, f, send, *far = call(
            functools.partial(x_kernel, sizes),
            [shaped(extent, 128), shaped(2 * planes, columns), shaped(2 * planes, extent)]
            + [shaped(rows, columns)] * (bits[2] - 1),
            (e, co, pair, near, *gots),
        )
        bigs = [near] + [crossed(array, 2, "gz") for array in far]
        gots = all_pairs([send] * bits[1], "gy")
        final = repeat == STEPS - 1
        q = [] if final else [shaped(extent, 128)]
        small = shaped(small_rows + (0 if final else 8), 128)
        left, right, *sends = call(
            functools.partial(y_kernel, sizes, final),
            [shaped(extent, 128), shaped(4 * planes, columns)] + q + [small] * bits[2],
            (t, e, f, co, *gots),
        )
        if final:
            smalls = all_pairs(sends, "gz")
        else:
            q, *sends = sends
            smalls = all_pairs(sends, "gz")
            u, ux, uy, uz, t, e, *sends = call(
                functools.partial(rise_kernel, sizes),
                [block, shaped(planes, 8, columns), shaped(extent, 128)]
                + [shaped(2, rows, columns)]
                + step_out,
                (t, left, right, q, co, u, ux, uy, uz, *conduct)
                + (joule, gx_m, gy_m, *bigs, *smalls),
                scratch=[pltpu.VMEM((planes, rows + 8, columns), F32)],
            )
    return tuple(
        call(
            functools.partial(finish_kernel, sizes),
            [block, block],
            (t, left, right, co, u, joule, *bigs, *smalls),
            scratch=[pltpu.VMEM((planes, rows, columns), F32)] * 3
            + [pltpu.SemaphoreType.DMA((2, planes))],
            far_out=True,
        )
    )


def solution(mesh):
    return jax.shard_map(
        per_device,
        mesh=mesh,
        in_specs=(
            P("gz", "gx", "gy"),
            P(),
            P(),
            P("gz", "gx", "gy"),
            P(),
            P(("gx", "gy", "gz")),
            P(("gx", "gy", "gz")),
            P(("gx", "gy", "gz"), None),
            P(("gx", "gy", "gz")),
        ),
        out_specs=(P("gz", "gx", "gy"), P("gz", "gx", "gy")),
        check_vma=False,
    )
```

```python
import functools

import jax
import jax.numpy as jnp
from jax import lax
from jax.experimental import pallas as pl
from jax.experimental.pallas import tpu as pltpu
from jax.sharding import PartitionSpec as P

STEPS = 2
HEAT_SPREADING = 1000.0
STIFF = 1.5
WARMING_SLOPE = 0.1
OHMIC_POWER = 8.0

F32 = jnp.float32
BF16 = jnp.bfloat16
EXTRA = 16


def call(kernel, out_shapes, args, scratch=(), vmem=24, far=0, far_out=False):
    specs = [pl.BlockSpec(memory_space=pltpu.VMEM)] * (len(args) - far)
    specs += [pl.BlockSpec(memory_space=pl.ANY)] * far
    return pl.pallas_call(
        kernel,
        out_shape=out_shapes,
        in_specs=specs,
        out_specs=[pl.BlockSpec(memory_space=pl.ANY if far_out else pltpu.VMEM)]
        * len(out_shapes),
        scratch_shapes=list(scratch),
        compiler_params=pltpu.CompilerParams(vmem_limit_bytes=vmem * 2**20),
        cost_estimate=pl.CostEstimate(flops=0, bytes_accessed=1, transcendentals=0),
    )(*args)


def shaped(*shape, dtype=F32):
    return jax.ShapeDtypeStruct(shape, dtype)


def split(x):
    high = x.astype(BF16)
    return high, (x - high.astype(F32)).astype(BF16)


def iota(shape, dim):
    return lax.broadcasted_iota(jnp.int32, shape, dim)


def place():
    return [lax.axis_index(axis) for axis in ("gx", "gy", "gz")]


def copies(pairs, sems):
    return [
        pltpu.make_async_copy(src, dst, sems.at[k]) for k, (src, dst) in enumerate(pairs)
    ]


def plane_copies(pairs, sems):
    started = [
        [
            pltpu.make_async_copy(src.at[z], dst.at[z], sems.at[k, z])
            for z in range(dst.shape[0])
        ]
        for k, (src, dst) in enumerate(pairs)
    ]
    for copies_of_plane in zip(*started):
        for copy in copies_of_plane:
            copy.start()
    return started


def mm(a, b):
    return jnp.dot(a, b, preferred_element_type=F32)


def stacked(a, b):
    (a_high, a_low), (b_high, b_low) = split(a), split(b)
    return mm(
        jnp.concatenate([a_high, a_low, a_high], axis=1),
        jnp.concatenate([b_high, b_high, b_low], axis=0),
    )


def stacked_rows(a, b):
    more = -a.shape[0] % 16
    if more:
        a = jnp.concatenate([a, jnp.zeros((more, a.shape[1]), F32)], axis=0)
        b = jnp.concatenate([b, jnp.zeros((more, b.shape[1]), F32)], axis=0)
    (a_high, a_low), (b_high, b_low) = split(a), split(b)
    return lax.dot_general(
        jnp.concatenate([a_high, a_low, a_high], axis=0),
        jnp.concatenate([b_high, b_high, b_low], axis=0),
        (((0,), (0,)), ((), ())),
        preferred_element_type=F32,
    )


def mm_nt(a, b):
    return lax.dot_general(a, b, (((1,), (1,)), ((), ())), preferred_element_type=F32)


def table_rows(planes, rows, columns, nx, ny, nz, classes):
    at, places = 0, {}
    for name, items, each in (
        ("lx", 1, rows + EXTRA),
        ("ax", nz * (rows // 128), 2 * planes),
        ("by", nz, 2 * planes),
        ("dx", nx, planes),
        ("dxl", nx, 8),
        ("dy", ny, planes),
        ("cg", 1, 128),
        ("phz", planes + 2, 8),
        ("psz", planes + 2, 8),
        ("mz", 2, 128),
        ("wz", 1, 8),
        ("cond", planes, 8),
        ("kinds", classes, 8),
    ):
        places[name] = (at, each)
        at += items * each
    return places, at


class Group:
    def __init__(self, ref, place):
        self.ref, (self.at, self.each) = ref, place

    def rows(self, k):
        at = self.at + k * self.each
        return pl.ds(at if isinstance(at, int) else pl.multiple_of(at, 8), self.each)

    def __getitem__(self, k):
        return self.ref[self.rows(k), :]

    def __setitem__(self, k, value):
        self.ref[self.rows(k), :] = value


def groups_of(sizes, ref, *names):
    places, _ = table_rows(*sizes)
    return [Group(ref, places[name]) for name in names]


def partner(me, k, n):
    return me ^ k


def groups(n):
    return [k.bit_length() - 1 for k in range(1, n)]


def all_pairs(arrays, axis):
    n = lax.axis_size(axis)
    return [
        lax.ppermute(arrays[b], axis, [(i, i ^ k) for i in range(n)])
        for k, b in zip(range(1, n), groups(n))
    ]


def crossed(array, k, axis):
    return lax.ppermute(array, axis, [(i, i ^ k) for i in range(lax.axis_size(axis))])


def next_pairs(even, odd, axis):
    n = lax.axis_size(axis)
    first = lax.ppermute(even, axis, [(i, i ^ 1) for i in range(n)])
    if n == 2:
        return first, first
    pairs = [(i, i + 1) for i in range(1, n - 1, 2)]
    return first, lax.ppermute(odd, axis, pairs + [(b, a) for a, b in pairs])


def conductance(kind, own, scales):
    factor = jnp.zeros(kind.shape, F32)
    for category, scale in enumerate(scales):
        factor = jnp.where(kind == category, scale, factor)
    return own * factor


def faces(idx, own, scales, u_ref, kind_ref, zc, xs, ys):
    planes, rows, columns = u_ref.shape
    even = [idx[d] % 2 == 0 for d in range(2)]
    lane = iota((rows, columns), 1)
    kept = [jnp.zeros((rows, columns), F32) for _ in range(ys.shape[0])]
    for z in range(planes):
        u = u_ref[z]
        if z in (0, planes - 1):
            c = zc[min(z, 1)]
        else:
            c = conductance(kind_ref[z], own[z], scales)
        for slot, values in ((0, u), (1, c)):
            at = 2 * (slot * planes + z)
            for k in range(len(kept)):
                upper = even[1] if k == 0 else jnp.logical_not(even[1])
                turned = pltpu.roll(values, at + jnp.where(upper, 1, 0), 1)
                kept[k] = jnp.where(lane == at, turned, kept[k])
            first, last = values[0:1, :], values[rows - 1 : rows, :]
            xs[0, slot, z : z + 1, :] = jnp.where(even[0], last, first)
            xs[1, slot, z : z + 1, :] = jnp.where(even[0], first, last)
    for k, value in enumerate(kept):
        ys[k] = value


def shares(capacity):
    return capacity // 4, capacity - capacity // 4


def first_kernel(blocks, planes, area, capacity,
                 sheet_in, table_in, scaling_in, amps_in, ohms_in, tile_in, cell_in,
                 u_in, kind_in,
                 send_out, xs0_out, xs1_out, ys_out, zs0_out, zs1_out,
                 send, xs, ys, zc,
                 amps, ohms, tiles, cells, a_scr, b_scr, z_scr, k_scr, u_ref, kind_ref,
                 sheet, table, scaling, sems, plane_sems, out_sems):
    started = copies(
        [
            (amps_in, amps), (ohms_in, ohms), (tile_in, tiles), (cell_in, cells),
            (sheet_in, sheet), (table_in, table), (scaling_in, scaling),
        ],
        sems,
    )
    for copy in started:
        copy.start()
    loads = plane_copies([(u_in, u_ref), (kind_in, kind_ref)], plane_sems)
    for copy in started:
        copy.wait()
    dispatch(
        blocks, planes, area, capacity, amps, ohms, tiles, cells, send,
        a_scr, b_scr, z_scr, k_scr,
    )
    idx = place()
    even = idx[2] % 2 == 0
    top = u_ref.shape[0] - 1
    own = [table[sheet[idx[2] * planes + z]] for z in range(planes)]
    scales = [scaling[category] for category in range(scaling.shape[0])]
    stores = [(send, send_out)]
    for copies_of_plane in zip(*loads):
        for copy in copies_of_plane:
            copy.wait()
    zc[0] = conductance(kind_ref[0], own[0], scales)
    zc[1] = conductance(kind_ref[top], own[top], scales)
    for out, upper in ((zs0_out, even), (zs1_out, jnp.logical_not(even))):
        stores.append((u_ref.at[jnp.where(upper, top, 0)], out.at[0]))
        stores.append((zc.at[jnp.where(upper, 1, 0)], out.at[1]))
    stored = copies(stores, out_sems)
    for copy in stored:
        copy.start()
    faces(idx, own, scales, u_ref, kind_ref, zc, xs, ys)
    last = [
        pltpu.make_async_copy(src, dst, out_sems.at[len(stores) + k])
        for k, (src, dst) in enumerate(
            ((xs.at[0], xs0_out), (xs.at[1], xs1_out), (ys, ys_out))
        )
    ]
    for copy in last:
        copy.start()
    for copy in stored + last:
        copy.wait()


def dispatch(blocks, planes, area, capacity, amps, ohms, tiles, cells, send,
             a_scr, b_scr, z_scr, k_scr):
    chunks, lanes = amps.shape
    share, spare = shares(capacity)
    keys, main = blocks * planes, planes * share
    power = amps[...] * amps[...] * ohms[...]
    tile, cell = tiles[...], cells[...]
    plane, within = cell // area, cell % area
    key = tile * planes + plane
    p_high, p_low = split(power)
    pieces = [
        p_high.astype(F32),
        p_low.astype(F32),
        (within >> 8).astype(F32),
        (within & 255).astype(F32),
        plane.astype(F32),
    ]
    key_row, block_row = iota((keys, lanes), 0), iota((blocks, lanes), 0)
    place = iota((main, lanes), 0).astype(jnp.int16)
    one, none = jnp.ones((main, lanes), BF16), jnp.zeros((main, lanes), BF16)
    pair = 2 * lanes
    ahead = jnp.where(iota((pair, pair), 0) < iota((pair, pair), 1), 1.0, 0.0).astype(BF16)
    base = jnp.zeros((keys, lanes), F32)
    for c in range(0, chunks, 2):
        hits = [key_row == key[c + k : c + k + 1, :] for k in range(2)]
        ones = [jnp.where(hit, 1.0, 0.0) for hit in hits]
        counted = mm(jnp.concatenate(ones, axis=1).astype(BF16), ahead)
        for k in range(2):
            row, cols = slice(c + k, c + k + 1), slice((c + k) * lanes, (c + k + 1) * lanes)
            order = counted[:, k * lanes : (k + 1) * lanes] + base
            rank = jnp.sum(jnp.where(hits[k], order, 0.0), axis=0, keepdims=True)
            rank = rank.astype(jnp.int32)
            k_scr[row, :] = rank
            slot = jnp.where(rank < share, plane[row, :] * share + rank, -1)
            b_scr[:main, cols] = jnp.where(place == slot.astype(jnp.int16), one, none)
            hit = block_row == tile[row, :]
            for n, piece in enumerate(pieces):
                a_scr[n * blocks : (n + 1) * blocks, cols] = jnp.where(
                    hit, piece[row, :], 0.0
                ).astype(BF16)
        base = base + (counted[:, pair - 1 :] + ones[1][:, lanes - 1 :])
    out = mm_nt(a_scr[: 4 * blocks, :], b_scr[:main, :])
    r = [out[k * blocks : (k + 1) * blocks] for k in range(4)]
    total = main + spare
    send[:, 0, :main] = r[0] + r[1]
    send[:, 0, total : total + main] = r[2] * 256.0 + r[3]
    send[:, 0, main:total] = jnp.zeros((blocks, spare), F32)
    send[:, 0, total + main :] = jnp.zeros((blocks, spare), F32)
    z_scr[...] = jnp.maximum(base - float(share), 0.0)

    @pl.when(jnp.max(z_scr[...]) > 0.0)
    def _():
        step = min(keys, 256)
        r, n = iota((step, step), 0), iota((step, step), 1)
        earlier = jnp.where((r // planes == n // planes) & (n < r), 1.0, 0.0).astype(BF16)
        for at in range(0, keys, step):
            part = slice(at, at + step)
            z_scr[part, :] = mm(earlier, z_scr[part, :].astype(BF16))
        place = iota((spare, lanes), 0)
        for c in range(chunks):
            row, cols = slice(c, c + 1), slice(c * lanes, (c + 1) * lanes)
            hit = key_row == key[row, :]
            first = jnp.sum(jnp.where(hit, z_scr[...], 0.0), axis=0, keepdims=True)
            rank = k_scr[row, :]
            slot = jnp.where(rank < share, -1, rank - share + first.astype(jnp.int32))
            b_scr[:spare, cols] = jnp.where(place == slot, 1.0, 0.0).astype(BF16)
        out = mm_nt(a_scr[...], b_scr[:spare, :])
        r = [out[k * blocks : (k + 1) * blocks] for k in range(5)]
        send[:, 0, main:total] = r[0] + r[1]
        send[:, 0, total + main :] = r[2] * 256.0 + r[3] + r[4] * float(area)


def joule_into(got, joule, r_scr, k_scr):
    planes, rows, columns = joule.shape
    sources, total = got.shape[0], got.shape[1] // 2
    spare = r_scr.shape[1] // sources
    main = total - spare
    share = main // planes
    lanes = 128
    per = lanes // share
    each = sources // per
    lane = iota((each, lanes), 1) // share
    row = iota((rows, lanes), 0).astype(F32).astype(BF16)
    column = iota((columns, lanes), 0).astype(F32).astype(BF16)
    one, none = jnp.ones((rows, lanes), BF16), jnp.zeros((rows, lanes), BF16)
    blank = jnp.zeros((columns, lanes), BF16)

    def gathered(values, h):
        out = values[:each]
        for g in range(per):
            part = values[g * each : (g + 1) * each]
            by = (g - h) * share % lanes
            part = pltpu.roll(part, by, 1) if by else part
            out = part if g == 0 else jnp.where(lane == g, part, out)
        return out

    for z in range(planes):
        at = z * share // lanes * lanes
        power = gathered(got[:, at : at + lanes], z % per)
        cell = gathered(got[:, total + at : total + at + lanes], z % per).astype(jnp.int32)
        high, low = split(power)
        high, low = high.astype(F32), low.astype(F32)
        x = (cell // columns).astype(F32)
        y = (cell % columns).astype(F32)
        lefts, rights = [], []
        for s in range(each):
            part = slice(s, s + 1)
            lefts.append(jnp.where(row == x[part, :].astype(BF16), one, none))
            hit = column == y[part, :].astype(BF16)
            rights.append(
                jnp.concatenate(
                    [
                        jnp.where(hit, high[part, :].astype(BF16), blank),
                        jnp.where(hit, low[part, :].astype(BF16), blank),
                    ],
                    axis=0,
                )
            )
        sums = mm_nt(jnp.concatenate(lefts, axis=1), jnp.concatenate(rights, axis=1))
        joule[z] = sums[:, :columns] + sums[:, columns:]

    @pl.when(jnp.max(got[:, main:total]) > 0.0)
    def _():
        column = iota((columns, spare), 0)
        for s in range(sources):
            power = got[s : s + 1, main:total]
            cell = got[s : s + 1, total + main :].astype(jnp.int32)
            part = slice(s * spare, (s + 1) * spare)
            high, low = split(power)
            hit = column == cell % columns
            r_scr[:columns, part] = jnp.where(hit, high.astype(F32), 0.0).astype(BF16)
            r_scr[columns:, part] = jnp.where(hit, low.astype(F32), 0.0).astype(BF16)
            k_scr[:, part] = jnp.broadcast_to(cell // columns, (8, spare))
        width = sources * spare
        step = 2048 if width % 2048 == 0 else width
        row = iota((rows, step), 0)

        def plane(z, carry):
            sums = jnp.zeros((rows, 2 * columns), F32)
            for at in range(0, width, step):
                hit = row == k_scr[0:1, at : at + step] - z * rows
                onehot = jnp.where(hit, 1.0, 0.0).astype(BF16)
                sums = sums + mm_nt(onehot, r_scr[:, at : at + step])
            joule[z] += sums[:, :columns] + sums[:, columns:]
            return carry

        lax.fori_loop(0, planes, plane, 0)


def line_parts(position, theta, start, cells):
    growing, falling = jnp.exp(position * theta), jnp.exp(-position * theta)
    lower = growing + falling * jnp.exp(-(2.0 * start + 1.0) * theta)
    upper = falling + growing * jnp.exp(-(2.0 * (cells - start) - 1.0) * theta)
    return lower, upper


def line(conduct, cells):
    lead = HEAT_SPREADING * STIFF * conduct
    t = 0.5 / jnp.sqrt(lead)
    theta = 2.0 * jnp.log1p(t + t * t / (1.0 + jnp.sqrt(1.0 + t * t)))
    scale = 1.0 / (jnp.sqrt(4.0 * lead + 1.0) * (1.0 - jnp.exp(-2.0 * cells * theta)))
    return theta, scale


def coefficients(sizes, idx, sheet, table, scaling, gx_ref, gy_ref, co, z_scr):
    planes, rows, columns, nx, ny, nz, classes = sizes
    lanes = 128
    extent = rows + EXTRA
    lx, ax, by, dx, dxl, dy, cg, phz, psz, mz, wz, cond_rows, kind_rows = groups_of(
        sizes, co, "lx", "ax", "by", "dx", "dxl", "dy", "cg", "phz", "psz", "mz", "wz",
        "cond", "kinds",
    )
    for category in range(classes):
        kind_rows[category] = jnp.full((8, lanes), scaling[category], F32)
    gx, gy, gz = idx[0], idx[1], idx[2]
    x0, xn = (gx * rows).astype(F32), float(nx * rows)
    y0, yn = (gy * columns).astype(F32), float(ny * columns)

    def wide(array, width):
        return jnp.concatenate([array] * (width // lanes), axis=1)

    def rows_of(first):
        value = jnp.ones((planes, lanes), F32)
        for z in range(planes):
            one = table[sheet[first + z]]
            value = jnp.where(iota((planes, lanes), 0) == z, one, value)
        return value

    lane_z = iota((8, lanes), 1) % planes
    by_lane = jnp.ones((8, lanes), F32)
    own = []
    for z in range(planes):
        value = table[sheet[gz * planes + z]]
        own.append(value)
        cond_rows[z] = jnp.full((8, lanes), value, F32)
        by_lane = jnp.where(lane_z == z, value, by_lane)
    theta_lane, scale_lane = line(by_lane, yn)
    theta_rows, _ = line(rows_of(gz * planes), 1.0)
    for k in range(nx):
        dx[k] = jnp.exp(-float(k * rows) * theta_rows)
        dxl[k] = jnp.exp(-float(k * rows) * theta_lane)
    for k in range(ny):
        dy[k] = jnp.exp(-float(k * columns) * theta_rows)

    for part in range(nz):
        conduct = rows_of(part * planes)
        theta, scale = line(conduct, xn)
        low, high = line_parts(
            iota((planes, rows), 1).astype(F32), wide(theta, rows), x0, xn
        )
        both = jnp.concatenate([high * wide(scale, rows), low * wide(scale, rows)], axis=0)
        for half in range(rows // lanes):
            ax[part * (rows // lanes) + half] = both[:, half * lanes : (half + 1) * lanes]
        theta, scale = line(conduct, yn)
        low, high = line_parts(iota((planes, columns), 1).astype(F32), theta, y0, yn)
        by[part] = jnp.concatenate([high * scale, low * scale], axis=0)

    minus, plus = jnp.full((8, lanes), -1.0, F32), jnp.full((8, lanes), float(columns), F32)
    low_b, high_b = line_parts(minus, theta_lane, y0, yn)
    low_t, high_t = line_parts(plus, theta_lane, y0, yn)
    r, n = iota((lanes, lanes), 0), iota((lanes, lanes), 1)
    same = r % planes == n % planes
    kind = jnp.where(same, (r // planes) * 4 + n // planes, -1)
    cg[0] = jnp.where(
        kind == 8, (high_b * scale_lane)[0:1, :],
        jnp.where(
            kind == 9, (high_t * scale_lane)[0:1, :],
            jnp.where(
                kind == 12, (low_b * scale_lane)[0:1, :],
                jnp.where(kind == 13, (low_t * scale_lane)[0:1, :], 0.0),
            ),
        ),
    )

    order = iota((extent, lanes), 0)
    index = jnp.where(order == rows, -1, jnp.where(order == rows + 1, rows, order))
    position = index.astype(F32)
    real = order < rows + 2
    index_w, order_w = wide(index, rows), wide(order, rows)
    at_or_past = index_w >= iota((extent, rows), 1)
    lane = iota((extent, lanes), 1)
    packed = jnp.zeros((extent, lanes), F32)
    y_col = iota((columns, columns), 0).astype(F32)
    y_i, y_j = iota((columns, columns), 0), iota((columns, columns), 1)
    y_past = y_j >= y_i
    for z in range(planes):
        theta, k_x = line(jnp.full((8, lanes), own[z], F32), xn)
        theta1, k1 = theta[0:1, :], k_x[0:1, :]
        low_c, high_c = line_parts(position, theta1, x0, xn)
        low_c = jnp.where(real, low_c * k1, 0.0)
        high_c = jnp.where(real, high_c * k1, 0.0)
        packed = jnp.where(lane == z, high_c, jnp.where(lane == planes + z, low_c, packed))
        low_r, high_r = line_parts(
            iota((8, rows), 1).astype(F32), wide(theta, rows), x0, xn
        )
        low_r, high_r = low_r[0:1, :], high_r[0:1, :]
        g = jnp.where(at_or_past, wide(high_c, rows) * low_r, wide(low_c, rows) * high_r)
        g = jnp.where(order_w == rows + 2, low_r, jnp.where(order_w == rows + 3, high_r, g))
        gx_ref[z, :extent, :], gx_ref[z, extent:, :] = split(g)

        theta, k_y = line(jnp.full((8, lanes), own[z], F32), yn)
        theta1, k1 = theta[0:1, :], k_y[0:1, :]
        low_r, high_r = line_parts(iota((8, columns), 1).astype(F32), theta, y0, yn)
        low_r, high_r = low_r[0:1, :], high_r[0:1, :]
        low_c, high_c = line_parts(y_col, theta1, y0, yn)
        low_b, _ = line_parts(minus[0:1, :], theta1, y0, yn)
        _, high_t = line_parts(plus[0:1, :], theta1, y0, yn)
        g = k1 * jnp.where(y_past, high_r * low_c, low_r * high_c)
        ext = jnp.zeros((columns, lanes), F32)
        for e, values in enumerate((low_b * high_c * k1, high_t * low_c * k1, low_c, high_c)):
            ext = jnp.where(y_j == e * planes + z, values, ext)
        gy_ref[z, :, :lanes], gy_ref[planes + z, :, :lanes] = split(g)
        gy_ref[z, :, lanes:], gy_ref[planes + z, :, lanes:] = split(ext)
    lx[0] = packed

    total = planes * nz
    cond = [jnp.full((8, lanes), table[sheet[z]], F32) for z in range(total)]
    lead = [HEAT_SPREADING * STIFF * 0.5 * (cond[z] + cond[z + 1]) for z in range(total - 1)]
    lower = [jnp.ones((8, lanes), F32)]
    flux = HEAT_SPREADING * STIFF * cond[0]
    resist = [1.0 / value for value in lead]
    for z in range(total - 1):
        flux = flux + lower[z]
        lower.append(lower[z] + flux * resist[z])
    weight = 1.0 / (flux + lower[total - 1])
    upper = [None] * total
    upper[total - 1] = weight
    flux = jnp.zeros((8, lanes), F32)
    for z in range(total - 2, -1, -1):
        flux = flux + upper[z + 1]
        upper[z] = upper[z + 1] + flux * resist[z]
    zero = jnp.zeros((8, lanes), F32)
    z_scr[0], z_scr[total + 3] = zero, zero
    z_scr[total + 1], z_scr[total + 2] = zero, zero
    for z in range(total):
        z_scr[1 + z] = lower[z]
        z_scr[total + 3 + z] = upper[z]
    z_scr[2 * total + 3] = zero
    mine = gz * planes
    for z in range(planes + 2):
        phz[z] = z_scr[mine + z]
        psz[z] = jnp.where(mine + z == 0, zero, z_scr[total + 2 + mine + z])

    low_lane, high_lane = zero, zero
    pair_z = iota((8, lanes), 1) // 2
    side = jnp.where(pair_z < planes, 1 - iota((8, lanes), 1) % 2, -1)
    for z in range(planes):
        low_lane = jnp.where(pair_z == z, phz[z + 1], low_lane)
        high_lane = jnp.where(pair_z == z, psz[z + 1], high_lane)
    row_p, lane_p = iota((planes, lanes), 0), iota((planes, lanes), 1)
    low_rows, high_rows = jnp.zeros((planes, lanes), F32), jnp.zeros((planes, lanes), F32)
    for z in range(planes):
        low_rows = jnp.where(row_p == z, phz[z + 1][0:1, :], low_rows)
        high_rows = jnp.where(row_p == z, psz[z + 1][0:1, :], high_rows)
    blocks, ends = [], []
    for e in range(2):
        g = jnp.where(
            lane_p // 2 >= row_p,
            low_rows * high_lane[0:1, :],
            high_rows * low_lane[0:1, :],
        )
        blocks.append(jnp.where(side[0:1, :] == e, g, 0.0))
        ends.append(
            jnp.where(lane_p == e, low_rows, jnp.where(lane_p == 2 + e, high_rows, 0.0))
        )
    rest = jnp.zeros((lanes - 2 * planes, lanes), F32)
    mz[0] = jnp.concatenate(blocks + [rest], axis=0)
    mz[1] = jnp.concatenate(ends + [rest], axis=0)
    row8 = iota((8, lanes), 0)
    wz[0] = jnp.where(
        (row8 < 2) & (side == row8),
        high_lane,
        jnp.where((row8 >= 2) & (row8 < 4) & (side == row8 - 2), low_lane, 0.0),
    )


def slopes(
    counts, idx, cond, scales, u_ref, kind_ref, xr0, xr1, yr0, yr1, zr0, zr1,
    ux, uy, uz, kx0, kx1, ky0, ky1, kz,
):
    planes, rows, columns = u_ref.shape
    even = [idx[d] % 2 == 0 for d in range(3)]
    at_low = [idx[d] == 0 for d in range(3)]
    at_high = [idx[d] == counts[d] - 1 for d in range(3)]
    row, lane = iota((rows, columns), 0), iota((rows, columns), 1)

    def ends(first, second, d):
        return jnp.where(even[d], second, first), jnp.where(even[d], first, second)

    low, high = ends(xr0[0], xr1[0], 0)
    ux[...] = jnp.zeros(ux.shape, F32)
    for z in range(planes):
        ux[z, 0:1, :] = low[z : z + 1, :]
        ux[z, 1:2, :] = high[z : z + 1, :]
    x_low, x_high = ends(xr0[1], xr1[1], 0)
    low, high = ends(yr0[...], yr1[...], 1)
    both = jnp.where(lane % 2 == 0, high, pltpu.roll(low, 1, 1))
    uy[...] = jnp.zeros(uy.shape, F32)
    uy[:rows, :] = jnp.where(lane < 2 * planes, both, 0.0)
    low, high = ends(zr0[0], zr1[0], 2)
    uz[0] = jnp.where(at_low[2], 0.0, low)
    uz[1] = high
    z_low, z_high = ends(zr0[1], zr1[1], 2)
    half = 0.5 * HEAT_SPREADING
    c_before = None
    for z in range(planes):
        c = conductance(kind_ref[z], cond[z][0:1, :], scales)
        first = jnp.where(at_low[0], -c[0:1, :], x_low[z : z + 1, :])
        final = jnp.where(at_high[0], -c[rows - 1 :, :], x_high[z : z + 1, :])
        kx0[z] = half * (c + jnp.where(row == 0, first, pltpu.roll(c, 1, 0)))
        kx1[z] = half * (c + jnp.where(row == rows - 1, final, pltpu.roll(c, rows - 1, 0)))
        edge = pltpu.roll(both, columns - 1 - 2 * (planes + z), 1)
        first = jnp.where(at_low[1], -c, edge)
        final = jnp.where(at_high[1], -c, edge)
        ky0[z] = half * (c + jnp.where(lane == 0, first, pltpu.roll(c, 1, 1)))
        ky1[z] = half * (c + jnp.where(lane == columns - 1, final, pltpu.roll(c, columns - 1, 1)))
        if z == 0:
            kz[z] = half * (c + jnp.where(at_low[2], c, z_low))
        else:
            kz[z] = half * (c + c_before)
        c_before = c
        if z == planes - 1:
            kz[planes] = half * jnp.where(at_high[2], 0.0, c + z_high)


def outflow(z, u_ref, ux, uy, uz, kx0, kx1, ky0, ky1, kz):
    planes, rows, columns = u_ref.shape
    u = u_ref[z]
    row, lane = iota((rows, columns), 0), iota((rows, columns), 1)
    edge = pltpu.roll(uy[:rows, :], columns - 1 - 2 * z, 1)
    below = uz[0] if z == 0 else u_ref[z - 1]
    above = uz[1] if z == planes - 1 else u_ref[z + 1]
    total = kx0[z] * (jnp.where(row == 0, ux[z, 0:1, :], pltpu.roll(u, 1, 0)) - u)
    total += kx1[z] * (
        jnp.where(row == rows - 1, ux[z, 1:2, :], pltpu.roll(u, rows - 1, 0)) - u
    )
    total += ky0[z] * (jnp.where(lane == 0, edge, pltpu.roll(u, 1, 1)) - u)
    total += ky1[z] * (
        jnp.where(lane == columns - 1, edge, pltpu.roll(u, columns - 1, 1)) - u
    )
    return total + kz[z] * (below - u) + kz[z + 1] * (above - u)


def advance(idx, source_of, gx_ref, gy_ref, phz, psz, t_ref, e_ref, z_sends, x_sends):
    planes, extent, columns = t_ref.shape
    rows = extent - EXTRA
    sums = jnp.zeros((extent, 128), F32)
    below, above = jnp.zeros((rows, columns), F32), jnp.zeros((rows, columns), F32)
    for z in range(planes):
        high, low = split(source_of(z))
        out = mm(gx_ref[z], jnp.concatenate([high, low], axis=1))
        t = out[:extent, :columns] + (out[:extent, columns:] + out[extent:, :columns])
        high, low = split(t)
        twice = jnp.concatenate([gy_ref[z], gy_ref[z]], axis=0)
        out = mm(jnp.concatenate([high, low], axis=1), twice) + mm(high, gy_ref[planes + z])
        t_ref[z] = out[:, :columns]
        sums += out[:, columns:]
        main = out[:rows, :columns]
        below += phz[z + 1][0:1, :] * main
        above += psz[z + 1][0:1, :] * main
    e_ref[...] = sums
    for b, send in enumerate(x_sends):
        take = jnp.where((idx[0] >> b) % 2 == 0, 0, 1)
        for z in range(planes):
            pair = t_ref[z, rows + 2 : rows + 4, :]
            send[z : z + 1, :] = jnp.where(take == 0, pair[0:1], pair[1:2])
        pair = sums[rows + 2 : rows + 4, :]
        send[planes:, :] = jnp.broadcast_to(
            jnp.where(take == 0, pair[0:1], pair[1:2]), (8, 128)
        )
    deep = len(z_sends) > 1
    rising = (idx[2] >> (1 if deep else 0)) % 2 == 0
    z_sends[0][...] = jnp.where(rising, below, above)
    if deep:
        z_sends[1][...] = jnp.where(rising, above, below)


def joule_kernel(sizes, sheet_in, table_in, scaling_in, got_in, gx_ref, gy_ref, co, joule,
                 r_scr, k_scr, z_scr, got, sheet, table, scaling, sems):
    started = copies(
        [
            (sheet_in, sheet), (table_in, table), (scaling_in, scaling),
            (got_in.at[:, 0, :], got),
        ],
        sems,
    )
    for copy in started:
        copy.start()
    for copy in started[:3]:
        copy.wait()
    coefficients(sizes, place(), sheet, table, scaling, gx_ref, gy_ref, co, z_scr)
    started[3].wait()
    joule_into(got, joule, r_scr, k_scr)


def start_kernel(sizes, xr0, xr1, yr0, yr1, zr0, zr1,
                 u_ref, kind_ref, gx_ref, gy_ref, co, joule,
                 ux, uy, uz, kx0, kx1, ky0, ky1, kz, t_ref, e_ref, *sends):
    idx = place()
    phz, psz, cond, kinds = groups_of(sizes, co, "phz", "psz", "cond", "kinds")
    scales = [kinds[category][0:1, :] for category in range(sizes[6])]
    slopes(
        sizes[3:], idx, cond, scales, u_ref, kind_ref, xr0, xr1, yr0, yr1, zr0, zr1,
        ux, uy, uz, kx0, kx1, ky0, ky1, kz,
    )

    deep = 2 if sizes[5] > 2 else 1

    def source_of(z):
        out = outflow(z, u_ref, ux, uy, uz, kx0, kx1, ky0, ky1, kz)
        return out + OHMIC_POWER * ((1.0 + WARMING_SLOPE * u_ref[z]) * joule[z])

    advance(
        idx, source_of, gx_ref, gy_ref, phz, psz, t_ref, e_ref,
        sends[:deep], sends[deep:],
    )


def x_kernel(sizes, e_ref, co, pair, near, *rest):
    idx = place()
    planes, nx = sizes[0], sizes[3]
    gots, (e_out, f_out, send), far = rest[: nx - 1], rest[nx - 1 : nx + 2], rest[nx + 2 :]
    for out in far:
        out[...] = pair[...] + near[...]
    dx, dxl, lx = groups_of(sizes, co, "dx", "dxl", "lx")
    me = idx[0]
    sums = [[jnp.zeros((planes, 128), F32), jnp.zeros((8, 128), F32)] for _ in range(2)]
    for k, got in zip(range(1, nx), gots):
        other = partner(me, k, nx)
        far = jnp.abs(me - other)
        pair = got[:planes, :] * dx[far], got[planes:, :] * dxl[far]
        for side, keep in ((0, other < me), (1, other > me)):
            for part in range(2):
                sums[side][part] += jnp.where(keep, pair[part], 0.0)
    f_out[:planes, :], f_out[planes:, :] = sums[0][0], sums[1][0]
    row, lane = iota((planes, 128), 0), iota((planes, 128), 1)
    own = lane % planes == row
    ext = jnp.concatenate(
        [jnp.where(own, sums[0][1][0:1, :], 0.0), jnp.where(own, sums[1][1][0:1, :], 0.0)],
        axis=0,
    )
    e = e_ref[...] + stacked(lx[0][:, : 2 * planes], ext)
    e_out[...] = e
    send[...] = e.T[2 * planes : 4 * planes]


def four(rows):
    return jnp.concatenate([rows] * 4, axis=0)


def weights(ref, planes):
    row = iota((planes, 128), 0)
    values = jnp.zeros((planes, 128), F32)
    for z in range(planes):
        values = jnp.where(row == z, ref[z + 1][0:1, :], values)
    return values


def y_kernel(sizes, final, t_ref, e_ref, f_ref, co, *rest):
    idx = place()
    ny = sizes[4]
    dy, lx, by, cg, phz, psz, mz = groups_of(
        sizes, co, "dy", "lx", "by", "cg", "phz", "psz", "mz"
    )
    gots, rest = rest[: ny - 1], rest[ny - 1 :]
    l_ref, b_ref = rest[:2]
    sends, q_ref = (rest[2:], None) if final else (rest[3:], rest[2])
    planes, extent, columns = t_ref.shape
    rows = extent - EXTRA
    me = idx[1]
    row = iota((2 * planes, extent), 0)
    across = jnp.zeros((2 * planes, extent), F32)
    for k, got in zip(range(1, ny), gots):
        other = partner(me, k, ny)
        far = jnp.concatenate([dy[jnp.abs(me - other)][:, 0:1]] * 2, axis=0)
        keep = (row < planes) == (other < me)
        across += jnp.where(keep, got[...] * far, 0.0)
    others = jnp.concatenate(
        [
            jnp.zeros((2 * planes, extent), F32),
            across,
            jnp.zeros((128 - 4 * planes, extent), F32),
        ],
        axis=0,
    ).T
    left = lx[0] + others
    l_ref[...] = left
    right = jnp.concatenate([f_ref[...], by[idx[2]]], axis=0)
    b_ref[...] = right
    low, high = weights(phz, planes), weights(psz, planes)
    if not final:
        lane = iota((extent, 128), 1)
        q = jnp.where(lane < 2 * planes, e_ref[...], 0.0) + stacked(others, cg[0])
        q_ref[...] = q
        edge = stacked(q[:rows], mz[1]).T
        ghost = slice(rows, rows + 8)
        both = jnp.concatenate([right * four(low), right * four(high)], axis=1)
        ghosts = stacked(left[ghost, : 4 * planes], both)
        g_low, g_high = ghosts[:, :128], ghosts[:, 128:]
        for z in range(planes):
            value = t_ref[z, ghost, :]
            g_low += phz[z + 1][0:1, :] * value
            g_high += psz[z + 1][0:1, :] * value
    if ny == 2:
        across = jnp.where(me == 1, across[:planes], across[planes:])
    for b, send in enumerate(sends):
        lower = (idx[2] >> b) % 2 == 0
        scale = jnp.where(lower, low, high)
        at = 0
        if not final:
            send[:2, :] = jnp.where(lower, g_low[:2], g_high[:2])
            ends = jnp.where(lower, edge[:2], edge[2:4])
            for part in range(rows // 128):
                send[2 + 2 * part : 4 + 2 * part, :] = ends[:, part * 128 : (part + 1) * 128]
            at = 8
        send[at : at + 2 * planes, :] = f_ref[...] * jnp.concatenate([scale] * 2, axis=0)
        at += 2 * planes
        many = across.shape[0]
        scale = jnp.concatenate([scale] * (many // planes), axis=0)
        for part in range(rows // 128):
            send[at : at + many, :] = across[:, part * 128 : (part + 1) * 128] * scale
            at += many


def carried(nz, idx, bigs, smalls, ax, by, rows, ghosts):
    me = idx[2]
    planes = by.each // 2
    if nz == 2:
        below = jnp.where(me == 1, bigs[0][...], 0.0)
        above = jnp.where(me == 1, 0.0, bigs[0][...])
    else:
        near, aside, far = (big[...] for big in bigs)
        below = jnp.where(me == 1, near, 0.0) + jnp.where(me == 3, aside, 0.0)
        above = jnp.where(me == 2, near, 0.0) + jnp.where(me == 0, aside, 0.0)
        below += jnp.where(me > 1, far, 0.0)
        above += jnp.where(me > 1, 0.0, far)
    g_below = g_above = 0.0
    ends = [0.0, 0.0]
    lefts, rights = [], []
    for k, small in zip(range(1, nz), smalls):
        other = partner(me, k, nz)
        lower = other < me
        at = 0
        halves = rows // 128
        if ghosts:
            g_below += jnp.where(lower, small[:2, :], 0.0)
            g_above += jnp.where(lower, 0.0, small[:2, :])
            value = jnp.concatenate(
                [small[2 + 2 * p : 4 + 2 * p, :] for p in range(halves)], axis=1
            )
            ends[0] += jnp.where(lower, value, 0.0)
            ends[1] += jnp.where(lower, 0.0, value)
            at = 8
        both = at + 2 * planes
        many = (small.shape[0] - both) // halves
        across = [small[both + p * many : both + (p + 1) * many, :] for p in range(halves)]
        near = [ax[other * halves + half] for half in range(halves)]
        lefts += [jnp.concatenate(near, axis=1), jnp.concatenate(across, axis=1)]
        lines = by[other]
        if many == planes:
            lines = jnp.where(idx[1] == 1, lines[:planes], lines[planes:])
        right = jnp.concatenate([small[at:both, :], lines], axis=0)
        rights.append(
            jnp.concatenate(
                [jnp.where(lower, right, 0.0), jnp.where(lower, 0.0, right)], axis=1
            )
        )
    edges = None
    if ghosts:
        edges = jnp.concatenate(ends + [jnp.zeros((4, rows), F32)], axis=0)
        none = jnp.zeros((6, 128), F32)
        g_below = jnp.concatenate([g_below, none], axis=0)
        g_above = jnp.concatenate([g_above, none], axis=0)
    more = stacked_rows(jnp.concatenate(lefts, axis=0), jnp.concatenate(rights, axis=0))
    below, above = below + more[:, :128], above + more[:, 128:]
    return below, above, g_below, g_above, edges


def whole_planes(t_ref, l_ref, b_ref, second, extent):
    planes, _, columns = t_ref.shape
    high, low = split(l_ref[:extent, : 4 * planes])
    left = jnp.concatenate([high, low, high], axis=1)
    right = b_ref[...]
    row = iota(right.shape, 0) % planes
    for z in range(0, planes, 2):
        own = [jnp.where(row == z + k, right, 0.0) for k in range(2)]
        r_high, r_low = split(jnp.concatenate(own, axis=1))
        out = mm(left, jnp.concatenate([r_high, r_high, r_low], axis=0))
        for k in range(2):
            second[z + k] = t_ref[z + k, :extent, :] + out[:, k * columns : (k + 1) * columns]


def change(outside, second, phz, psz, below, above, emit):
    planes = second.shape[0]
    tails = [above]
    for z in range(planes - 1, -1, -1):
        tails.append(tails[-1] + psz[z + 1][0:1, :] * second[z])
    tails = tails[::-1]
    if outside:
        emit(-1, psz[0][0:1, :] * below + phz[0][0:1, :] * tails[0])
    head = below
    for z in range(planes):
        head = head + phz[z + 1][0:1, :] * second[z]
        emit(z, psz[z + 1][0:1, :] * head + phz[z + 1][0:1, :] * tails[z + 1])
    if outside:
        emit(planes, psz[planes + 1][0:1, :] * head + phz[planes + 1][0:1, :] * above)


def rise_kernel(sizes, final, t_in, l_ref, b_ref, q_ref, co,
                u_ref, ux, uy, uz, kx0, kx1, ky0, ky1, kz, joule, gx_ref, gy_ref, *rest):
    idx = place()
    nz = sizes[5]
    phz, psz, mz, wz, ax, by = groups_of(sizes, co, "phz", "psz", "mz", "wz", "ax", "by")
    deep = 2 if nz > 2 else 1
    many = 3 if nz > 2 else 1
    bigs, smalls, rest = rest[:many], rest[many : many + nz - 1], rest[many + nz - 1 :]
    if final:
        u_out, t_ref, e_ref = rest[:3]
        sends, (second, ux_out, uy_out, uz_out) = rest[3:-4], rest[-4:]
    else:
        u_out, t_ref, e_ref, ux_out, uy_out, uz_out = rest[:6]
        sends, second = rest[6:-1], rest[-1]
    planes, rows, columns = u_ref.shape
    whole_planes(t_in, l_ref, b_ref, second, rows + 8)
    below, above, g_below, g_above, edges = carried(nz, idx, bigs, smalls, ax, by, rows, True)

    def emit(z, value):
        if z == -1:
            uz_out[0] = uz[0] + value[:rows]
        elif z == planes:
            uz_out[1] = uz[1] + value[:rows]
        else:
            u_out[z] = u_ref[z] + value[:rows]
            ux_out[z] = ux[z] + value[rows:]

    change(
        True, second, phz, psz,
        jnp.concatenate([below, g_below], axis=0),
        jnp.concatenate([above, g_above], axis=0),
        emit,
    )
    grown = stacked(q_ref[:rows, :], mz[0]) + stacked_rows(edges, wz[0])
    uy_out[...] = uy[...]
    uy_out[:rows, :] = uy[:rows, :] + grown

    def source_of(z):
        out = outflow(z, u_out, ux_out, uy_out, uz_out, kx0, kx1, ky0, ky1, kz)
        return out + OHMIC_POWER * ((1.0 + WARMING_SLOPE * u_out[z]) * joule[z])

    advance(
        idx, source_of, gx_ref, gy_ref, phz, psz, t_ref, e_ref,
        sends[:deep], sends[deep:],
    )


def finish_kernel(sizes, t_in, l_ref, b_ref, co, u_ref, joule, *rest):
    idx = place()
    nz = sizes[5]
    phz, psz, ax, by = groups_of(sizes, co, "phz", "psz", "ax", "by")
    deep = 2 if nz > 2 else 1
    many = 3 if nz > 2 else 1
    bigs, smalls, rest = rest[:many], rest[many : many + nz - 1], rest[many + nz - 1 :]
    u_out, heat_out, u_scr, heat_scr, second, sems = rest
    rows = u_ref.shape[1]
    started = []
    whole_planes(t_in, l_ref, b_ref, second, rows)
    below, above, _, _, _ = carried(nz, idx, bigs, smalls, ax, by, rows, False)

    def emit(z, value):
        u = u_ref[z] + value
        u_scr[z] = u
        heat_scr[z] = (1.0 + WARMING_SLOPE * u) * joule[z]
        for k, (src, dst) in enumerate(((u_scr, u_out), (heat_scr, heat_out))):
            started.append(pltpu.make_async_copy(src.at[z], dst.at[z], sems.at[k, z]))
            started[-1].start()

    change(False, second, phz, psz, below, above, emit)
    for copy in started:
        copy.wait()


def per_device(
    starting_warmth,
    sheet_stratum_number,
    stratum_heat_conduction,
    substance_kind,
    substance_kind_scaling,
    wire_piece_amperes,
    wire_piece_ohms_base,
    wire_piece_tile,
    wire_piece_voxel,
):
    planes, rows, columns = starting_warmth.shape
    counts = tuple(lax.axis_size(axis) for axis in ("gx", "gy", "gz"))
    nx, ny, nz = counts
    assert nz in (2, 4)
    bits = [(n - 1).bit_length() for n in counts]
    devices = nx * ny * nz
    extent = rows + EXTRA
    block = shaped(planes, rows, columns)
    tables = sheet_stratum_number, stratum_heat_conduction, substance_kind_scaling
    scalars = [pltpu.SMEM(part.shape, part.dtype) for part in tables]

    count = wire_piece_amperes.shape[0]
    capacity = 2 * count // devices
    lanes = 128
    chunks = count // lanes
    segments = tuple(
        part.reshape(chunks, lanes)
        for part in (
            wire_piece_amperes, wire_piece_ohms_base, wire_piece_tile, wire_piece_voxel
        )
    )
    share, spare = shares(capacity)
    slots = planes * share + spare
    y_faces = 1 if ny == 2 else 2
    send, xs0, xs1, ys, zs0, zs1 = call(
        functools.partial(first_kernel, devices, planes, rows * columns, capacity),
        [
            shaped(devices, 1, 2 * slots),
            shaped(2, planes, columns),
            shaped(2, planes, columns),
            shaped(y_faces, rows, 128),
            shaped(2, rows, columns),
            shaped(2, rows, columns),
        ],
        (*tables, *segments, starting_warmth, substance_kind),
        far=9,
        far_out=True,
        vmem=60,
        scratch=[
            pltpu.VMEM((devices, 1, 2 * slots), F32),
            pltpu.VMEM((2, 2, planes, columns), F32),
            pltpu.VMEM((y_faces, rows, 128), F32),
            pltpu.VMEM((2, rows, columns), F32),
        ]
        + [pltpu.VMEM((chunks, lanes), part.dtype) for part in segments]
        + [
            pltpu.VMEM((5 * devices, count), BF16),
            pltpu.VMEM((max(planes * share, spare), count), BF16),
            pltpu.VMEM((devices * planes, lanes), F32),
            pltpu.VMEM((chunks, lanes), jnp.int32),
            pltpu.VMEM(block.shape, F32),
            pltpu.VMEM(block.shape, jnp.int32),
            *scalars,
            pltpu.SemaphoreType.DMA((7,)),
            pltpu.SemaphoreType.DMA((2, planes)),
            pltpu.SemaphoreType.DMA((8,)),
        ],
    )
    got = lax.all_to_all(send, ("gx", "gy", "gz"), split_axis=0, concat_axis=0, tiled=True)

    zr = next_pairs(zs0, zs1, "gz")
    xr = next_pairs(xs0, xs1, "gx")
    yr = next_pairs(ys[0], ys[-1], "gy")
    sizes = (planes, rows, columns, nx, ny, nz, substance_kind_scaling.shape[0])
    parts = [
        shaped(planes, 2 * extent, rows, dtype=BF16),
        shaped(2 * planes, columns, 256, dtype=BF16),
        shaped(table_rows(*sizes)[1], lanes),
    ]
    step_out = [shaped(planes, extent, columns), shaped(extent, 128)]
    step_out += [shaped(rows, columns)] * bits[2] + [shaped(planes + 8, columns)] * bits[0]
    total = devices * spare
    ghosts = [shaped(planes, 8, columns), shaped(extent, 128), shaped(2, rows, columns)]
    gx_m, gy_m, co, joule = call(
        functools.partial(joule_kernel, sizes),
        parts + [block],
        (*tables, got),
        far=4,
        vmem=24,
        scratch=[
            pltpu.VMEM((2 * columns, total), BF16),
            pltpu.VMEM((8, total), jnp.int32),
            pltpu.VMEM((2 * planes * nz + 4, 8, lanes), F32),
            pltpu.VMEM((devices, 2 * slots), F32),
            *scalars,
            pltpu.SemaphoreType.DMA((4,)),
        ],
    )
    ux, uy, uz, *rest = call(
        functools.partial(start_kernel, sizes),
        ghosts + [block] * 4 + [shaped(planes + 1, rows, columns)] + step_out,
        (*xr, *yr, *zr, starting_warmth, substance_kind, gx_m, gy_m, co, joule),
    )
    conduct, (t, e, *sends) = rest[:5], rest[5:]
    u = starting_warmth
    lines = planes if ny == 2 else 2 * planes
    small_rows = 2 * planes + lines * (rows // 128)
    for repeat in range(STEPS):
        pair, *beside = sends[: bits[2]]
        gots = all_pairs(sends[bits[2] :], "gx")
        near = crossed(pair, 1, "gz")
        e, f, send, *far = call(
            functools.partial(x_kernel, sizes),
            [shaped(extent, 128), shaped(2 * planes, columns), shaped(2 * planes, extent)]
            + [shaped(rows, columns)] * (bits[2] - 1),
            (e, co, pair, near, *gots),
        )
        bigs = [near]
        if nz > 2:
            bigs.append(lax.ppermute(beside[0], "gz", [(1, 0), (2, 3)]))
            bigs.append(crossed(far[0], 2, "gz"))
        gots = all_pairs([send] * bits[1], "gy")
        final = repeat == STEPS - 1
        q = [] if final else [shaped(extent, 128)]
        small = shaped(small_rows + (0 if final else 8), 128)
        left, right, *sends = call(
            functools.partial(y_kernel, sizes, final),
            [shaped(extent, 128), shaped(4 * planes, columns)] + q + [small] * bits[2],
            (t, e, f, co, *gots),
        )
        if final:
            smalls = all_pairs(sends, "gz")
        else:
            q, *sends = sends
            smalls = all_pairs(sends, "gz")
            last = repeat == STEPS - 2
            u, t, e, *sends = call(
                functools.partial(rise_kernel, sizes, last),
                [block] + step_out[:2] + ([] if last else ghosts) + step_out[2:],
                (t, left, right, q, co, u, ux, uy, uz, *conduct)
                + (joule, gx_m, gy_m, *bigs, *smalls),
                scratch=[pltpu.VMEM((planes, rows + 8, columns), F32)]
                + [pltpu.VMEM(o.shape, F32) for o in (ghosts if last else [])],
            )
            if not last:
                ux, uy, uz, *sends = sends
    return tuple(
        call(
            functools.partial(finish_kernel, sizes),
            [block, block],
            (t, left, right, co, u, joule, *bigs, *smalls),
            scratch=[pltpu.VMEM((planes, rows, columns), F32)] * 3
            + [pltpu.SemaphoreType.DMA((2, planes))],
            far_out=True,
        )
    )


def solution(mesh):
    return jax.shard_map(
        per_device,
        mesh=mesh,
        in_specs=(
            P("gz", "gx", "gy"),
            P(),
            P(),
            P("gz", "gx", "gy"),
            P(),
            P(("gx", "gy", "gz")),
            P(("gx", "gy", "gz")),
            P(("gx", "gy", "gz"), None),
            P(("gx", "gy", "gz")),
        ),
        out_specs=(P("gz", "gx", "gy"), P("gz", "gx", "gy")),
        check_vma=False,
    )
```
